32 devices in a mesh: wide: 8 (over z, y), narrow: 4 (over x, core).
Axes of the slice: x: 2, y: 2, z: 4, core: 2. Of those that a mesh axis runs over, the one named last changes fastest.
Arguments:
- pixels: bfloat16 [8192, 1536], P(('wide', 'narrow')), may hold values from -6 to 6
- clip_index: int32 [4, 2048], replicated, may hold values from 0 to 4, as said below
- patch_weight: float32 [1536, 1024], P(('wide', 'narrow')), may hold values from -0.15625 to 0.15625
- encoder_attention: float32 [1024, 3072], P(('wide', 'narrow')), may hold values from -0.1875 to 0.1875
- encoder_output: float32 [1024, 1024], P(('wide', 'narrow')), may hold values from -1.5 to 1.5
- encoder_expand: float32 [1024, 4096], P(('wide', 'narrow')), may hold values from -0.1875 to 0.1875
- encoder_reduce: float32 [4096, 1024], P(('wide', 'narrow')), may hold values from -0.09375 to 0.09375
- predictor_embed: float32 [1024, 384], P(('wide', 'narrow')), may hold values from -0.1875 to 0.1875
- predictor_weights: float32 [1536, 3, 384], P(('wide', 'narrow')), may hold values from -3 to 3
- encoder_gains: float32 [2, 1024], replicated, may hold values from 0.5 to 1.5
- encoder_biases: float32 [9, 1024], replicated, may hold values from -2 to 2
- predictor_gains: float32 [2, 384], replicated, may hold values from 0.5 to 1.5
- predictor_biases: float32 [9, 384], replicated, may hold values from -2 to 2
- cotangent: bfloat16 [8192, 384], P(('wide', 'narrow')), may hold values from -6 to 6
Outputs:
- pred_output: bfloat16 [8192, 384], P(('wide', 'narrow'))
- pixel_grad: bfloat16 [8192, 1536], P(('wide', 'narrow'))
- patch_weight_grad: float32 [1536, 1024], P(('wide', 'narrow'))
- encoder_attention_grad: float32 [1024, 3072], P(('wide', 'narrow'))
- encoder_output_grad: float32 [1024, 1024], P(('wide', 'narrow'))
- encoder_expand_grad: float32 [1024, 4096], P(('wide', 'narrow'))
- encoder_reduce_grad: float32 [4096, 1024], P(('wide', 'narrow'))
- predictor_embed_grad: float32 [1024, 384], P(('wide', 'narrow'))
- predictor_weights_grad: float32 [1536, 3, 384], P(('wide', 'narrow'))
- encoder_gains_grad: float32 [2, 1024], replicated
- encoder_biases_grad: float32 [9, 1024], replicated
- predictor_gains_grad: float32 [2, 384], replicated
- predictor_biases_grad: float32 [9, 384], replicated
The draws below stay inside these ranges and needn't reach their ends.
Inputs may be any that keep to these rules, and one draw needn't show every extreme that they name: `clip_index`: ids never fall along a row. Every row holds, in order: a still of 196 tokens (id 0), a piece of 1 to 87 tokens (id 1), a clip of 1568 tokens (id 2) that covers positions 255 through 2048 - 256, a still of 196 tokens (id 3) and a piece of the remaining tokens (id 4); the two pieces have 88 tokens together.
All inputs are finite; a program needn't handle non-finite values.
Results may differ from the reference program's by a relative error of at most 0.017.
Values may be sent and summed in bfloat16 or wider, within the bound.
No kernel may reach another device: no remote copies, remote signals or barrier semaphores. Data moves between devices by JAX's collectives and lax.ppermute only.
A program may use at most 320 MiB of HBM per device.

```python
import jax
import jax.numpy as jnp
from jax import lax

D = 1024
FF = 4096
HEADS = 16
PIX = 1536
PRED_WIDTH = 384
PRED_FF = 1536
PRED_HEADS = 12
TOK_DEV = 256
STILL_TOK = 196
REST = 88
GROUP_TOK = 2048
CLIP_TOK = 1568
GROUPS = 4
TOKENS = 8192


def draw_clip_index(key, part):
    key = jax.random.fold_in(key, 11)
    margin = TOK_DEV - 1 - STILL_TOK
    lowest = max(1, REST - margin)
    highest = min(REST - 1, margin)
    first_piece = jax.random.randint(key, (GROUPS, 1), lowest, highest + 1)
    position = jnp.arange(GROUP_TOK, dtype=jnp.int32)[None, :]
    clip_start = STILL_TOK + first_piece
    clip_end = clip_start + CLIP_TOK
    labels = (position >= STILL_TOK).astype(jnp.int32)
    labels = labels + (position >= clip_start).astype(jnp.int32)
    labels = labels + (position >= clip_end).astype(jnp.int32)
    labels = labels + (position >= clip_end + STILL_TOK).astype(jnp.int32)
    return labels.astype(jnp.int32)


def draw_predictor_weights(key, part):
    key = jax.random.fold_in(key, 23)
    noise = jnp.clip(jax.random.normal(key, (PRED_FF, 3, PRED_WIDTH), jnp.float32), -5.0, 5.0)
    row_index = jnp.arange(PRED_FF)[:, None]
    slot_index = jnp.arange(3)[None, :]
    factor = jnp.where(slot_index == 2, PRED_FF ** (-0.5), PRED_WIDTH ** (-0.5))
    factor = jnp.where((slot_index == 0) & (row_index >= 3 * PRED_WIDTH), (PRED_WIDTH // 8) ** (-0.5), factor)
    return noise * factor[:, :, None]


def block_scale(key, extent, pieces, smallest, high):
    factor_of = 1.0
    for axis_at, shards_of in pieces:
        heights = jax.random.uniform(jax.random.fold_in(jax.random.fold_in(key, 6), axis_at), (shards_of,), jnp.float32, smallest / len(pieces), high / len(pieces))
        factor_of = factor_of * jnp.repeat(jnp.exp(heights), extent[axis_at] // shards_of).reshape((-1,) + (1,) * (len(extent) - 1 - axis_at))
    return factor_of


def bell_draw(own_key, dims, scale, limit, pieces=(), held_as=jnp.bfloat16):
    values = jax.random.normal(own_key, dims, jnp.float32) * scale
    if len(pieces) > 0:
        values = block_scale(own_key, dims, pieces, -0.22, 0.18) * values
    return jnp.clip(values, min=-limit, max=limit).astype(held_as)


def setup_inputs(seed: int = 0) -> dict:
    key_list = jax.random.split(jax.random.key(seed), 15)
    return {
        "pixels": bell_draw(key_list[0], (TOKENS, PIX), 1.0, 6.0, ((0, 32),)),
        "clip_index": draw_clip_index(jax.random.fold_in(key_list[14], 71), 0),
        "patch_weight": bell_draw(key_list[2], (PIX, D), PIX ** -0.5, 0.15625, ((0, 32),), jnp.float32),
        "encoder_attention": bell_draw(key_list[3], (D, 3 * D), D ** -0.5, 0.1875, ((0, 32),), jnp.float32),
        "encoder_output": bell_draw(key_list[4], (D, D), (D // 64) ** -0.5, 1.5, ((0, 32),), jnp.float32),
        "encoder_expand": bell_draw(key_list[5], (D, FF), D ** -0.5, 0.1875, ((0, 32),), jnp.float32),
        "encoder_reduce": bell_draw(key_list[6], (FF, D), FF ** -0.5, 0.09375, ((0, 32),), jnp.float32),
        "predictor_embed": bell_draw(key_list[7], (D, PRED_WIDTH), D ** -0.5, 0.1875, ((0, 32),), jnp.float32),
        "predictor_weights": draw_predictor_weights(jax.random.fold_in(key_list[14], 71), 0),
        "encoder_gains": jnp.clip(1.0 + 0.1 * jax.random.normal(key_list[9], (2, D), jnp.float32), 0.5, 1.5),
        "encoder_biases": bell_draw(key_list[10], (9, D), 0.3, 2.0, (), jnp.float32),
        "predictor_gains": jnp.clip(1.0 + 0.1 * jax.random.normal(key_list[11], (2, PRED_WIDTH), jnp.float32), 0.5, 1.5),
        "predictor_biases": bell_draw(key_list[12], (9, PRED_WIDTH), 0.3, 2.0, (), jnp.float32),
        "cotangent": bell_draw(key_list[13], (TOKENS, PRED_WIDTH), 1.0, 6.0, ((0, 32),)),
    }


EPSILON = 1e-06
GELU_SCALE = 0.7978845608028654
MASKED = -1e+30

@jax.custom_vjp
def low(v):
    return lax.optimization_barrier(v.astype(jnp.bfloat16)).astype(jnp.float32)

@jax.custom_vjp
def low_back(v):
    return v

def low_keep(v):
    return (low(v), None)

def low_pass(kept, grad):
    return (grad,)

def back_keep(v):
    return (v, None)

def back_low(kept, grad):
    return (low(grad),)
low.defvjp(low_keep, low_pass)
low_back.defvjp(back_keep, back_low)

def matmul(left, right):
    return jnp.dot(left, right, precision=lax.Precision.HIGHEST)

def layer_norm(values, gain, bias):
    center = values - lax.optimization_barrier(jnp.mean(values, -1, keepdims=True))
    spread = lax.optimization_barrier(jnp.mean(center * center, -1, keepdims=True))
    return center * lax.rsqrt(spread + EPSILON) * gain + bias

def smooth_gate(values):
    return 0.5 * values * (1.0 + jnp.tanh(GELU_SCALE * (values + 0.044715 * values * values * values)))

def attend(queries, keys, values, labels, heads):
    row_count, width = queries.shape
    head_size = width // heads
    query_heads = queries.reshape(row_count, heads, head_size)
    key_heads = keys.reshape(row_count, heads, head_size)
    value_heads = values.reshape(row_count, heads, head_size)
    block_rows = min(512, row_count)

    def one_block(offset):
        query_block = lax.dynamic_slice_in_dim(query_heads, offset, block_rows, 0)
        label_block = lax.dynamic_slice_in_dim(labels, offset, block_rows, 0)
        raw_scores = jnp.einsum('thd,khd->htk', query_block, key_heads, precision=lax.Precision.HIGHEST)
        scores = low_back(raw_scores) * head_size ** (-0.5)
        mask = label_block[:, None] == labels[None, :]
        scores = jnp.where(mask[None], scores, MASKED)
        top_score = lax.optimization_barrier(jnp.max(scores, -1, keepdims=True))
        expo = jnp.exp(scores - top_score)
        probs = expo / lax.optimization_barrier(jnp.sum(expo, -1, keepdims=True))
        mixed = jnp.einsum('htk,khd->thd', low(probs), value_heads, precision=lax.Precision.HIGHEST)
        return mixed.reshape(block_rows, width)
    offsets = (jnp.arange(row_count // block_rows) * block_rows).astype(jnp.int32)
    blocks = lax.map(jax.checkpoint(one_block), offsets)
    return blocks.reshape(row_count, width)

def residual_block(inputs, weights, gains, biases, labels, heads):
    attention_weight, output_weight, expand_weight, reduce_weight = weights
    width = inputs.shape[1]
    normed = low(layer_norm(inputs, gains[0], biases[1]))
    projected = low(low_back(matmul(normed, low(attention_weight))))
    attended = low(low_back(attend(projected[:, :width], projected[:, width:2 * width], projected[:, 2 * width:], labels, heads)))
    middle = inputs + low_back(matmul(attended, low(output_weight))) + biases[2]
    second = low(layer_norm(middle, gains[1], biases[3]))
    expanded = low_back(matmul(second, low(expand_weight))) + biases[5:9].reshape(-1)
    activated = low(smooth_gate(expanded))
    return middle + low_back(matmul(activated, low(reduce_weight))) + biases[4]

def network(pixel_values, labels, patch_weight, encoder_attention, encoder_output, encoder_expand, encoder_reduce, predictor_embed, predictor_weights, encoder_gains, encoder_biases, predictor_gains, predictor_biases):
    embedded = low_back(matmul(pixel_values, low(patch_weight))) + encoder_biases[0]
    encoded = residual_block(embedded, (encoder_attention, encoder_output, encoder_expand, encoder_reduce), encoder_gains, encoder_biases, labels, HEADS)
    predictor_in = low_back(matmul(low(encoded), low(predictor_embed))) + predictor_biases[0]
    width = predictor_weights.shape[2]
    parts = (predictor_weights[:3 * width, 0, :].T, predictor_weights[3 * width:, 0, :].T, predictor_weights[:, 1, :].T, predictor_weights[:, 2, :])
    return residual_block(predictor_in, parts, predictor_gains, predictor_biases, labels, PRED_HEADS)

def reference(pixels, clip_index, patch_weight, encoder_attention, encoder_output, encoder_expand, encoder_reduce, predictor_embed, predictor_weights, encoder_gains, encoder_biases, predictor_gains, predictor_biases, cotangent):
    weights = tuple((item.astype(jnp.float32) for item in (patch_weight, encoder_attention, encoder_output, encoder_expand, encoder_reduce, predictor_embed, predictor_weights, encoder_gains, encoder_biases, predictor_gains, predictor_biases)))
    pixel_groups = pixels.reshape(GROUPS, GROUP_TOK, PIX)
    grad_groups = cotangent.reshape(GROUPS, GROUP_TOK, PRED_WIDTH)

    def group_step(totals, items):
        pixel_block, labels, grad_block = items

        def forward(pixel_values, *params):
            return network(pixel_values, labels, *params)
        result, pull = jax.vjp(forward, pixel_block.astype(jnp.float32), *weights)
        grads = pull(grad_block.astype(jnp.float32))
        totals = tuple((left + right for left, right in zip(totals, grads[1:])))
        return (totals, (result.astype(jnp.bfloat16), grads[0].astype(jnp.bfloat16)))
    zero_sums = tuple((jnp.zeros_like(item) for item in weights))
    totals, (results, pixel_grads) = lax.scan(group_step, zero_sums, (pixel_groups, clip_index, grad_groups))
    return (results.reshape(TOKENS, PRED_WIDTH), pixel_grads.reshape(TOKENS, PIX), totals[0], totals[1], totals[2], totals[3], totals[4], totals[5], totals[6], totals[7], totals[8], totals[9], totals[10])
```

```python
import functools

import jax
import jax.numpy as jnp
from jax import lax
from jax.experimental import pallas as pl
from jax.experimental.pallas import tpu as pltpu
from jax.sharding import Mesh
from jax.sharding import PartitionSpec as P

HEADS = 16
PRED_HEADS = 12

EPSILON = 1e-06
GELU_SCALE = 0.7978845608028654
LOG2E = 1.4426950408889634
MASKED = -1e30

PLANE = 8
BLOCK = 256
CLIP_LOW = 224
CLIP_HIGH = 1824
MARGIN = 32
CLIP_ID = 2

AXES = ("z", "y", "x", "c")
GROUP_AXES = ("y", "x", "c")
VMEM_LIMIT = 48 * 1024 * 1024


def swap(value, axis, distance=1):
    size = lax.axis_size(axis)
    return lax.ppermute(value, axis, [(i, i ^ distance) for i in range(size)])


def after(value, *others):
    return lax.optimization_barrier((value,) + others)[0]


def to_half(values):
    return values.astype(jnp.bfloat16)


def to_full(values):
    return values.astype(jnp.float32)


def product(left, right):
    return jnp.dot(left, right, preferred_element_type=jnp.float32)


def left_product(left, right):
    return lax.dot_general(
        left, right, (((0,), (0,)), ((), ())), preferred_element_type=jnp.float32
    )


def right_product(left, right):
    return lax.dot_general(
        left, right, (((1,), (1,)), ((), ())), preferred_element_type=jnp.float32
    )


def layer_norm(values, gain, bias):
    center = values - jnp.mean(values, -1, keepdims=True)
    spread = jnp.mean(center * center, -1, keepdims=True)
    return center * lax.rsqrt(spread + EPSILON) * gain + bias


def smooth_gate(values):
    return (
        0.5 * values * (1.0 + jnp.tanh(GELU_SCALE * (values + 0.044715 * values * values * values)))
    )


def place(own, got, axis, position):
    low = lax.axis_index(axis) == 0
    return jnp.stack([jnp.where(low, own, got), jnp.where(low, got, own)], position)


def gather_rows(shard, order, wait_for=None):
    if wait_for is not None:
        shard = after(shard, wait_for)
    rows, columns = shard.shape
    size = lax.axis_size("z")
    if size == 4:
        parts = [shard] + [swap(shard, "z", d) for d in (1, 2, 3)]
        me = lax.axis_index("z")
        token = parts[3]
        held = jnp.stack([lax.select_n(me ^ b, *parts) for b in range(4)], 0)
    else:
        held = lax.all_gather(shard, "z", axis=0, tiled=False)
        token = held
    first, second = order
    held = place(held, swap(held, first), first, 1)
    held = place(held, swap(held, second), second, 2 if second == "x" else 1)
    held = place(held, swap(held, "c"), "c", 3)
    return held.reshape(size * PLANE * rows, columns), token


def pick(value, axis, position, other):
    index = lax.axis_index(axis)
    return lax.dynamic_index_in_dim(value, 1 - index if other else index, position, keepdims=False)


def scatter_rows(grads, order):
    size = lax.axis_size("z")
    views = [g.reshape(size, 2, 2, 2, g.shape[0] // (size * PLANE), g.shape[1]) for g in grads]

    def side(other):
        picked = [pick(v, "c", 3, other) for v in views]
        return picked[0] if len(picked) == 1 else jnp.concatenate(picked, -1)

    held = to_half(to_full(side(False)) + to_full(swap(side(True), "c")))
    for axis in order:
        position = 2 if axis == "x" and held.ndim == 5 else 1
        got = swap(pick(held, axis, position, True), axis)
        held = to_half(to_full(pick(held, axis, position, False)) + to_full(got))
    if size == 4:
        me = lax.axis_index("z")
        total = to_full(lax.dynamic_index_in_dim(held, me, 0, keepdims=False))
        for d in (1, 2, 3):
            total += to_full(swap(lax.dynamic_index_in_dim(held, me ^ d, 0, keepdims=False), "z", d))
        return total
    return lax.psum_scatter(to_full(held), "z", scatter_dimension=0, tiled=False)


def total_over_devices(value):
    for axis in ("c", "x", "y", "z"):
        distance = 1
        while distance < lax.axis_size(axis):
            value = value + swap(value, axis, distance)
            distance *= 2
    return value


def nt(left, right):
    return lax.dot_general(
        left, right, (((1,), (1,)), ((), ())), preferred_element_type=jnp.float32
    )


def head_lanes(values, head, size):
    lane = lax.broadcasted_iota(jnp.int32, values.shape, 1)
    return jnp.where((lane >= head * size) & (lane < (head + 1) * size), values, jnp.zeros_like(values))


def clip_bias(label_column_ref):
    low = label_column_ref[CLIP_LOW : CLIP_LOW + MARGIN, :]
    high = label_column_ref[CLIP_HIGH - MARGIN : CLIP_HIGH, :]
    return jnp.where(low == CLIP_ID, 0.0, MASKED), jnp.where(high == CLIP_ID, 0.0, MASKED)


def add_margins(scores, biases):
    low, high = biases
    return jnp.concatenate(
        [scores[:MARGIN] + low, scores[MARGIN:-MARGIN], scores[-MARGIN:] + high], 0
    )


def softmax_columns(scores):
    top = jnp.max(scores, 0, keepdims=True)
    expo = jnp.exp2(scores - top)
    total = jnp.sum(expo, 0, keepdims=True)
    return to_half(expo), total, top + jnp.log2(total)


def attend_kernel(size, qkv_ref, column_ref, row_ref, out_ref, log_ref, q_s, k_s, vt_s, ot_s):
    both = 2 * size
    factor = LOG2E * size**-0.5
    q_s[...] = qkv_ref[:, :both]
    k_s[...] = qkv_ref[:, both : 2 * both]
    vt_s[...] = to_half(to_full(qkv_ref[:, 2 * both :]).T)
    biases = clip_bias(column_ref)

    def over_clip(queries):
        keys = k_s[CLIP_LOW:CLIP_HIGH, :]
        values_t = vt_s[:, CLIP_LOW:CLIP_HIGH]
        outs, logs = [], []
        for head in range(2):
            scores = add_margins(nt(keys, head_lanes(queries, head, size)) * factor, biases)
            probs, total, log_total = softmax_columns(scores)
            mixed = product(values_t, probs) / total
            outs.append(mixed[head * size : (head + 1) * size])
            logs.append(log_total)
        return jnp.concatenate(outs, 0), jnp.concatenate(logs, 0)

    def over_block(start):
        keys = k_s[start : start + BLOCK, :]
        values_t = vt_s[:, start : start + BLOCK]
        queries = q_s[start : start + BLOCK, :]
        same = column_ref[start : start + BLOCK, :] == row_ref[:, start : start + BLOCK]
        outs, logs = [], []
        for head in range(2):
            scores = jnp.where(same, nt(keys, head_lanes(queries, head, size)) * factor, MASKED)
            probs, total, log_total = softmax_columns(scores)
            mixed = product(values_t, probs) / total
            outs.append(mixed[head * size : (head + 1) * size])
            logs.append(log_total)
        return jnp.concatenate(outs, 0), jnp.concatenate(logs, 0)

    @pl.loop(1, PLANE - 1)
    def _(block):
        start = pl.multiple_of(block * BLOCK, BLOCK)
        out, logs = over_clip(q_s[pl.ds(start, BLOCK), :])
        ot_s[:, pl.ds(start, BLOCK)] = out
        log_ref[:2, pl.ds(start, BLOCK)] = logs

    last = (PLANE - 1) * BLOCK
    edge_out, edge_logs = over_clip(
        jnp.concatenate(
            [q_s[BLOCK - 128 : BLOCK, :], q_s[last : last + 128, :]], 0
        )
    )
    for start, at, inner in ((0, 128, 0), (last, 0, 128)):
        out, logs = over_block(start)
        ot_s[:, start : start + BLOCK] = out
        log_ref[:2, start : start + BLOCK] = logs
        where = start + at
        clip = row_ref[:, where : where + 128] == CLIP_ID
        ot_s[:, where : where + 128] = jnp.where(
            clip, edge_out[:, inner : inner + 128], ot_s[:, where : where + 128]
        )
        log_ref[:2, where : where + 128] = jnp.where(
            clip, edge_logs[:, inner : inner + 128], log_ref[:2, where : where + 128]
        )
    log_ref[2:, :] = jnp.zeros((6, PLANE * BLOCK), jnp.float32)
    out_ref[...] = to_half(ot_s[...].T)


def attend_back_kernel(
    size, qkv_ref, out_ref, grad_ref, log_ref, column_ref, row_ref, dqkv_ref,
    q_s, k_s, v_s, kt_s, d_s, dqt_s, dk_s, dv_s,
):
    both = 2 * size
    factor = LOG2E * size**-0.5
    scale = size**-0.5
    q_s[...] = qkv_ref[:, :both]
    k_s[...] = qkv_ref[:, both : 2 * both]
    v_s[...] = qkv_ref[:, 2 * both :]
    kt_s[...] = to_half(to_full(qkv_ref[:, both : 2 * both]).T)
    weighted = (to_full(grad_ref[...]) * to_full(out_ref[...])).T
    for head in range(2):
        d_s[head : head + 1, :] = jnp.sum(
            weighted[head * size : (head + 1) * size], 0, keepdims=True
        )
    dk_s[...] = jnp.zeros_like(dk_s)
    dv_s[...] = jnp.zeros_like(dv_s)
    biases = clip_bias(column_ref)

    def pulled(keys, values, keys_t, queries, grads, logs, centres, masked):
        outs, probs_all, scores_all, queries_all, grads_all = [], [], [], [], []
        for head in range(2):
            own_queries = head_lanes(queries, head, size)
            own_grads = head_lanes(grads, head, size)
            probs = jnp.exp2(masked(nt(keys, own_queries) * factor) - logs[head : head + 1])
            pull = nt(values, own_grads)
            grad_scores = to_half(probs * (pull - centres[head : head + 1]))
            outs.append(product(keys_t, grad_scores)[head * size : (head + 1) * size] * scale)
            probs_all.append(to_half(probs))
            scores_all.append(grad_scores)
            queries_all.append(own_queries)
            grads_all.append(own_grads)
        grad_keys = sum(product(s, q) for s, q in zip(scores_all, queries_all)) * scale
        grad_values = sum(product(p, g) for p, g in zip(probs_all, grads_all))
        return jnp.concatenate(outs, 0), grad_keys, grad_values

    def over_clip(queries, grads, logs, centres):
        return pulled(
            k_s[CLIP_LOW:CLIP_HIGH, :],
            v_s[CLIP_LOW:CLIP_HIGH, :],
            kt_s[:, CLIP_LOW:CLIP_HIGH],
            queries,
            grads,
            logs,
            centres,
            lambda scores: add_margins(scores, biases),
        )

    @pl.loop(1, PLANE - 1)
    def _(block):
        start = pl.multiple_of(block * BLOCK, BLOCK)
        here = pl.ds(start, BLOCK)
        out, grad_keys, grad_values = over_clip(
            q_s[here, :], grad_ref[here, :], log_ref[:2, here], d_s[:2, here]
        )
        dqt_s[:, here] = out
        dk_s[CLIP_LOW:CLIP_HIGH, :] += grad_keys
        dv_s[CLIP_LOW:CLIP_HIGH, :] += grad_values

    last = (PLANE - 1) * BLOCK
    near, far = slice(BLOCK - 128, BLOCK), slice(last, last + 128)

    def ends(ref, axis):
        if axis == 0:
            return jnp.concatenate([ref[near, :], ref[far, :]], 0)
        return jnp.concatenate([ref[:2, near], ref[:2, far]], 1)

    edge_labels = jnp.concatenate([row_ref[:, near], row_ref[:, far]], 1)
    edge_logs = jnp.where(edge_labels == CLIP_ID, ends(log_ref, 1), -MASKED)
    edge_out, grad_keys, grad_values = over_clip(
        ends(q_s, 0), ends(grad_ref, 0), edge_logs, ends(d_s, 1)
    )
    dk_s[CLIP_LOW:CLIP_HIGH, :] += grad_keys
    dv_s[CLIP_LOW:CLIP_HIGH, :] += grad_values
    for start, at, inner in ((0, 128, 0), (last, 0, 128)):
        here = slice(start, start + BLOCK)
        labels = row_ref[:, here]
        same = column_ref[here, :] == labels
        logs = jnp.where(labels == CLIP_ID, -MASKED, log_ref[:2, here])
        out, grad_keys, grad_values = pulled(
            k_s[here, :],
            v_s[here, :],
            kt_s[:, here],
            q_s[here, :],
            grad_ref[here, :],
            logs,
            d_s[:2, here],
            lambda scores: jnp.where(same, scores, MASKED),
        )
        dqt_s[:, here] = out
        where = slice(start + at, start + at + 128)
        dqt_s[:, where] += edge_out[:, inner : inner + 128]
        dk_s[here, :] += grad_keys
        dv_s[here, :] += grad_values
    dqkv_ref[:, :both] = to_half(dqt_s[...].T)
    dqkv_ref[:, both : 2 * both] = to_half(dk_s[...])
    dqkv_ref[:, 2 * both :] = to_half(dv_s[...])


def attend(qkv, labels):
    tokens, width = qkv.shape
    both = width // 3
    return pl.pallas_call(
        functools.partial(attend_kernel, both // 2),
        out_shape=(
            jax.ShapeDtypeStruct((tokens, both), jnp.bfloat16),
            jax.ShapeDtypeStruct((8, tokens), jnp.float32),
        ),
        scratch_shapes=[
            pltpu.VMEM((tokens, both), jnp.bfloat16),
            pltpu.VMEM((tokens, both), jnp.bfloat16),
            pltpu.VMEM((both, tokens), jnp.bfloat16),
            pltpu.VMEM((both, tokens), jnp.float32),
        ],
        compiler_params=pltpu.CompilerParams(vmem_limit_bytes=VMEM_LIMIT),
        cost_estimate=pl.CostEstimate(
            flops=8 * tokens * tokens * both, bytes_accessed=8 * tokens * both, transcendentals=0
        ),
        name="attend",
    )(qkv, labels[:, None], labels[None, :])


def attend_back(qkv, out, grad, logs, labels):
    tokens, width = qkv.shape
    both = width // 3
    return pl.pallas_call(
        functools.partial(attend_back_kernel, both // 2),
        out_shape=jax.ShapeDtypeStruct((tokens, width), jnp.bfloat16),
        scratch_shapes=[
            pltpu.VMEM((tokens, both), jnp.bfloat16),
            pltpu.VMEM((tokens, both), jnp.bfloat16),
            pltpu.VMEM((tokens, both), jnp.bfloat16),
            pltpu.VMEM((both, tokens), jnp.bfloat16),
            pltpu.VMEM((8, tokens), jnp.float32),
            pltpu.VMEM((both, tokens), jnp.float32),
            pltpu.VMEM((tokens, both), jnp.float32),
            pltpu.VMEM((tokens, both), jnp.float32),
        ],
        compiler_params=pltpu.CompilerParams(vmem_limit_bytes=VMEM_LIMIT),
        cost_estimate=pl.CostEstimate(
            flops=20 * tokens * tokens * both, bytes_accessed=16 * tokens * both, transcendentals=0
        ),
        name="attend_back",
    )(qkv, out, grad, logs, labels[:, None], labels[None, :])


def to_heads(values, width):
    rows = values.shape[0]
    parts = jnp.moveaxis(values.reshape(rows, PLANE, width), 1, 0)
    moved = lax.all_to_all(parts, GROUP_AXES, split_axis=0, concat_axis=0, tiled=True)
    return moved.reshape(PLANE * rows, width)


def to_tokens(values):
    rows = values.shape[0] // PLANE
    parts = values.reshape(PLANE, rows, values.shape[1])
    moved = lax.all_to_all(parts, GROUP_AXES, split_axis=0, concat_axis=0, tiled=True)
    return jnp.moveaxis(moved, 0, 1)


def encoder_columns(weight):
    rows, columns = weight.shape
    return weight.reshape(rows, 3, PLANE, -1).transpose(0, 2, 1, 3).reshape(rows, columns)


def encoder_columns_back(weight):
    rows, columns = weight.shape
    return weight.reshape(rows, PLANE, 3, -1).transpose(0, 2, 1, 3).reshape(rows, columns)


def slots(values, axis):
    values = jnp.moveaxis(values, axis, 0)
    size = values.shape[0] // PRED_HEADS
    rest = values.shape[1:]
    full = values[: 8 * size].reshape((4, 2 * size) + rest)
    half = values[8 * size :].reshape((4, size) + rest)
    half = jnp.concatenate([half, jnp.zeros_like(half)], 1)
    return jnp.concatenate([full, half], 0)


def slots_back(values):
    size = values.shape[1] // 2
    rest = values.shape[2:]
    return jnp.concatenate(
        [values[:4].reshape((8 * size,) + rest), values[4:, :size].reshape((4 * size,) + rest)], 0
    )


def predictor_projection(weight):
    width = weight.shape[1]
    parts = jnp.stack([slots(weight[i * width : (i + 1) * width], 0) for i in range(3)], 1)
    return parts.reshape(-1, width)


def predictor_projection_back(grad):
    width = grad.shape[1]
    parts = grad.reshape(PLANE, 3, -1, width)
    return jnp.concatenate([slots_back(parts[:, i]) for i in range(3)], 0)


def feed_forward(inputs, attended, output, expand, reduce, gains, biases):
    middle = inputs + output(attended) + biases[2]
    second = to_half(layer_norm(middle, gains[1], biases[3]))
    expanded = expand(second) + biases[5:].reshape(-1)
    activated = to_half(smooth_gate(expanded))
    result = middle + reduce(activated) + biases[4]
    return result, (middle, second, expanded, activated)


def feed_backward(grad_result, saved, gains, biases, reduce_back, expand_back):
    middle, second, expanded, activated = saved
    result_half = to_half(grad_result)
    grad_activated = reduce_back(result_half)
    gate_value, gate_pull = jax.vjp(smooth_gate, expanded)
    grad_expanded = gate_pull(grad_activated)[0]
    expanded_half = to_half(grad_expanded)
    grad_second = expand_back(expanded_half)
    second_value, second_pull = jax.vjp(layer_norm, middle, gains[1], biases[3])
    grad_from_norm, grad_gain_two, grad_bias_three = second_pull(grad_second)
    grad_middle = grad_result + grad_from_norm
    sums = (
        jnp.sum(grad_middle, 0),
        grad_bias_three,
        jnp.sum(grad_result, 0),
        jnp.sum(grad_expanded, 0),
        grad_gain_two,
    )
    return grad_middle, result_half, expanded_half, sums


def per_device(
    pixels,
    clip_index,
    patch_weight,
    encoder_attention,
    encoder_output,
    encoder_expand,
    encoder_reduce,
    predictor_embed,
    predictor_weights,
    encoder_gains,
    encoder_biases,
    predictor_gains,
    predictor_biases,
    cotangent,
):
    labels = lax.dynamic_index_in_dim(clip_index, lax.axis_index("z"), 0, keepdims=False)
    width = encoder_output.shape[1]
    pred_width = predictor_embed.shape[1]
    hidden = encoder_expand.shape[1]
    pair = width // PLANE

    patch, token = gather_rows(to_half(patch_weight), ("y", "x"))
    attention, token = gather_rows(encoder_columns(to_half(encoder_attention)), ("x", "y"), token)
    mixed, token = gather_rows(
        jnp.concatenate(
            [to_half(encoder_output), to_half(encoder_expand), to_half(predictor_embed)], 1
        ),
        ("y", "x"),
        token,
    )
    output = mixed[:, :width]
    expand = mixed[:, width : width + hidden]
    embed = mixed[:, width + hidden :]
    reduce, token = gather_rows(to_half(encoder_reduce), ("x", "y"), token)
    shard_rows = predictor_weights.shape[0]
    predictor, token = gather_rows(
        to_half(predictor_weights).reshape(shard_rows, 3 * pred_width), ("y", "x"), token
    )
    pred_projection = predictor_projection(predictor[: 3 * pred_width, :pred_width])
    pred_output = predictor[3 * pred_width :, :pred_width]
    pred_expand = predictor[:, pred_width : 2 * pred_width]
    pred_reduce = predictor[:, 2 * pred_width :]

    embedded = product(pixels, patch) + encoder_biases[0]
    normed = to_half(layer_norm(embedded, encoder_gains[0], encoder_biases[1]))
    qkv = to_heads(to_half(product(normed, attention)), 3 * pair)
    mixed_heads, logs = attend(qkv, labels)
    attended = to_tokens(mixed_heads).reshape(-1, width)
    encoded, encoder_saved = feed_forward(
        embedded,
        attended,
        lambda v: product(v, output),
        lambda v: product(v, expand),
        lambda v: product(v, reduce),
        encoder_gains,
        encoder_biases,
    )
    encoded_half = to_half(encoded)
    predictor_in = product(encoded_half, embed) + predictor_biases[0]
    pred_normed = to_half(layer_norm(predictor_in, predictor_gains[0], predictor_biases[1]))
    pred_pair = pred_projection.shape[0] // (3 * PLANE)
    pred_qkv = to_heads(to_half(right_product(pred_normed, pred_projection)), 3 * pred_pair)
    pred_heads, pred_logs = attend(pred_qkv, labels)
    pred_attended = slots_back(jnp.moveaxis(to_tokens(pred_heads), 0, 2)).T
    prediction, pred_saved = feed_forward(
        predictor_in,
        pred_attended,
        lambda v: right_product(v, pred_output),
        lambda v: right_product(v, pred_expand),
        lambda v: product(v, pred_reduce),
        predictor_gains,
        predictor_biases,
    )

    grad_middle, result_half, expanded_half, pred_sums = feed_backward(
        to_full(cotangent),
        pred_saved,
        predictor_gains,
        predictor_biases,
        lambda v: right_product(v, pred_reduce),
        lambda v: product(v, pred_expand),
    )
    middle_half = to_half(grad_middle)
    pred_reduce_grad = to_half(left_product(pred_saved[3], result_half))
    pred_expand_grad = to_half(left_product(expanded_half, pred_saved[1]))
    pred_output_grad = to_half(left_product(middle_half, pred_attended))
    grad_attended = to_half(product(middle_half, pred_output))
    grad_heads = to_heads(
        jnp.moveaxis(slots(grad_attended, 1), 2, 0).reshape(-1, PLANE * pred_pair), pred_pair
    )
    grad_qkv = attend_back(pred_qkv, pred_heads, grad_heads, pred_logs, labels)
    grad_projected = to_tokens(grad_qkv).reshape(-1, 3 * PLANE * pred_pair)
    pred_projection_grad = predictor_projection_back(
        to_half(left_product(grad_projected, pred_normed))
    )
    grad_normed = product(grad_projected, pred_projection)
    value, pull = jax.vjp(layer_norm, predictor_in, predictor_gains[0], predictor_biases[1])
    grad_into_norm, pred_gain_one, pred_bias_one = pull(grad_normed)
    grad_pred_in = grad_middle + grad_into_norm
    predictor_grad = scatter_rows(
        [jnp.concatenate([pred_projection_grad, pred_output_grad], 0), pred_expand_grad, pred_reduce_grad],
        ("x", "y"),
    )
    pred_in_half = to_half(grad_pred_in)
    grad_encoded = right_product(pred_in_half, embed)
    embed_grad = to_half(left_product(encoded_half, pred_in_half))

    grad_middle, result_half, expanded_half, sums = feed_backward(
        grad_encoded,
        encoder_saved,
        encoder_gains,
        encoder_biases,
        lambda v: right_product(v, reduce),
        lambda v: right_product(v, expand),
    )
    middle_half = to_half(grad_middle)
    reduce_grad = scatter_rows([to_half(left_product(encoder_saved[3], result_half))], ("y", "x"))
    grad_attended = to_half(right_product(middle_half, output))
    mixed_grad = scatter_rows(
        [
            to_half(left_product(attended, middle_half)),
            to_half(left_product(encoder_saved[1], expanded_half)),
            embed_grad,
        ],
        ("x", "y"),
    )
    grad_heads = to_heads(grad_attended, pair)
    grad_qkv = attend_back(qkv, mixed_heads, grad_heads, logs, labels)
    grad_projected = to_tokens(grad_qkv).reshape(-1, 3 * width)
    attention_grad = scatter_rows([to_half(left_product(normed, grad_projected))], ("y", "x"))
    grad_normed = right_product(grad_projected, attention)
    value, pull = jax.vjp(layer_norm, embedded, encoder_gains[0], encoder_biases[1])
    grad_into_norm, gain_one, bias_one = pull(grad_normed)
    grad_embedded = grad_middle + grad_into_norm
    embedded_half = to_half(grad_embedded)
    patch_grad = scatter_rows([to_half(left_product(pixels, embedded_half))], ("x", "y"))
    pixel_grad = to_half(right_product(embedded_half, patch))

    vectors = [
        gain_one,
        sums[4],
        jnp.sum(grad_embedded, 0),
        bias_one,
        sums[0],
        sums[1],
        sums[2],
        sums[3],
        pred_gain_one,
        pred_sums[4],
        jnp.sum(grad_pred_in, 0),
        pred_bias_one,
        pred_sums[0],
        pred_sums[1],
        pred_sums[2],
        pred_sums[3],
    ]
    total = total_over_devices(jnp.concatenate(vectors).reshape(-1, 128)).reshape(-1)
    split = 11 * width
    encoder_vectors = total[:split].reshape(11, width)
    predictor_vectors = total[split:].reshape(11, pred_width)
    return (
        to_half(prediction),
        pixel_grad,
        patch_grad,
        encoder_columns_back(attention_grad),
        mixed_grad[:, :width],
        mixed_grad[:, width : width + hidden],
        reduce_grad,
        mixed_grad[:, width + hidden :],
        predictor_grad.reshape(shard_rows, 3, pred_width),
        encoder_vectors[:2],
        encoder_vectors[2:],
        predictor_vectors[:2],
        predictor_vectors[2:],
    )


def solution(mesh):
    wide, narrow = mesh.devices.shape
    fine = Mesh(mesh.devices.reshape(wide // 2, 2, narrow // 2, 2), AXES)
    rows = P(AXES, None)
    rows_three = P(AXES, None, None)
    in_specs = (rows, P(), rows, rows, rows, rows, rows, rows, rows_three, P(), P(), P(), P(), rows)
    out_specs = (rows,) * 8 + (rows_three, P(), P(), P(), P())
    return jax.shard_map(
        per_device, mesh=fine, in_specs=in_specs, out_specs=out_specs, check_vma=False
    )
```

```python
import functools
import itertools

import jax
import jax.numpy as jnp
from jax import lax
from jax.experimental import pallas as pl
from jax.experimental.pallas import tpu as pltpu
from jax.sharding import Mesh
from jax.sharding import PartitionSpec as P

HEADS = 16
PRED_HEADS = 12

EPSILON = 1e-06
GELU_SCALE = 0.7978845608028654
LOG2E = 1.4426950408889634
MASKED = -1e30

PLANE = 8
BLOCK = 256
CLIP_LOW = 224
CLIP_HIGH = 1824
MARGIN = 32
CLIP_ID = 2

AXES = ("z", "y", "x", "c")
GROUP_AXES = ("y", "x", "c")
CHIP_AXES = ("y", "x")
VMEM_LIMIT = 48 * 1024 * 1024


def swap(value, axis, distance=1):
    size = lax.axis_size(axis)
    return lax.ppermute(value, axis, [(i, i ^ distance) for i in range(size)])


class Order:
    def __init__(self):
        self.clock = ()

    def enter(self, *values):
        if self.clock:
            values = lax.optimization_barrier(values + self.clock)[: len(values)]
        return values if len(values) > 1 else values[0]

    def leave(self, *values):
        self.clock = values
        return values if len(values) > 1 else values[0]


def to_half(values):
    return values.astype(jnp.bfloat16)


def to_full(values):
    return values.astype(jnp.float32)


def product(left, right):
    return jnp.dot(left, right, preferred_element_type=jnp.float32)


def left_product(left, right):
    return lax.dot_general(
        left, right, (((0,), (0,)), ((), ())), preferred_element_type=jnp.float32
    )


def position(axis):
    if isinstance(axis, tuple):
        return lax.axis_index(axis[0]) // axis[1] % 2
    return lax.axis_index(axis)


def leading(value):
    return list(itertools.product(*(range(n) for n in value.shape[:-2])))


def aligned(value):
    return value.shape[-2] % 16 == 0


def small_kernel(kernel, outs, ins, axes, name):
    bits = jnp.stack([position(axis) for axis in axes]).astype(jnp.int32)
    vmem = pl.BlockSpec(memory_space=pltpu.VMEM)
    return pl.pallas_call(
        kernel,
        out_shape=[jax.ShapeDtypeStruct(shape, jnp.bfloat16) for shape in outs],
        in_specs=[pl.BlockSpec(memory_space=pltpu.SMEM)] + [vmem] * len(ins),
        out_specs=[vmem] * len(outs),
        compiler_params=pltpu.CompilerParams(vmem_limit_bytes=VMEM_LIMIT),
        name=name,
    )(bits, *ins)


def join(items):
    shapes = [own.shape[:at] + (2,) + own.shape[at:] for own, _, _, at in items]
    if not aligned(items[0][0]):
        low = [position(axis) == 0 for _, _, axis, _ in items]
        return [
            jnp.stack([jnp.where(l, own, got), jnp.where(l, got, own)], at)
            for l, (own, got, _, at) in zip(low, items)
        ]

    def kernel(bits, *refs):
        outs = refs[2 * len(items) :]
        for i, (own, got, _, at) in enumerate(items):
            for index in leading(own):
                for bit, ref in ((bits[i], refs[2 * i]), (1 - bits[i], refs[2 * i + 1])):
                    outs[i][index[:at] + (bit,) + index[at:]] = ref[index]

    ins = [v for own, got, _, _ in items for v in (own, got)]
    return small_kernel(kernel, shapes, ins, [axis for _, _, axis, _ in items], "join")


def join_all(one, got_one, two, got_two):
    if not aligned(one):
        first, second = join([(one, got_one, "x", 2), (two, got_two, "y", 1)])
        return jnp.concatenate([first, second], 0)
    half = one.shape[0]

    def kernel(bits, one, got_one, two, got_two, out):
        for h, k in itertools.product(range(half), range(2)):
            out[h, k, bits[0]] = one[h, k]
            out[h, k, 1 - bits[0]] = got_one[h, k]
            out[half + h, bits[1], k] = two[h, k]
            out[half + h, 1 - bits[1], k] = got_two[h, k]

    shape = (2 * half, 2) + one.shape[1:]
    return small_kernel(kernel, [shape], [one, got_one, two, got_two], ["x", "y"], "join_all")[0]


def in_turn(own, got, axis):
    if not aligned(own):
        low = position(axis) == 0
        return [jnp.where(low, own, got), jnp.where(low, got, own)]

    def kernel(bits, own, got, first, second):
        for index in leading(own):
            low = bits[0] == 0
            first[index] = jnp.where(low, own[index], got[index])
            second[index] = jnp.where(low, got[index], own[index])

    return small_kernel(kernel, [own.shape] * 2, [own, got], [axis], "in_turn")


def split(items):
    if not aligned(items[0][0][0]):
        outs = []
        for parts, axis, at in items:
            total = to_half(sum(to_full(p) for p in parts))
            for index in (position(axis), 1 - position(axis)):
                outs.append(lax.dynamic_index_in_dim(total, index, at, keepdims=False))
        return outs
    shapes = [p[0].shape[:at] + p[0].shape[at + 1 :] for p, _, at in items]

    def kernel(bits, *refs):
        outs = refs[sum(len(p) for p, _, _ in items) :]
        start = 0
        for i, (parts, _, at) in enumerate(items):
            ins = refs[start : start + len(parts)]
            start += len(parts)
            for index in leading(outs[2 * i]):
                for bit, out in ((bits[i], outs[2 * i]), (1 - bits[i], outs[2 * i + 1])):
                    where = index[:at] + (bit,) + index[at:]
                    if len(ins) == 1:
                        out[index] = ins[0][where]
                    else:
                        out[index] = to_half(sum(to_full(ref[where]) for ref in ins))

    ins = [v for parts, _, _ in items for v in parts]
    outs = [shape for shape in shapes for _ in range(2)]
    return small_kernel(kernel, outs, ins, [axis for _, axis, _ in items], "split")


def split_halves(one, two, axis):
    if not aligned(one[0]):
        first, second = (to_half(sum(to_full(p) for p in parts)) for parts in (one, two))
        low = position(axis) == 0
        return jnp.where(low, first, second), jnp.where(low, second, first)

    def kernel(bits, *refs):
        keep, send = refs[-2:]
        for index in leading(keep):
            first = to_half(sum(to_full(ref[index]) for ref in refs[: len(one)]))
            second = to_half(sum(to_full(ref[index]) for ref in refs[len(one) : -2]))
            low = bits[0] == 0
            keep[index] = jnp.where(low, first, second)
            send[index] = jnp.where(low, second, first)

    return small_kernel(kernel, [one[0].shape] * 2, [*one, *two], [axis], "split_halves")


class Gather:
    def __init__(self, order, shard, both=False):
        self.order, self.both, self.distance = order, both, 1
        self.held = shard

    def along_z(self):
        if self.distance == 1:
            held = self.order.enter(self.held)[None]
        else:
            held, got = self.order.enter(self.held, self.flight)
            held = join([(held, got, ("z", self.distance // 2), 0)])[0]
            held = held.reshape((-1,) + held.shape[2:])
        self.held = self.order.leave(held)
        self.flight = swap(self.held, "z", self.distance)
        self.distance *= 2

    def rest_of_z(self):
        while self.distance < lax.axis_size("z"):
            self.along_z()

    def first(self):
        held, got = self.order.enter(self.held, self.flight)
        self.held = self.order.leave(*in_turn(held, got, ("z", self.distance // 2)))
        self.flight = [swap(self.held[0], "y"), swap(self.held[1], "x")]

    def second(self):
        one, two, *got = self.order.enter(*self.held, *self.flight)
        self.held = self.order.leave(*join([(one, got[0], "y", 1), (two, got[1], "x", 1)]))
        self.flight = [swap(self.held[0], "x"), swap(self.held[1], "y")]

    def done(self):
        one, two, *got = self.order.enter(*self.held, *self.flight)
        held = self.order.leave(join_all(one, got[0], two, got[1]))
        if self.both:
            self.held, self.flight = held, swap(held, "c")
        else:
            self.own = held.reshape(-1, held.shape[-1])

    def cores(self):
        held, got = self.order.enter(self.held, self.flight)
        whole = join([(held, got, "c", 3)])[0]
        self.whole = whole.reshape(-1, whole.shape[-1])


class Scatter:
    def __init__(self, order, grads):
        self.order, self.distance = order, 0
        self.start([grads.reshape(lax.axis_size("z"), 2, 2, -1, grads.shape[-1])])

    @classmethod
    def of_cores(cls, order, grads):
        self = cls.__new__(cls)
        self.order, self.distance = order, 0
        view = grads.reshape(lax.axis_size("z"), 2, 2, 2, -1, grads.shape[-1])
        keep, send = split([([view], "c", 3)])
        self.held, self.flight = keep, swap(order.leave(send), "c")
        return self

    def first(self):
        got = self.order.enter(self.flight)
        self.start([self.held, got])

    def start(self, parts):
        half = parts[0].shape[0] // 2
        one, two = [p[:half] for p in parts], [p[half:] for p in parts]
        keep_one, send_one, keep_two, send_two = split([(one, "x", 2), (two, "y", 1)])
        sent = self.order.leave(send_one, send_two)
        self.held = [keep_one, keep_two]
        self.flight = [swap(sent[0], "x"), swap(sent[1], "y")]

    def second(self):
        got = self.order.enter(*self.flight)
        one, two = ([h, g] for h, g in zip(self.held, got))
        keep_one, send_one, keep_two, send_two = split([(one, "y", 1), (two, "x", 1)])
        sent = self.order.leave(send_one, send_two)
        self.held = [keep_one, keep_two]
        self.flight = [swap(sent[0], "y"), swap(sent[1], "x")]

    def along_z(self):
        if self.distance == 0:
            got = self.order.enter(*self.flight)
            one, two = ([h, g] for h, g in zip(self.held, got))
            self.distance = lax.axis_size("z") // 2
            keep, send = split_halves(one, two, ("z", self.distance))
        else:
            self.distance //= 2
            got = self.order.enter(self.flight)
            parts = [v.reshape((2, -1) + v.shape[1:]) for v in (self.held, got)]
            keep, send = split([(parts, ("z", self.distance), 0)])
        self.held = keep
        self.flight = swap(self.order.leave(send), "z", self.distance)

    def rest_of_z(self):
        while self.distance > 1:
            self.along_z()

    def done(self):
        got = self.order.enter(self.flight)
        self.total = self.order.leave(to_half(to_full(self.held[0]) + to_full(got[0])))

    def column_halves(self):
        total = self.total.reshape(2, -1, self.total.shape[-1])
        core = lax.axis_index("c")
        mine = lax.dynamic_index_in_dim(total, core, 0, False)
        theirs = swap(lax.dynamic_index_in_dim(total, 1 - core, 0, False), "c")
        low = core == 0
        return to_full(jnp.where(low, mine, theirs)), to_full(jnp.where(low, theirs, mine))


def both_rows(keep, send):
    got = swap(send, "c")
    low = lax.axis_index("c") == 0
    return jnp.where(low, jnp.concatenate([keep, got], 0), jnp.concatenate([got, keep], 0))


def column_half(value, other=False):
    size = value.shape[-1] // 2
    core = lax.axis_index("c")
    return lax.dynamic_slice_in_dim(value, (1 - core if other else core) * size, size, value.ndim - 1)


def odd_blocks(value, other=False):
    core = lax.axis_index("c")
    blocks = value.reshape(value.shape[0], -1, 2, 128)
    return lax.dynamic_index_in_dim(blocks, 1 - core if other else core, 2, False).reshape(
        value.shape[0], -1
    )


def nt(left, right):
    return lax.dot_general(
        left, right, (((1,), (1,)), ((), ())), preferred_element_type=jnp.float32
    )


def norm_parts(values):
    center = values - jnp.mean(values, -1, keepdims=True)
    factor = lax.rsqrt(jnp.mean(center * center, -1, keepdims=True) + EPSILON)
    return center * factor, factor


def norm(values, gain, bias):
    return norm_parts(values)[0] * gain + bias


def norm_back(values, gain, grad):
    shape, factor = norm_parts(values)
    inner = grad * gain
    mean = jnp.mean(inner, -1, keepdims=True)
    along = jnp.mean(inner * shape, -1, keepdims=True)
    return (
        factor * (inner - mean - shape * along),
        jnp.sum(grad * shape, 0, keepdims=True),
        jnp.sum(grad, 0, keepdims=True),
    )


def gate(values):
    return 0.5 * values * (1.0 + jnp.tanh(GELU_SCALE * (values + 0.044715 * values * values * values)))


def gate_slope(values):
    square = values * values
    slope = jnp.tanh(GELU_SCALE * values * (1.0 + 0.044715 * square))
    return 0.5 * (1.0 + slope) + 0.5 * values * (1.0 - slope * slope) * (
        GELU_SCALE * (1.0 + 3 * 0.044715 * square)
    )


def columns(side, size, start=0, width=None):
    return pl.ds(pl.multiple_of(side * size + start, 128), size if width is None else width)


def run(kernel, outs, ins, grid=(), in_specs=None, out_specs=None, scratch=(), name=None, **more):
    whole = pl.BlockSpec(memory_space=pltpu.VMEM)
    in_specs = in_specs or {}
    out_specs = out_specs or {}

    def spec(given, value):
        if given is not None:
            return given
        if not grid:
            return whole
        return pl.BlockSpec(value.shape, lambda *_, rank=len(value.shape): (0,) * rank)

    core = lax.axis_index("c").astype(jnp.int32).reshape(1)
    outs = [jax.ShapeDtypeStruct(shape, dtype) for shape, dtype in outs]
    return pl.pallas_call(
        kernel,
        out_shape=outs,
        grid=grid,
        in_specs=[pl.BlockSpec(memory_space=pltpu.SMEM)]
        + [spec(in_specs.get(i), v) for i, v in enumerate(ins)],
        out_specs=[spec(out_specs.get(i), v) for i, v in enumerate(outs)],
        scratch_shapes=scratch,
        compiler_params=pltpu.CompilerParams(vmem_limit_bytes=VMEM_LIMIT),
        name=name,
        **more,
    )(core, *ins)


HALF = jnp.bfloat16
FULL = jnp.float32


def embed_kernel(core, mine, theirs, weight, out_mine, out_theirs):
    out_mine[...] = product(mine[...], weight[...])
    out_theirs[...] = product(theirs[...], weight[...])


def embed_tokens(mine, theirs, weight):
    shape = ((mine.shape[0], weight.shape[1]), FULL)
    return run(embed_kernel, [shape, shape], [mine, theirs, weight], name="embed_tokens")


def norm_kernel(core, mine, got, gains, biases, embedded, normed):
    size = mine.shape[1]
    embedded[:, columns(core[0], size)] = mine[...]
    embedded[:, columns(1 - core[0], size)] = got[...]
    values = embedded[...] + biases[0:1]
    embedded[...] = values
    normed[...] = to_half(norm(values, gains[0:1], biases[1:2]))


def norm_tokens(mine, got, gains, biases):
    shape = (mine.shape[0], gains.shape[1])
    return run(
        norm_kernel, [(shape, FULL), (shape, HALF)], [mine, got, gains, biases], name="norm_tokens"
    )


def token_rows(side, rows):
    return pl.ds(pl.multiple_of(side * rows, rows), rows)


def project_kernel(core, mine, got, weight, both, out):
    rows = mine.shape[0]

    @pl.when(pl.program_id(0) == 0)
    def _():
        both[token_rows(core[0], rows), :] = mine[...]
        both[token_rows(1 - core[0], rows), :] = got[...]

    out[0] = to_half(product(both[...], weight[...]))


def project_tokens(mine, got, weight):
    rows, width = mine.shape
    each = weight.shape[1] // 4
    return run(
        project_kernel,
        [((2 * rows, width), HALF), ((4, 2 * rows, each), HALF)],
        [mine, got, weight],
        grid=(4,),
        in_specs={2: pl.BlockSpec((width, each), lambda j: (0, j))},
        out_specs={1: pl.BlockSpec((1, 2 * rows, each), lambda j: (j, 0, 0))},
        name="project_tokens",
    )


def middle_kernel(
    core, embedded, parts, got, weight, gains, biases, attended, middle, second
):
    rows = got.shape[1]
    each = parts.shape[2]
    width = embedded.shape[1]
    for q in range(4):
        attended[:, columns(core[0], 4 * each, q * each, each)] = parts[
            q, token_rows(core[0], rows), :
        ]
        attended[:, columns(1 - core[0], 4 * each, q * each, each)] = got[q]
    values = embedded[...] + product(attended[...], weight[:, :width]) + biases[2:3]
    middle[...] = values
    second[...] = to_half(norm(values, gains[1:2], biases[3:4]))


def middle_tokens(embedded, parts, got, weight, gains, biases):
    shape = embedded.shape
    return run(
        middle_kernel,
        [(shape, HALF), (shape, FULL), (shape, HALF)],
        [embedded, parts, got, weight, gains, biases],
        name="middle_tokens",
    )


def expand_kernel(core, mine, got, weight, bias, both, expanded, activated):
    rows = mine.shape[0]

    @pl.when(pl.program_id(0) == 0)
    def _():
        both[:rows, :] = mine[...]
        both[rows:, :] = got[...]

    values = product(both[...], weight[...]) + bias[...]
    expanded[...] = values
    activated[...] = to_half(gate(values))


def expand_tokens(mine, got, weight, bias):
    rows, width = mine.shape
    hidden = weight.shape[1]
    tile = pl.BlockSpec((2 * rows, 512), lambda j: (0, j))
    return run(
        expand_kernel,
        [((2 * rows, width), HALF), ((2 * rows, hidden), FULL), ((2 * rows, hidden), HALF)],
        [mine, got, weight, bias],
        grid=(hidden // 512,),
        in_specs={
            2: pl.BlockSpec((width, 512), lambda j: (0, j)),
            3: pl.BlockSpec((1, 512), lambda j: (0, j)),
        },
        out_specs={1: tile, 2: tile},
        name="expand_tokens",
    )


def reduce_kernel(core, activated, weight, mine, theirs, total):
    step = pl.program_id(0)
    rows = mine.shape[0]
    values = product(activated[...], weight[...])

    @pl.when(step == 0)
    def _():
        total[...] = values

    @pl.when(step > 0)
    def _():
        total[...] += values

    @pl.when(step == pl.num_programs(0) - 1)
    def _():
        mine[...] = total[:rows, :]
        theirs[...] = total[rows:, :]


def reduce_tokens(activated, weight):
    rows, hidden = activated.shape
    width = weight.shape[1]
    shape = ((rows // 2, width), FULL)
    return run(
        reduce_kernel,
        [shape, shape],
        [activated, weight],
        grid=(hidden // 512,),
        in_specs={
            0: pl.BlockSpec((rows, 512), lambda j: (0, j)),
            1: pl.BlockSpec((512, width), lambda j: (j, 0)),
        },
        scratch=[pltpu.VMEM((rows, width), FULL)],
        name="reduce_tokens",
    )


def slot_of(p, size):
    return (2 * p * size, 2 * size) if p < 4 else (8 * size + (p - 4) * size, size)


def encode_kernel(
    core, middle, mine, got, weight, biases, pred_weight, pred_gains, pred_biases,
    encoded, pred_in, normed, parts, projected,
):
    full = middle.shape[1]
    encoded[...] = to_half(middle[...] + (mine[...] + got[...]) + biases[4:5])
    values = product(encoded[...], weight[:, full:]) + pred_biases[0:1]
    pred_in[...] = values
    normed[...] = to_half(norm(values, pred_gains[0:1], pred_biases[1:2]))
    width = values.shape[1]
    projected[...] = nt(normed[...], pred_weight[...])
    both = parts.shape[2] // 3
    for p in range(PLANE):
        start, size = slot_of(p, both // 2)
        for t in range(3):
            parts[p, :, t * both : t * both + size] = to_half(
                projected[:, t * width + start : t * width + start + size]
            )
            if size < both:
                parts[p, :, t * both + size : (t + 1) * both] = jnp.zeros(
                    (parts.shape[1], both - size), HALF
                )


def encode_tokens(middle, mine, got, weight, biases, pred_weights, pred_gains, pred_biases):
    rows = middle.shape[0]
    width = pred_gains.shape[1]
    each = 3 * 2 * width // PRED_HEADS
    return run(
        encode_kernel,
        [
            (middle.shape, HALF),
            ((rows, width), FULL),
            ((rows, width), HALF),
            ((PLANE, rows, each), HALF),
        ],
        [middle, mine, got, weight, biases, pred_weights, pred_gains, pred_biases],
        grid=(1,),
        in_specs={5: pl.BlockSpec((3 * width, width), lambda j: (0, 0))},
        scratch=[pltpu.VMEM((rows, 3 * width), FULL)],
        name="encode_tokens",
    )


def pred_feed_kernel(
    core, pred_in, parts, weights, gains, biases, hidden_bias, cotangent,
    prediction, grad_middle, grad_weights, grad_parts, sums, hidden_sums, attended, expanded, work,
):
    width = pred_in.shape[1]
    both = parts.shape[2]
    for p in range(PLANE):
        start, size = slot_of(p, both // 2)
        attended[:, start : start + size] = parts[p, :, :size]
    out_rows = slice(3 * width, weights.shape[0])
    slot = [slice(i * width, (i + 1) * width) for i in range(3)]
    middle = pred_in[...] + nt(attended[...], weights[out_rows, slot[0]]) + biases[2:3]
    second = to_half(norm(middle, gains[1:2], biases[3:4]))
    expanded[...] = nt(second, weights[:, slot[1]]) + hidden_bias[...]
    activated = to_half(gate(expanded[...]))
    result = middle + product(activated, weights[:, slot[2]]) + biases[4:5]
    prediction[...] = to_half(result)
    half_grad = cotangent[...]
    grad = to_full(half_grad)
    sums[2:3, :] = jnp.sum(grad, 0, keepdims=True)
    grad_weights[:, slot[2]] = to_half(left_product(activated, half_grad))
    grad_expanded = nt(half_grad, weights[:, slot[2]]) * gate_slope(expanded[...])
    hidden_sums[...] = jnp.sum(grad_expanded, 0, keepdims=True)
    expanded_half = to_half(grad_expanded)
    grad_weights[:, slot[1]] = to_half(left_product(expanded_half, second))
    grad_second = product(expanded_half, weights[:, slot[1]])
    from_norm, gain, bias = norm_back(middle, gains[1:2], grad_second)
    total = grad + from_norm
    grad_middle[...] = total
    sums[0:1, :] = jnp.sum(total, 0, keepdims=True)
    sums[1:2, :] = bias
    sums[3:4, :] = gain
    sums[4:8, :] = jnp.zeros((4, width), FULL)
    middle_half = to_half(total)
    grad_weights[out_rows, slot[0]] = to_half(left_product(middle_half, attended[...]))
    work[...] = product(middle_half, weights[out_rows, slot[0]])
    for p in range(PLANE):
        start, size = slot_of(p, both // 2)
        grad_parts[p, :, :size] = to_half(work[:, start : start + size])
        if size < both:
            grad_parts[p, :, size:] = jnp.zeros((parts.shape[1], both - size), HALF)


def pred_feed(pred_in, parts, weights, gains, biases, cotangent):
    rows, width = pred_in.shape
    hidden = weights.shape[0]
    return run(
        pred_feed_kernel,
        [
            ((rows, width), HALF),
            ((rows, width), FULL),
            (weights.shape, HALF),
            (parts.shape, HALF),
            ((8, width), FULL),
            ((1, hidden), FULL),
        ],
        [pred_in, parts, weights, gains, biases, biases[5:].reshape(1, hidden), cotangent],
        scratch=[
            pltpu.VMEM((rows, width), HALF),
            pltpu.VMEM((rows, hidden), FULL),
            pltpu.VMEM((rows, width), FULL),
        ],
        name="pred_feed",
    )


def pred_back_kernel(
    core, parts, normed, pred_in, grad_middle, weight, gains, embed, _,
    grad_weight, half_in, grad_encoded, encoded_half, sums, projected,
):
    width = pred_in.shape[1]
    both = parts.shape[2] // 3
    for p in range(PLANE):
        start, size = slot_of(p, both // 2)
        for t in range(3):
            projected[:, t * width + start : t * width + start + size] = parts[
                p, :, t * both : t * both + size
            ]
    grad_weight[...] = to_half(left_product(projected[...], normed[...]))
    grad_normed = product(projected[...], weight[...])
    into_norm, gain, bias = norm_back(pred_in[...], gains[0:1], grad_normed)
    total = grad_middle[...] + into_norm
    sums[0:1, :] = jnp.sum(total, 0, keepdims=True)
    sums[1:2, :] = bias
    sums[2:3, :] = gain
    sums[3:8, :] = jnp.zeros((5, width), FULL)
    half_in[...] = to_half(total)
    values = nt(half_in[...], embed[:, embed.shape[1] - width :])
    grad_encoded[...] = values
    encoded_half[...] = to_half(values)


def pred_back(parts, normed, pred_in, grad_middle, weights, gains, embed, grad_weights):
    rows, width = pred_in.shape
    full = embed.shape[0]
    block = pl.BlockSpec((3 * width, width), lambda j: (0, 0))
    return run(
        pred_back_kernel,
        [
            (grad_weights.shape, HALF),
            ((rows, width), HALF),
            ((rows, full), FULL),
            ((rows, full), HALF),
            ((8, width), FULL),
        ],
        [parts, normed, pred_in, grad_middle, weights, gains, embed, grad_weights],
        grid=(1,),
        in_specs={4: block, 7: pl.BlockSpec(memory_space=pl.ANY)},
        out_specs={0: block},
        scratch=[pltpu.VMEM((rows, 3 * width), HALF)],
        name="pred_back",
        input_output_aliases={8: 0},
    )


def reduce_back_kernel(core, mine, got, weight, expanded, both, out, sums):
    rows = mine.shape[0]

    @pl.when(pl.program_id(0) == 0)
    def _():
        both[:rows, :] = mine[...]
        both[rows:, :] = got[...]

    values = nt(both[...], weight[...]) * gate_slope(expanded[...])
    out[...] = to_half(values)
    sums[...] = jnp.sum(values, 0, keepdims=True)


def reduce_back(mine, got, weight, expanded):
    rows, hidden = expanded.shape
    width = mine.shape[1]
    tile = pl.BlockSpec((rows, 512), lambda j: (0, j))
    return run(
        reduce_back_kernel,
        [((rows, width), HALF), ((rows, hidden), HALF), ((1, hidden), FULL)],
        [mine, got, weight, expanded],
        grid=(hidden // 512,),
        in_specs={2: pl.BlockSpec((512, width), lambda j: (j, 0)), 3: tile},
        out_specs={1: tile, 2: pl.BlockSpec((1, 512), lambda j: (0, j))},
        name="reduce_back",
    )


def expand_back_kernel(core, grad, weight, mine, theirs, total):
    step = pl.program_id(0)
    rows = mine.shape[0]
    values = nt(grad[...], weight[...])

    @pl.when(step == 0)
    def _():
        total[...] = values

    @pl.when(step > 0)
    def _():
        total[...] += values

    @pl.when(step == pl.num_programs(0) - 1)
    def _():
        mine[...] = total[:rows, :]
        theirs[...] = total[rows:, :]


def expand_back(grad, weight):
    rows, hidden = grad.shape
    width = weight.shape[0]
    shape = ((rows // 2, width), FULL)
    return run(
        expand_back_kernel,
        [shape, shape],
        [grad, weight],
        grid=(hidden // 512,),
        in_specs={
            0: pl.BlockSpec((rows, 512), lambda j: (0, j)),
            1: pl.BlockSpec((width, 512), lambda j: (0, j)),
        },
        scratch=[pltpu.VMEM((rows, width), FULL)],
        name="expand_back",
    )


def middle_back_kernel(
    core, middle, grad, mine, got, gains, weight, grad_middle, half_middle, sums, keep, send, work
):
    width = middle.shape[1]
    from_norm, gain, bias = norm_back(middle[...], gains[1:2], mine[...] + got[...])
    values = grad[...] + from_norm
    grad_middle[...] = values
    sums[0:1, :] = jnp.sum(values, 0, keepdims=True)
    sums[1:2, :] = bias
    sums[2:3, :] = jnp.sum(grad[...], 0, keepdims=True)
    sums[3:4, :] = gain
    sums[4:8, :] = jnp.zeros((4, width), FULL)
    half_middle[...] = to_half(values)
    work[...] = to_half(nt(half_middle[...], weight[:, :width]))
    each = keep.shape[2]
    for q in range(4):
        keep[q] = work[:, columns(core[0], 4 * each, q * each, each)]
        send[q] = work[:, columns(1 - core[0], 4 * each, q * each, each)]


def middle_back(middle, grad, mine, got, gains, weight):
    rows, width = middle.shape
    parts = ((4, rows, width // PLANE), HALF)
    return run(
        middle_back_kernel,
        [((rows, width), FULL), ((rows, width), HALF), ((8, width), FULL), parts, parts],
        [middle, grad, mine, got, gains, weight],
        scratch=[pltpu.VMEM((rows, width), HALF)],
        name="middle_back",
    )


def project_back_kernel(core, parts, weight, mine, theirs, total):
    step = pl.program_id(0)
    rows = mine.shape[0]
    values = nt(parts[0], weight[...])

    @pl.when(step == 0)
    def _():
        total[...] = values

    @pl.when(step > 0)
    def _():
        total[...] += values

    @pl.when(step == pl.num_programs(0) - 1)
    def _():
        mine[...] = total[token_rows(core[0], rows), :]
        theirs[...] = total[token_rows(1 - core[0], rows), :]


def project_back(parts, weight):
    _, rows, each = parts.shape
    width = weight.shape[0]
    shape = ((rows // 2, width), FULL)
    return run(
        project_back_kernel,
        [shape, shape],
        [parts, weight],
        grid=(4,),
        in_specs={
            0: pl.BlockSpec((1, rows, each), lambda j: (j, 0, 0)),
            1: pl.BlockSpec((width, each), lambda j: (0, j)),
        },
        scratch=[pltpu.VMEM((rows, width), FULL)],
        name="project_back",
    )


def input_back_kernel(core, embedded, grad, mine, got, gains, keep, send, sums, work):
    into_norm, gain, bias = norm_back(embedded[...], gains[0:1], mine[...] + got[...])
    values = grad[...] + into_norm
    sums[0:1, :] = jnp.sum(values, 0, keepdims=True)
    sums[1:2, :] = bias
    sums[2:3, :] = gain
    sums[3:8, :] = jnp.zeros((5, values.shape[1]), FULL)
    work[...] = to_half(values)
    size = keep.shape[1]
    keep[...] = work[:, columns(core[0], size)]
    send[...] = work[:, columns(1 - core[0], size)]


def input_back(embedded, grad, mine, got, gains):
    rows, width = embedded.shape
    part = ((rows, width // 2), HALF)
    return run(
        input_back_kernel,
        [part, part, ((8, width), FULL)],
        [embedded, grad, mine, got, gains],
        scratch=[pltpu.VMEM((rows, width), HALF)],
        name="input_back",
    )


def pixel_kernel(core, mine, got, weight, out_mine, out_theirs):
    out_mine[...] = nt(mine[...], weight[...])
    out_theirs[...] = to_half(nt(got[...], weight[...]))


def pixel_back(mine, got, weight):
    shape = (mine.shape[0], weight.shape[0])
    return run(
        pixel_kernel, [(shape, FULL), (shape, HALF)], [mine, got, weight], name="pixel_back"
    )


def weight_kernel(count, core, *refs):
    lefts, rights, out = refs[:count], refs[count : 2 * count], refs[-1]
    if len(rights[0].shape) == 3:
        each = rights[0].shape[2]
        for q in range(rights[0].shape[0]):
            out[:, q * each : (q + 1) * each] = to_half(left_product(lefts[0][...], rights[0][q]))
    else:
        values = left_product(lefts[0][...], rights[0][...])
        for left, right in zip(lefts[1:], rights[1:]):
            values += left_product(left[...], right[...])
        out[...] = to_half(values)


def weight_grad(lefts, rights, name="weight_grad"):
    depth = lefts[0].shape[1]
    right = rights[0]
    width = right.shape[0] * right.shape[2] if right.ndim == 3 else right.shape[1]
    block = 512 if depth % 512 == 0 else 256
    return run(
        functools.partial(weight_kernel, len(lefts)),
        [((depth, width), HALF)],
        [*lefts, *rights],
        grid=(depth // block,),
        in_specs={
            i: pl.BlockSpec((v.shape[0], block), lambda j: (0, j)) for i, v in enumerate(lefts)
        },
        out_specs={0: pl.BlockSpec((block, width), lambda j: (j, 0))},
        name=name,
    )[0]


def side_kernel(core, left_one, left_two, right_one, right_two, out):
    width = right_one.shape[1]
    out[:, :width] = to_half(left_product(left_one[...], right_one[...]))
    out[:, width:] = to_half(left_product(left_two[...], right_two[...]))


def weight_grads(lefts, rights):
    depth = lefts[0].shape[1]
    width = rights[0].shape[1] + rights[1].shape[1]
    tile = pl.BlockSpec((lefts[0].shape[0], 512), lambda j: (0, j))
    return run(
        side_kernel,
        [((depth, width), HALF)],
        [*lefts, *rights],
        grid=(depth // 512,),
        in_specs={0: tile, 1: tile},
        out_specs={0: pl.BlockSpec((512, width), lambda j: (j, 0))},
        name="weight_grads",
    )[0]


def total_over_devices(value):
    for axis in ("c", "x", "y", "z"):
        distance = 1
        while distance < lax.axis_size(axis):
            value = value + swap(value, axis, distance)
            distance *= 2
    return value


def head_lanes(values, head, size):
    lane = lax.broadcasted_iota(jnp.int32, values.shape, 1)
    return jnp.where((lane >= head * size) & (lane < (head + 1) * size), values, jnp.zeros_like(values))


def clip_bias(label_column_ref):
    low = label_column_ref[CLIP_LOW : CLIP_LOW + MARGIN, :]
    high = label_column_ref[CLIP_HIGH - MARGIN : CLIP_HIGH, :]
    return jnp.where(low == CLIP_ID, 0.0, MASKED), jnp.where(high == CLIP_ID, 0.0, MASKED)


def add_margins(scores, biases):
    low, high = biases
    return jnp.concatenate(
        [scores[:MARGIN] + low, scores[MARGIN:-MARGIN], scores[-MARGIN:] + high], 0
    )


def softmax_columns(scores):
    top = jnp.max(scores, 0, keepdims=True)
    expo = jnp.exp2(scores - top)
    total = jnp.sum(expo, 0, keepdims=True)
    return to_half(expo), total, top + jnp.log2(total)


def attend_kernel(size, qkv_ref, column_ref, row_ref, out_ref, log_ref, q_s, k_s, vt_s, ot_s):
    both = 2 * size
    factor = LOG2E * size**-0.5
    q_s[...] = qkv_ref[:, :both]
    k_s[...] = qkv_ref[:, both : 2 * both]
    vt_s[...] = to_half(to_full(qkv_ref[:, 2 * both :]).T)
    biases = clip_bias(column_ref)

    def over_clip(queries):
        keys = k_s[CLIP_LOW:CLIP_HIGH, :]
        values_t = vt_s[:, CLIP_LOW:CLIP_HIGH]
        outs, logs = [], []
        for head in range(2):
            scores = add_margins(nt(keys, head_lanes(queries, head, size)) * factor, biases)
            probs, total, log_total = softmax_columns(scores)
            mixed = product(values_t, probs) / total
            outs.append(mixed[head * size : (head + 1) * size])
            logs.append(log_total)
        return jnp.concatenate(outs, 0), jnp.concatenate(logs, 0)

    def over_block(start):
        keys = k_s[start : start + BLOCK, :]
        values_t = vt_s[:, start : start + BLOCK]
        queries = q_s[start : start + BLOCK, :]
        same = column_ref[start : start + BLOCK, :] == row_ref[:, start : start + BLOCK]
        outs, logs = [], []
        for head in range(2):
            scores = jnp.where(same, nt(keys, head_lanes(queries, head, size)) * factor, MASKED)
            probs, total, log_total = softmax_columns(scores)
            mixed = product(values_t, probs) / total
            outs.append(mixed[head * size : (head + 1) * size])
            logs.append(log_total)
        return jnp.concatenate(outs, 0), jnp.concatenate(logs, 0)

    @pl.loop(1, PLANE - 1)
    def _(block):
        start = pl.multiple_of(block * BLOCK, BLOCK)
        out, logs = over_clip(q_s[pl.ds(start, BLOCK), :])
        ot_s[:, pl.ds(start, BLOCK)] = out
        log_ref[:2, pl.ds(start, BLOCK)] = logs

    last = (PLANE - 1) * BLOCK
    edge_out, edge_logs = over_clip(
        jnp.concatenate(
            [q_s[BLOCK - 128 : BLOCK, :], q_s[last : last + 128, :]], 0
        )
    )
    for start, at, inner in ((0, 128, 0), (last, 0, 128)):
        out, logs = over_block(start)
        ot_s[:, start : start + BLOCK] = out
        log_ref[:2, start : start + BLOCK] = logs
        where = start + at
        clip = row_ref[:, where : where + 128] == CLIP_ID
        ot_s[:, where : where + 128] = jnp.where(
            clip, edge_out[:, inner : inner + 128], ot_s[:, where : where + 128]
        )
        log_ref[:2, where : where + 128] = jnp.where(
            clip, edge_logs[:, inner : inner + 128], log_ref[:2, where : where + 128]
        )
    log_ref[2:, :] = jnp.zeros((6, PLANE * BLOCK), jnp.float32)
    out_ref[...] = to_half(ot_s[...].T)


def attend_back_kernel(
    size, qkv_ref, out_ref, grad_ref, log_ref, column_ref, row_ref, dqkv_ref,
    q_s, k_s, v_s, kt_s, d_s, dqt_s, dk_s, dv_s,
):
    both = 2 * size
    factor = LOG2E * size**-0.5
    scale = size**-0.5
    q_s[...] = qkv_ref[:, :both]
    k_s[...] = qkv_ref[:, both : 2 * both]
    v_s[...] = qkv_ref[:, 2 * both :]
    kt_s[...] = to_half(to_full(qkv_ref[:, both : 2 * both]).T)
    weighted = (to_full(grad_ref[...]) * to_full(out_ref[...])).T
    for head in range(2):
        d_s[head : head + 1, :] = jnp.sum(
            weighted[head * size : (head + 1) * size], 0, keepdims=True
        )
    dk_s[...] = jnp.zeros_like(dk_s)
    dv_s[...] = jnp.zeros_like(dv_s)
    biases = clip_bias(column_ref)

    def pulled(keys, values, keys_t, queries, grads, logs, centres, masked):
        outs, probs_all, scores_all, queries_all, grads_all = [], [], [], [], []
        for head in range(2):
            own_queries = head_lanes(queries, head, size)
            own_grads = head_lanes(grads, head, size)
            probs = jnp.exp2(masked(nt(keys, own_queries) * factor) - logs[head : head + 1])
            pull = nt(values, own_grads)
            grad_scores = to_half(probs * (pull - centres[head : head + 1]))
            outs.append(product(keys_t, grad_scores)[head * size : (head + 1) * size] * scale)
            probs_all.append(to_half(probs))
            scores_all.append(grad_scores)
            queries_all.append(own_queries)
            grads_all.append(own_grads)
        grad_keys = sum(product(s, q) for s, q in zip(scores_all, queries_all)) * scale
        grad_values = sum(product(p, g) for p, g in zip(probs_all, grads_all))
        return jnp.concatenate(outs, 0), grad_keys, grad_values

    def over_clip(queries, grads, logs, centres):
        return pulled(
            k_s[CLIP_LOW:CLIP_HIGH, :],
            v_s[CLIP_LOW:CLIP_HIGH, :],
            kt_s[:, CLIP_LOW:CLIP_HIGH],
            queries,
            grads,
            logs,
            centres,
            lambda scores: add_margins(scores, biases),
        )

    @pl.loop(1, PLANE - 1)
    def _(block):
        start = pl.multiple_of(block * BLOCK, BLOCK)
        here = pl.ds(start, BLOCK)
        out, grad_keys, grad_values = over_clip(
            q_s[here, :], grad_ref[here, :], log_ref[:2, here], d_s[:2, here]
        )
        dqt_s[:, here] = out
        dk_s[CLIP_LOW:CLIP_HIGH, :] += grad_keys
        dv_s[CLIP_LOW:CLIP_HIGH, :] += grad_values

    last = (PLANE - 1) * BLOCK
    near, far = slice(BLOCK - 128, BLOCK), slice(last, last + 128)

    def ends(ref, axis):
        if axis == 0:
            return jnp.concatenate([ref[near, :], ref[far, :]], 0)
        return jnp.concatenate([ref[:2, near], ref[:2, far]], 1)

    edge_labels = jnp.concatenate([row_ref[:, near], row_ref[:, far]], 1)
    edge_logs = jnp.where(edge_labels == CLIP_ID, ends(log_ref, 1), -MASKED)
    edge_out, grad_keys, grad_values = over_clip(
        ends(q_s, 0), ends(grad_ref, 0), edge_logs, ends(d_s, 1)
    )
    dk_s[CLIP_LOW:CLIP_HIGH, :] += grad_keys
    dv_s[CLIP_LOW:CLIP_HIGH, :] += grad_values
    for start, at, inner in ((0, 128, 0), (last, 0, 128)):
        here = slice(start, start + BLOCK)
        labels = row_ref[:, here]
        same = column_ref[here, :] == labels
        logs = jnp.where(labels == CLIP_ID, -MASKED, log_ref[:2, here])
        out, grad_keys, grad_values = pulled(
            k_s[here, :],
            v_s[here, :],
            kt_s[:, here],
            q_s[here, :],
            grad_ref[here, :],
            logs,
            d_s[:2, here],
            lambda scores: jnp.where(same, scores, MASKED),
        )
        dqt_s[:, here] = out
        where = slice(start + at, start + at + 128)
        dqt_s[:, where] += edge_out[:, inner : inner + 128]
        dk_s[here, :] += grad_keys
        dv_s[here, :] += grad_values
    dqkv_ref[:, :both] = to_half(dqt_s[...].T)
    dqkv_ref[:, both : 2 * both] = to_half(dk_s[...])
    dqkv_ref[:, 2 * both :] = to_half(dv_s[...])


def attend(qkv, labels):
    tokens, width = qkv.shape
    both = width // 3
    return pl.pallas_call(
        functools.partial(attend_kernel, both // 2),
        out_shape=(
            jax.ShapeDtypeStruct((tokens, both), jnp.bfloat16),
            jax.ShapeDtypeStruct((8, tokens), jnp.float32),
        ),
        scratch_shapes=[
            pltpu.VMEM((tokens, both), jnp.bfloat16),
            pltpu.VMEM((tokens, both), jnp.bfloat16),
            pltpu.VMEM((both, tokens), jnp.bfloat16),
            pltpu.VMEM((both, tokens), jnp.float32),
        ],
        compiler_params=pltpu.CompilerParams(vmem_limit_bytes=VMEM_LIMIT),
        name="attend",
    )(qkv, labels[:, None], labels[None, :])


def attend_back(qkv, out, grad, logs, labels):
    tokens, width = qkv.shape
    both = width // 3
    return pl.pallas_call(
        functools.partial(attend_back_kernel, both // 2),
        out_shape=jax.ShapeDtypeStruct((tokens, width), jnp.bfloat16),
        scratch_shapes=[
            pltpu.VMEM((tokens, both), jnp.bfloat16),
            pltpu.VMEM((tokens, both), jnp.bfloat16),
            pltpu.VMEM((tokens, both), jnp.bfloat16),
            pltpu.VMEM((both, tokens), jnp.bfloat16),
            pltpu.VMEM((8, tokens), jnp.float32),
            pltpu.VMEM((both, tokens), jnp.float32),
            pltpu.VMEM((tokens, both), jnp.float32),
            pltpu.VMEM((tokens, both), jnp.float32),
        ],
        compiler_params=pltpu.CompilerParams(vmem_limit_bytes=VMEM_LIMIT),
        name="attend_back",
    )(qkv, out, grad, logs, labels[:, None], labels[None, :])


def to_heads(parts, axes):
    moved = lax.all_to_all(parts, axes, split_axis=0, concat_axis=0, tiled=True)
    return moved.reshape(-1, parts.shape[2])


def to_tokens(values, axes):
    count = PLANE // (2 if len(axes) == 2 else 1)
    parts = values.reshape(count, -1, values.shape[1])
    return lax.all_to_all(parts, axes, split_axis=0, concat_axis=0, tiled=True)


def encoder_columns(weight):
    rows, columns = weight.shape
    return weight.reshape(rows, 3, PLANE, -1).transpose(0, 2, 1, 3).reshape(rows, columns)


def encoder_columns_back(weight):
    rows, columns = weight.shape
    return weight.reshape(rows, PLANE, 3, -1).transpose(0, 2, 1, 3).reshape(rows, columns)


def per_device(
    pixels,
    clip_index,
    patch_weight,
    encoder_attention,
    encoder_output,
    encoder_expand,
    encoder_reduce,
    predictor_embed,
    predictor_weights,
    encoder_gains,
    encoder_biases,
    predictor_gains,
    predictor_biases,
    cotangent,
):
    labels = lax.dynamic_index_in_dim(clip_index, lax.axis_index("z"), 0, keepdims=False)
    width = encoder_output.shape[1]
    pred_width = predictor_embed.shape[1]
    hidden = encoder_expand.shape[1]

    order = Order()
    shard_rows = predictor_weights.shape[0]
    rows = pixels.shape[0]
    core = lax.axis_index("c")
    low = core == 0
    wide_columns = encoder_columns(to_half(encoder_attention))
    half_patch, half_expand = to_half(patch_weight), to_half(encoder_expand)
    patch = Gather(order, both_rows(column_half(half_patch), column_half(half_patch, True)))
    attention = Gather(order, both_rows(column_half(wide_columns), column_half(wide_columns, True)))
    expand = Gather(order, both_rows(odd_blocks(half_expand), odd_blocks(half_expand, True)))
    reduce = Gather(order, to_half(encoder_reduce))
    output = Gather(
        order, jnp.concatenate([to_half(encoder_output), to_half(predictor_embed)], 1), True
    )
    predictor = Gather(
        order, to_half(predictor_weights).reshape(shard_rows, 3 * pred_width), True
    )
    hidden_bias = encoder_biases[5:].reshape(-1, 2, 128)
    hidden_bias = lax.dynamic_index_in_dim(hidden_bias, core, 1, False).reshape(1, -1)

    patch.along_z()
    order.leave(attention.held, expand.held)
    pixels_got = swap(pixels, "c")
    attention.along_z()
    patch.rest_of_z()
    patch.first()
    attention.rest_of_z()
    output.along_z()
    patch.second()
    attention.first()
    output.rest_of_z()
    patch.done()
    mine, theirs = embed_tokens(pixels, order.enter(pixels_got), patch.own)
    got = swap(order.leave(theirs), "c")
    attention.second()
    embedded, normed = norm_tokens(mine, order.enter(got), encoder_gains, encoder_biases)
    normed = order.leave(normed)
    normed_got = swap(normed, "c")
    expand.along_z()
    output.first()
    expand.rest_of_z()
    attention.done()

    normed, normed_got = order.enter(normed, normed_got)
    normed_both, parts = project_tokens(normed, normed_got, attention.own)
    qkv = to_heads(order.leave(parts), CHIP_AXES)
    output.second()
    reduce.along_z()
    expand.first()
    reduce.rest_of_z()
    qkv = order.enter(qkv)
    mixed_heads, logs = attend(qkv, labels)
    parts = to_tokens(order.leave(mixed_heads), CHIP_AXES)
    output.done()
    expand.second()
    predictor.along_z()
    output.cores()
    reduce.first()
    predictor.rest_of_z()
    parts = order.enter(parts)
    theirs = lax.dynamic_slice_in_dim(parts, (1 - core) * rows, rows, 1)
    got = swap(order.leave(theirs), "c")
    attended, middle, second = middle_tokens(
        embedded, parts, order.enter(got), output.whole, encoder_gains, encoder_biases
    )
    second = order.leave(second)
    second_got = swap(second, "c")
    expand.done()
    second, second_got = order.enter(second, second_got)
    second_both, expanded, activated = expand_tokens(second, second_got, expand.own, hidden_bias)
    order.leave(activated)
    reduce.second()
    predictor.first()
    reduce.done()
    mine, theirs = reduce_tokens(order.enter(activated), reduce.own)
    got = swap(order.leave(theirs), "c")
    predictor.second()
    predictor.done()
    predictor.cores()
    weights = predictor.whole
    encoded, pred_in, pred_normed, parts = encode_tokens(
        middle,
        mine,
        got,
        output.whole,
        encoder_biases,
        weights,
        predictor_gains,
        predictor_biases,
    )
    pred_qkv = to_heads(parts, GROUP_AXES)
    pred_heads, pred_logs = attend(pred_qkv, labels)
    prediction, pred_middle_grad, pred_grads, parts, pred_sums, pred_hidden_sums = pred_feed(
        pred_in,
        to_tokens(pred_heads, GROUP_AXES),
        weights,
        predictor_gains,
        predictor_biases,
        cotangent,
    )

    grad_qkv = attend_back(
        pred_qkv, pred_heads, to_heads(parts, GROUP_AXES), pred_logs, labels
    )
    pred_grads, half_in, grad_encoded, encoded_half, pred_in_sums = pred_back(
        to_tokens(grad_qkv, GROUP_AXES),
        pred_normed,
        pred_in,
        pred_middle_grad,
        weights,
        predictor_gains,
        output.whole,
        pred_grads,
    )

    encoded_half = order.leave(encoded_half)
    half_got = swap(encoded_half, "c")
    sum_p = Scatter.of_cores(order, order.enter(pred_grads))
    encoded_half, half_got = order.enter(encoded_half, half_got)
    grad_both, grad_expanded, hidden_sums = reduce_back(
        encoded_half, half_got, reduce.own, expanded
    )
    order.leave(grad_expanded)
    sum_r = Scatter(order, weight_grad([activated], [order.enter(grad_both)]))
    mine, theirs = expand_back(order.enter(grad_expanded), expand.own)
    got = swap(order.leave(theirs), "c")
    sum_p.first()
    grad_middle, half_middle, middle_sums, keep, send = middle_back(
        middle, grad_encoded, mine, order.enter(got), encoder_gains, output.whole
    )
    got = swap(order.leave(send), "c")
    sum_e = Scatter(order, weight_grad([second_both], [order.enter(grad_expanded)]))
    keep, got = order.enter(keep, got)
    parts = jnp.where(low, jnp.concatenate([keep, got], 1), jnp.concatenate([got, keep], 1))
    grad_heads = to_heads(order.leave(parts), CHIP_AXES)
    sum_r.second()
    late_middle, late_in = order.enter(half_middle, half_in)
    sum_o = Scatter.of_cores(order, weight_grads([attended, encoded], [late_middle, late_in]))
    sum_p.second()
    grad_heads = order.enter(grad_heads)
    grad_qkv = attend_back(qkv, mixed_heads, grad_heads, logs, labels)
    parts = to_tokens(order.leave(grad_qkv), CHIP_AXES)
    sum_r.along_z()
    sum_o.first()
    sum_e.second()
    sum_r.rest_of_z()
    sum_p.along_z()
    parts = order.enter(parts)
    sum_a = Scatter(order, weight_grad([normed_both], [parts]))
    mine, theirs = project_back(order.enter(parts), attention.own)
    got = swap(order.leave(theirs), "c")
    sum_o.second()
    sum_r.done()
    sum_p.rest_of_z()
    keep, send, out_sums = input_back(
        embedded, grad_middle, mine, order.enter(got), encoder_gains
    )
    got = swap(order.leave(send), "c")
    sum_e.along_z()
    got = order.enter(got)
    sum_k = Scatter(order, weight_grad([pixels, pixels_got], [keep, got]))
    pixel_mine, pixel_theirs = pixel_back(keep, order.enter(got), patch.own)
    pixel_theirs = swap(order.leave(pixel_theirs), "c")
    sum_a.second()
    sum_e.rest_of_z()
    sum_k.second()
    sum_a.along_z()
    sum_e.done()
    sum_o.along_z()
    sum_p.done()
    sum_a.rest_of_z()
    sum_o.rest_of_z()
    sum_k.along_z()
    sum_a.done()
    sum_o.done()
    sum_k.rest_of_z()
    sum_k.done()
    pixel_grad = to_half(pixel_mine + to_full(pixel_theirs))

    patch_grad = jnp.concatenate(sum_k.column_halves(), 1)
    attention_grad = jnp.concatenate(sum_a.column_halves(), 1)
    expand_grad = jnp.stack(
        [v.reshape(v.shape[0], -1, 128) for v in sum_e.column_halves()], 2
    ).reshape(-1, hidden)
    reduce_grad = to_full(sum_r.total)
    output_grad, embed_grad = (to_full(v) for v in jnp.split(sum_o.total, [width], 1))
    predictor_grad = to_full(sum_p.total)
    hidden_sums = jnp.where(
        jnp.arange(2)[None, :, None] == core, hidden_sums.reshape(-1, 1, 128), 0.0
    ).reshape(1, -1)

    vectors = [
        out_sums[2],
        middle_sums[3],
        out_sums[0],
        out_sums[1],
        middle_sums[0],
        middle_sums[1],
        middle_sums[2],
        hidden_sums[0],
        pred_in_sums[2],
        pred_sums[3],
        pred_in_sums[0],
        pred_in_sums[1],
        pred_sums[0],
        pred_sums[1],
        pred_sums[2],
        pred_hidden_sums[0],
    ]
    total = total_over_devices(jnp.concatenate(vectors).reshape(-1, 128)).reshape(-1)
    split = 11 * width
    encoder_vectors = total[:split].reshape(11, width)
    predictor_vectors = total[split:].reshape(11, pred_width)
    return (
        prediction,
        pixel_grad,
        patch_grad,
        encoder_columns_back(attention_grad),
        output_grad,
        expand_grad,
        reduce_grad,
        embed_grad,
        predictor_grad.reshape(shard_rows, 3, pred_width),
        encoder_vectors[:2],
        encoder_vectors[2:],
        predictor_vectors[:2],
        predictor_vectors[2:],
    )


def solution(mesh):
    wide, narrow = mesh.devices.shape
    fine = Mesh(mesh.devices.reshape(wide // 2, 2, narrow // 2, 2), AXES)
    rows = P(AXES, None)
    rows_three = P(AXES, None, None)
    in_specs = (rows, P(), rows, rows, rows, rows, rows, rows, rows_three, P(), P(), P(), P(), rows)
    out_specs = (rows,) * 8 + (rows_three, P(), P(), P(), P())
    return jax.shard_map(
        per_device, mesh=fine, in_specs=in_specs, out_specs=out_specs, check_vma=False
    )
```

```python
import functools
import itertools

import jax
import jax.numpy as jnp
from jax import lax
from jax.experimental import pallas as pl
from jax.experimental.pallas import tpu as pltpu
from jax.sharding import Mesh
from jax.sharding import PartitionSpec as P

HEADS = 16
PRED_HEADS = 12

EPSILON = 1e-06
GELU_SCALE = 0.7978845608028654
LOG2E = 1.4426950408889634
MASKED = -1e30

PLANE = 8
BLOCK = 256
CLIP_LOW = 224
CLIP_HIGH = 1824
MARGIN = 32
CLIP_ID = 2

AXES = ("z", "y", "x", "c")
GROUP_AXES = ("y", "x", "c")
CHIP_AXES = ("y", "x")
VMEM_LIMIT = 48 * 1024 * 1024

COST = {
    "embed_tokens": 2.1,
    "norm_tokens": 1,
    "project_tokens": 4.5,
    "attend": 18,
    "middle_tokens": 3.9,
    "expand_tokens": 7.2,
    "reduce_tokens": 5.5,
    "encode_tokens": 3.5,
    "pred_feed": 6.7,
    "pred_back": 4.3,
    "attend_back": 19,
    "reduce_back": 7.1,
    "weight_grad": 4,
    "weight_grads": 2,
    "expand_back": 6.5,
    "middle_back": 3.9,
    "project_back": 6.5,
    "input_back": 2.2,
    "pixel_back": 1.9,
    "join": 1.5,
    "join_all": 2.5,
    "in_turn": 2,
    "split": 2,
    "split_halves": 1,
}


def estimate(name):
    return pl.CostEstimate(flops=int(COST[name] / 3 * 1.15e9), bytes_accessed=0, transcendentals=0)


def swap(value, axis, distance=1):
    size = lax.axis_size(axis)
    return lax.ppermute(value, axis, [(i, i ^ distance) for i in range(size)])


class Order:
    def __init__(self):
        self.clock = ()

    def enter(self, *values):
        if self.clock:
            values = lax.optimization_barrier(values + self.clock)[: len(values)]
        return values if len(values) > 1 else values[0]

    def leave(self, *values):
        self.clock = values
        return values if len(values) > 1 else values[0]


def to_half(values):
    return values.astype(jnp.bfloat16)


def to_full(values):
    return values.astype(jnp.float32)


def product(left, right):
    return jnp.dot(left, right, preferred_element_type=jnp.float32)


def left_product(left, right):
    return lax.dot_general(
        left, right, (((0,), (0,)), ((), ())), preferred_element_type=jnp.float32
    )


def position(axis):
    if isinstance(axis, tuple):
        return lax.axis_index(axis[0]) // axis[1] % 2
    return lax.axis_index(axis)


def leading(value):
    return list(itertools.product(*(range(n) for n in value.shape[:-2])))


def aligned(value):
    return value.shape[-2] % 16 == 0


def small_kernel(kernel, outs, ins, axes, name):
    bits = jnp.stack([position(axis) for axis in axes]).astype(jnp.int32)
    vmem = pl.BlockSpec(memory_space=pltpu.VMEM)
    return pl.pallas_call(
        kernel,
        out_shape=[jax.ShapeDtypeStruct(shape, jnp.bfloat16) for shape in outs],
        in_specs=[pl.BlockSpec(memory_space=pltpu.SMEM)] + [vmem] * len(ins),
        out_specs=[vmem] * len(outs),
        compiler_params=pltpu.CompilerParams(vmem_limit_bytes=VMEM_LIMIT),
        cost_estimate=estimate(name),
        name=name,
    )(bits, *ins)


def join(items):
    shapes = [own.shape[:at] + (2,) + own.shape[at:] for own, _, _, at in items]
    if not aligned(items[0][0]):
        low = [position(axis) == 0 for _, _, axis, _ in items]
        return [
            jnp.stack([jnp.where(l, own, got), jnp.where(l, got, own)], at)
            for l, (own, got, _, at) in zip(low, items)
        ]

    def kernel(bits, *refs):
        outs = refs[2 * len(items) :]
        for i, (own, got, _, at) in enumerate(items):
            for index in leading(own):
                for bit, ref in ((bits[i], refs[2 * i]), (1 - bits[i], refs[2 * i + 1])):
                    outs[i][index[:at] + (bit,) + index[at:]] = ref[index]

    ins = [v for own, got, _, _ in items for v in (own, got)]
    return small_kernel(kernel, shapes, ins, [axis for _, _, axis, _ in items], "join")


def join_all(one, got_one, two, got_two):
    if not aligned(one):
        first, second = join([(one, got_one, "x", 2), (two, got_two, "y", 1)])
        return jnp.concatenate([first, second], 0)
    half = one.shape[0]

    def kernel(bits, one, got_one, two, got_two, out):
        for h, k in itertools.product(range(half), range(2)):
            out[h, k, bits[0]] = one[h, k]
            out[h, k, 1 - bits[0]] = got_one[h, k]
            out[half + h, bits[1], k] = two[h, k]
            out[half + h, 1 - bits[1], k] = got_two[h, k]

    shape = (2 * half, 2) + one.shape[1:]
    return small_kernel(kernel, [shape], [one, got_one, two, got_two], ["x", "y"], "join_all")[0]


def in_turn(own, got, axis):
    if not aligned(own):
        low = position(axis) == 0
        return [jnp.where(low, own, got), jnp.where(low, got, own)]

    def kernel(bits, own, got, first, second):
        for index in leading(own):
            low = bits[0] == 0
            first[index] = jnp.where(low, own[index], got[index])
            second[index] = jnp.where(low, got[index], own[index])

    return small_kernel(kernel, [own.shape] * 2, [own, got], [axis], "in_turn")


def split(items):
    if not aligned(items[0][0][0]):
        outs = []
        for parts, axis, at in items:
            total = to_half(sum(to_full(p) for p in parts))
            for index in (position(axis), 1 - position(axis)):
                outs.append(lax.dynamic_index_in_dim(total, index, at, keepdims=False))
        return outs
    shapes = [p[0].shape[:at] + p[0].shape[at + 1 :] for p, _, at in items]

    def kernel(bits, *refs):
        outs = refs[sum(len(p) for p, _, _ in items) :]
        start = 0
        for i, (parts, _, at) in enumerate(items):
            ins = refs[start : start + len(parts)]
            start += len(parts)
            for index in leading(outs[2 * i]):
                for bit, out in ((bits[i], outs[2 * i]), (1 - bits[i], outs[2 * i + 1])):
                    where = index[:at] + (bit,) + index[at:]
                    if len(ins) == 1:
                        out[index] = ins[0][where]
                    else:
                        out[index] = to_half(sum(to_full(ref[where]) for ref in ins))

    ins = [v for parts, _, _ in items for v in parts]
    outs = [shape for shape in shapes for _ in range(2)]
    return small_kernel(kernel, outs, ins, [axis for _, axis, _ in items], "split")


def split_halves(one, two, axis):
    if not aligned(one[0]):
        first, second = (to_half(sum(to_full(p) for p in parts)) for parts in (one, two))
        low = position(axis) == 0
        return jnp.where(low, first, second), jnp.where(low, second, first)

    def kernel(bits, *refs):
        keep, send = refs[-2:]
        for index in leading(keep):
            first = to_half(sum(to_full(ref[index]) for ref in refs[: len(one)]))
            second = to_half(sum(to_full(ref[index]) for ref in refs[len(one) : -2]))
            low = bits[0] == 0
            keep[index] = jnp.where(low, first, second)
            send[index] = jnp.where(low, second, first)

    return small_kernel(kernel, [one[0].shape] * 2, [*one, *two], [axis], "split_halves")


class Gather:
    def __init__(self, order, shard, both=False):
        self.order, self.both, self.distance = order, both, 1
        self.held = shard

    def along_z(self):
        if self.distance == 1:
            held = self.order.enter(self.held)[None]
        else:
            held, got = self.order.enter(self.held, self.flight)
            held = join([(held, got, ("z", self.distance // 2), 0)])[0]
            held = held.reshape((-1,) + held.shape[2:])
        self.held = self.order.leave(held)
        self.flight = swap(self.held, "z", self.distance)
        self.distance *= 2

    def rest_of_z(self):
        while self.distance < lax.axis_size("z"):
            self.along_z()

    def first(self):
        held, got = self.order.enter(self.held, self.flight)
        self.held = self.order.leave(*in_turn(held, got, ("z", self.distance // 2)))
        self.flight = [swap(self.held[0], "y"), swap(self.held[1], "x")]

    def second(self):
        one, two, *got = self.order.enter(*self.held, *self.flight)
        self.held = self.order.leave(*join([(one, got[0], "y", 1), (two, got[1], "x", 1)]))
        self.flight = [swap(self.held[0], "x"), swap(self.held[1], "y")]

    def done(self):
        one, two, *got = self.order.enter(*self.held, *self.flight)
        held = self.order.leave(join_all(one, got[0], two, got[1]))
        if self.both:
            self.held, self.flight = held, swap(held, "c")
        else:
            self.own = held.reshape(-1, held.shape[-1])

    def cores(self):
        held, got = self.order.enter(self.held, self.flight)
        whole = join([(held, got, "c", 3)])[0]
        self.whole = whole.reshape(-1, whole.shape[-1])


class Scatter:
    def __init__(self, order, grads):
        self.order, self.distance = order, 0
        self.start([grads.reshape(lax.axis_size("z"), 2, 2, -1, grads.shape[-1])])

    @classmethod
    def of_cores(cls, order, grads):
        self = cls.__new__(cls)
        self.order, self.distance = order, 0
        view = grads.reshape(lax.axis_size("z"), 2, 2, 2, -1, grads.shape[-1])
        keep, send = split([([view], "c", 3)])
        self.held, self.flight = keep, swap(order.leave(send), "c")
        return self

    def first(self):
        got = self.order.enter(self.flight)
        self.start([self.held, got])

    def start(self, parts):
        half = parts[0].shape[0] // 2
        one, two = [p[:half] for p in parts], [p[half:] for p in parts]
        keep_one, send_one, keep_two, send_two = split([(one, "x", 2), (two, "y", 1)])
        sent = self.order.leave(send_one, send_two)
        self.held = [keep_one, keep_two]
        self.flight = [swap(sent[0], "x"), swap(sent[1], "y")]

    def second(self):
        got = self.order.enter(*self.flight)
        one, two = ([h, g] for h, g in zip(self.held, got))
        keep_one, send_one, keep_two, send_two = split([(one, "y", 1), (two, "x", 1)])
        sent = self.order.leave(send_one, send_two)
        self.held = [keep_one, keep_two]
        self.flight = [swap(sent[0], "y"), swap(sent[1], "x")]

    def along_z(self):
        if self.distance == 0:
            got = self.order.enter(*self.flight)
            one, two = ([h, g] for h, g in zip(self.held, got))
            self.distance = lax.axis_size("z") // 2
            keep, send = split_halves(one, two, ("z", self.distance))
        else:
            self.distance //= 2
            got = self.order.enter(self.flight)
            parts = [v.reshape((2, -1) + v.shape[1:]) for v in (self.held, got)]
            keep, send = split([(parts, ("z", self.distance), 0)])
        self.held = keep
        self.flight = swap(self.order.leave(send), "z", self.distance)

    def rest_of_z(self):
        while self.distance > 1:
            self.along_z()

    def done(self):
        got = self.order.enter(self.flight)
        self.total = self.order.leave(to_half(to_full(self.held[0]) + to_full(got[0])))

    def column_halves(self):
        total = self.total.reshape(2, -1, self.total.shape[-1])
        core = lax.axis_index("c")
        mine = lax.dynamic_index_in_dim(total, core, 0, False)
        theirs = swap(lax.dynamic_index_in_dim(total, 1 - core, 0, False), "c")
        low = core == 0
        return to_full(jnp.where(low, mine, theirs)), to_full(jnp.where(low, theirs, mine))


def both_rows(keep, send):
    got = swap(send, "c")
    low = lax.axis_index("c") == 0
    return jnp.where(low, jnp.concatenate([keep, got], 0), jnp.concatenate([got, keep], 0))


def column_half(value, other=False):
    size = value.shape[-1] // 2
    core = lax.axis_index("c")
    return lax.dynamic_slice_in_dim(value, (1 - core if other else core) * size, size, value.ndim - 1)


def odd_blocks(value, other=False):
    core = lax.axis_index("c")
    blocks = value.reshape(value.shape[0], -1, 2, 128)
    return lax.dynamic_index_in_dim(blocks, 1 - core if other else core, 2, False).reshape(
        value.shape[0], -1
    )


def nt(left, right):
    return lax.dot_general(
        left, right, (((1,), (1,)), ((), ())), preferred_element_type=jnp.float32
    )


def norm_parts(values):
    center = values - jnp.mean(values, -1, keepdims=True)
    factor = lax.rsqrt(jnp.mean(center * center, -1, keepdims=True) + EPSILON)
    return center * factor, factor


def norm(values, gain, bias):
    return norm_parts(values)[0] * gain + bias


def norm_back(values, gain, grad):
    shape, factor = norm_parts(values)
    inner = grad * gain
    mean = jnp.mean(inner, -1, keepdims=True)
    along = jnp.mean(inner * shape, -1, keepdims=True)
    return (
        factor * (inner - mean - shape * along),
        jnp.sum(grad * shape, 0, keepdims=True),
        jnp.sum(grad, 0, keepdims=True),
    )


def gate(values):
    return 0.5 * values * (1.0 + jnp.tanh(GELU_SCALE * (values + 0.044715 * values * values * values)))


def gate_slope(values):
    square = values * values
    slope = jnp.tanh(GELU_SCALE * values * (1.0 + 0.044715 * square))
    return 0.5 * (1.0 + slope) + 0.5 * values * (1.0 - slope * slope) * (
        GELU_SCALE * (1.0 + 3 * 0.044715 * square)
    )


def columns(side, size, start=0, width=None):
    return pl.ds(pl.multiple_of(side * size + start, 128), size if width is None else width)


def run(kernel, outs, ins, grid=(), in_specs=None, out_specs=None, scratch=(), name=None, **more):
    whole = pl.BlockSpec(memory_space=pltpu.VMEM)
    in_specs = in_specs or {}
    out_specs = out_specs or {}

    def spec(given, value):
        if given is not None:
            return given
        if not grid:
            return whole
        return pl.BlockSpec(value.shape, lambda *_, rank=len(value.shape): (0,) * rank)

    core = lax.axis_index("c").astype(jnp.int32).reshape(1)
    outs = [jax.ShapeDtypeStruct(shape, dtype) for shape, dtype in outs]
    return pl.pallas_call(
        kernel,
        out_shape=outs,
        grid=grid,
        in_specs=[pl.BlockSpec(memory_space=pltpu.SMEM)]
        + [spec(in_specs.get(i), v) for i, v in enumerate(ins)],
        out_specs=[spec(out_specs.get(i), v) for i, v in enumerate(outs)],
        scratch_shapes=scratch,
        compiler_params=pltpu.CompilerParams(vmem_limit_bytes=VMEM_LIMIT),
        cost_estimate=estimate(name),
        name=name,
        **more,
    )(core, *ins)


HALF = jnp.bfloat16
FULL = jnp.float32


def embed_kernel(core, mine, theirs, weight, out_mine, out_theirs):
    out_mine[...] = product(mine[...], weight[...])
    out_theirs[...] = product(theirs[...], weight[...])


def embed_tokens(mine, theirs, weight):
    shape = ((mine.shape[0], weight.shape[1]), FULL)
    return run(embed_kernel, [shape, shape], [mine, theirs, weight], name="embed_tokens")


def norm_kernel(core, mine, got, gains, biases, embedded, normed):
    size = mine.shape[1]
    embedded[:, columns(core[0], size)] = mine[...]
    embedded[:, columns(1 - core[0], size)] = got[...]
    values = embedded[...] + biases[0:1]
    embedded[...] = values
    normed[...] = to_half(norm(values, gains[0:1], biases[1:2]))


def norm_tokens(mine, got, gains, biases):
    shape = (mine.shape[0], gains.shape[1])
    return run(
        norm_kernel, [(shape, FULL), (shape, HALF)], [mine, got, gains, biases], name="norm_tokens"
    )


def token_rows(side, rows):
    return pl.ds(pl.multiple_of(side * rows, rows), rows)


def project_kernel(core, mine, got, weight, both, out):
    rows = mine.shape[0]

    @pl.when(pl.program_id(0) == 0)
    def _():
        both[token_rows(core[0], rows), :] = mine[...]
        both[token_rows(1 - core[0], rows), :] = got[...]

    out[0] = to_half(product(both[...], weight[...]))


def project_tokens(mine, got, weight):
    rows, width = mine.shape
    each = weight.shape[1] // 4
    return run(
        project_kernel,
        [((2 * rows, width), HALF), ((4, 2 * rows, each), HALF)],
        [mine, got, weight],
        grid=(4,),
        in_specs={2: pl.BlockSpec((width, each), lambda j: (0, j))},
        out_specs={1: pl.BlockSpec((1, 2 * rows, each), lambda j: (j, 0, 0))},
        name="project_tokens",
    )


def middle_kernel(
    core, embedded, parts, got, weight, gains, biases, attended, middle, second
):
    rows = got.shape[1]
    each = parts.shape[2]
    width = embedded.shape[1]
    for q in range(4):
        attended[:, columns(core[0], 4 * each, q * each, each)] = parts[
            q, token_rows(core[0], rows), :
        ]
        attended[:, columns(1 - core[0], 4 * each, q * each, each)] = got[q]
    values = embedded[...] + product(attended[...], weight[:, :width]) + biases[2:3]
    middle[...] = values
    second[...] = to_half(norm(values, gains[1:2], biases[3:4]))


def middle_tokens(embedded, parts, got, weight, gains, biases):
    shape = embedded.shape
    return run(
        middle_kernel,
        [(shape, HALF), (shape, FULL), (shape, HALF)],
        [embedded, parts, got, weight, gains, biases],
        name="middle_tokens",
    )


def expand_kernel(core, mine, got, weight, bias, both, expanded, activated):
    rows = mine.shape[0]

    @pl.when(pl.program_id(0) == 0)
    def _():
        both[:rows, :] = mine[...]
        both[rows:, :] = got[...]

    values = product(both[...], weight[...]) + bias[...]
    expanded[...] = values
    activated[...] = to_half(gate(values))


def expand_tokens(mine, got, weight, bias):
    rows, width = mine.shape
    hidden = weight.shape[1]
    tile = pl.BlockSpec((2 * rows, 512), lambda j: (0, j))
    return run(
        expand_kernel,
        [((2 * rows, width), HALF), ((2 * rows, hidden), FULL), ((2 * rows, hidden), HALF)],
        [mine, got, weight, bias],
        grid=(hidden // 512,),
        in_specs={
            2: pl.BlockSpec((width, 512), lambda j: (0, j)),
            3: pl.BlockSpec((1, 512), lambda j: (0, j)),
        },
        out_specs={1: tile, 2: tile},
        name="expand_tokens",
    )


def reduce_kernel(core, activated, weight, mine, theirs, total):
    step = pl.program_id(0)
    rows = mine.shape[0]
    values = product(activated[...], weight[...])

    @pl.when(step == 0)
    def _():
        total[...] = values

    @pl.when(step > 0)
    def _():
        total[...] += values

    @pl.when(step == pl.num_programs(0) - 1)
    def _():
        mine[...] = total[:rows, :]
        theirs[...] = total[rows:, :]


def reduce_tokens(activated, weight):
    rows, hidden = activated.shape
    width = weight.shape[1]
    shape = ((rows // 2, width), FULL)
    return run(
        reduce_kernel,
        [shape, shape],
        [activated, weight],
        grid=(hidden // 512,),
        in_specs={
            0: pl.BlockSpec((rows, 512), lambda j: (0, j)),
            1: pl.BlockSpec((512, width), lambda j: (j, 0)),
        },
        scratch=[pltpu.VMEM((rows, width), FULL)],
        name="reduce_tokens",
    )


def slot_of(p, size):
    return (2 * p * size, 2 * size) if p < 4 else (8 * size + (p - 4) * size, size)


def encode_kernel(
    core, middle, mine, got, weight, biases, pred_weight, pred_gains, pred_biases,
    encoded, pred_in, normed, parts, projected,
):
    full = middle.shape[1]
    encoded[...] = to_half(middle[...] + (mine[...] + got[...]) + biases[4:5])
    values = product(encoded[...], weight[:, full:]) + pred_biases[0:1]
    pred_in[...] = values
    normed[...] = to_half(norm(values, pred_gains[0:1], pred_biases[1:2]))
    width = values.shape[1]
    projected[...] = nt(normed[...], pred_weight[...])
    both = parts.shape[2] // 3
    for p in range(PLANE):
        start, size = slot_of(p, both // 2)
        for t in range(3):
            parts[p, :, t * both : t * both + size] = to_half(
                projected[:, t * width + start : t * width + start + size]
            )
            if size < both:
                parts[p, :, t * both + size : (t + 1) * both] = jnp.zeros(
                    (parts.shape[1], both - size), HALF
                )


def encode_tokens(middle, mine, got, weight, biases, pred_weights, pred_gains, pred_biases):
    rows = middle.shape[0]
    width = pred_gains.shape[1]
    each = 3 * 2 * width // PRED_HEADS
    return run(
        encode_kernel,
        [
            (middle.shape, HALF),
            ((rows, width), FULL),
            ((rows, width), HALF),
            ((PLANE, rows, each), HALF),
        ],
        [middle, mine, got, weight, biases, pred_weights, pred_gains, pred_biases],
        grid=(1,),
        in_specs={5: pl.BlockSpec((3 * width, width), lambda j: (0, 0))},
        scratch=[pltpu.VMEM((rows, 3 * width), FULL)],
        name="encode_tokens",
    )


def pred_feed_kernel(
    core, pred_in, parts, weights, gains, biases, hidden_bias, cotangent,
    prediction, grad_middle, grad_weights, grad_parts, sums, hidden_sums, attended, expanded, work,
):
    width = pred_in.shape[1]
    both = parts.shape[2]
    for p in range(PLANE):
        start, size = slot_of(p, both // 2)
        attended[:, start : start + size] = parts[p, :, :size]
    out_rows = slice(3 * width, weights.shape[0])
    slot = [slice(i * width, (i + 1) * width) for i in range(3)]
    middle = pred_in[...] + nt(attended[...], weights[out_rows, slot[0]]) + biases[2:3]
    second = to_half(norm(middle, gains[1:2], biases[3:4]))
    expanded[...] = nt(second, weights[:, slot[1]]) + hidden_bias[...]
    activated = to_half(gate(expanded[...]))
    result = middle + product(activated, weights[:, slot[2]]) + biases[4:5]
    prediction[...] = to_half(result)
    half_grad = cotangent[...]
    grad = to_full(half_grad)
    sums[2:3, :] = jnp.sum(grad, 0, keepdims=True)
    grad_weights[:, slot[2]] = to_half(left_product(activated, half_grad))
    grad_expanded = nt(half_grad, weights[:, slot[2]]) * gate_slope(expanded[...])
    hidden_sums[...] = jnp.sum(grad_expanded, 0, keepdims=True)
    expanded_half = to_half(grad_expanded)
    grad_weights[:, slot[1]] = to_half(left_product(expanded_half, second))
    grad_second = product(expanded_half, weights[:, slot[1]])
    from_norm, gain, bias = norm_back(middle, gains[1:2], grad_second)
    total = grad + from_norm
    grad_middle[...] = total
    sums[0:1, :] = jnp.sum(total, 0, keepdims=True)
    sums[1:2, :] = bias
    sums[3:4, :] = gain
    sums[4:8, :] = jnp.zeros((4, width), FULL)
    middle_half = to_half(total)
    grad_weights[out_rows, slot[0]] = to_half(left_product(middle_half, attended[...]))
    work[...] = product(middle_half, weights[out_rows, slot[0]])
    for p in range(PLANE):
        start, size = slot_of(p, both // 2)
        grad_parts[p, :, :size] = to_half(work[:, start : start + size])
        if size < both:
            grad_parts[p, :, size:] = jnp.zeros((parts.shape[1], both - size), HALF)


def pred_feed(pred_in, parts, weights, gains, biases, cotangent):
    rows, width = pred_in.shape
    hidden = weights.shape[0]
    return run(
        pred_feed_kernel,
        [
            ((rows, width), HALF),
            ((rows, width), FULL),
            (weights.shape, HALF),
            (parts.shape, HALF),
            ((8, width), FULL),
            ((1, hidden), FULL),
        ],
        [pred_in, parts, weights, gains, biases, biases[5:].reshape(1, hidden), cotangent],
        scratch=[
            pltpu.VMEM((rows, width), HALF),
            pltpu.VMEM((rows, hidden), FULL),
            pltpu.VMEM((rows, width), FULL),
        ],
        name="pred_feed",
    )


def pred_back_kernel(
    core, parts, normed, pred_in, grad_middle, weight, gains, embed, _,
    grad_weight, half_in, grad_encoded, encoded_half, sums, projected,
):
    width = pred_in.shape[1]
    both = parts.shape[2] // 3
    for p in range(PLANE):
        start, size = slot_of(p, both // 2)
        for t in range(3):
            projected[:, t * width + start : t * width + start + size] = parts[
                p, :, t * both : t * both + size
            ]
    grad_weight[...] = to_half(left_product(projected[...], normed[...]))
    grad_normed = product(projected[...], weight[...])
    into_norm, gain, bias = norm_back(pred_in[...], gains[0:1], grad_normed)
    total = grad_middle[...] + into_norm
    sums[0:1, :] = jnp.sum(total, 0, keepdims=True)
    sums[1:2, :] = bias
    sums[2:3, :] = gain
    sums[3:8, :] = jnp.zeros((5, width), FULL)
    half_in[...] = to_half(total)
    values = nt(half_in[...], embed[:, embed.shape[1] - width :])
    grad_encoded[...] = values
    encoded_half[...] = to_half(values)


def pred_back(parts, normed, pred_in, grad_middle, weights, gains, embed, grad_weights):
    rows, width = pred_in.shape
    full = embed.shape[0]
    block = pl.BlockSpec((3 * width, width), lambda j: (0, 0))
    return run(
        pred_back_kernel,
        [
            (grad_weights.shape, HALF),
            ((rows, width), HALF),
            ((rows, full), FULL),
            ((rows, full), HALF),
            ((8, width), FULL),
        ],
        [parts, normed, pred_in, grad_middle, weights, gains, embed, grad_weights],
        grid=(1,),
        in_specs={4: block, 7: pl.BlockSpec(memory_space=pl.ANY)},
        out_specs={0: block},
        scratch=[pltpu.VMEM((rows, 3 * width), HALF)],
        name="pred_back",
        input_output_aliases={8: 0},
    )


def reduce_back_kernel(core, mine, got, weight, expanded, both, out, sums):
    rows = mine.shape[0]

    @pl.when(pl.program_id(0) == 0)
    def _():
        both[:rows, :] = mine[...]
        both[rows:, :] = got[...]

    values = nt(both[...], weight[...]) * gate_slope(expanded[...])
    out[...] = to_half(values)
    sums[...] = jnp.sum(values, 0, keepdims=True)


def reduce_back(mine, got, weight, expanded):
    rows, hidden = expanded.shape
    width = mine.shape[1]
    tile = pl.BlockSpec((rows, 512), lambda j: (0, j))
    return run(
        reduce_back_kernel,
        [((rows, width), HALF), ((rows, hidden), HALF), ((1, hidden), FULL)],
        [mine, got, weight, expanded],
        grid=(hidden // 512,),
        in_specs={2: pl.BlockSpec((512, width), lambda j: (j, 0)), 3: tile},
        out_specs={1: tile, 2: pl.BlockSpec((1, 512), lambda j: (0, j))},
        name="reduce_back",
    )


def expand_back_kernel(core, grad, weight, mine, theirs, total):
    step = pl.program_id(0)
    rows = mine.shape[0]
    values = nt(grad[...], weight[...])

    @pl.when(step == 0)
    def _():
        total[...] = values

    @pl.when(step > 0)
    def _():
        total[...] += values

    @pl.when(step == pl.num_programs(0) - 1)
    def _():
        mine[...] = total[:rows, :]
        theirs[...] = total[rows:, :]


def expand_back(grad, weight):
    rows, hidden = grad.shape
    width = weight.shape[0]
    shape = ((rows // 2, width), FULL)
    return run(
        expand_back_kernel,
        [shape, shape],
        [grad, weight],
        grid=(hidden // 512,),
        in_specs={
            0: pl.BlockSpec((rows, 512), lambda j: (0, j)),
            1: pl.BlockSpec((width, 512), lambda j: (0, j)),
        },
        scratch=[pltpu.VMEM((rows, width), FULL)],
        name="expand_back",
    )


def middle_back_kernel(
    core, middle, grad, mine, got, gains, weight, grad_middle, half_middle, sums, keep, send, work
):
    width = middle.shape[1]
    from_norm, gain, bias = norm_back(middle[...], gains[1:2], mine[...] + got[...])
    values = grad[...] + from_norm
    grad_middle[...] = values
    sums[0:1, :] = jnp.sum(values, 0, keepdims=True)
    sums[1:2, :] = bias
    sums[2:3, :] = jnp.sum(grad[...], 0, keepdims=True)
    sums[3:4, :] = gain
    sums[4:8, :] = jnp.zeros((4, width), FULL)
    half_middle[...] = to_half(values)
    work[...] = to_half(nt(half_middle[...], weight[:, :width]))
    each = keep.shape[2]
    for q in range(4):
        keep[q] = work[:, columns(core[0], 4 * each, q * each, each)]
        send[q] = work[:, columns(1 - core[0], 4 * each, q * each, each)]


def middle_back(middle, grad, mine, got, gains, weight):
    rows, width = middle.shape
    parts = ((4, rows, width // PLANE), HALF)
    return run(
        middle_back_kernel,
        [((rows, width), FULL), ((rows, width), HALF), ((8, width), FULL), parts, parts],
        [middle, grad, mine, got, gains, weight],
        scratch=[pltpu.VMEM((rows, width), HALF)],
        name="middle_back",
    )


def project_back_kernel(core, parts, weight, mine, theirs, total):
    step = pl.program_id(0)
    rows = mine.shape[0]
    values = nt(parts[0], weight[...])

    @pl.when(step == 0)
    def _():
        total[...] = values

    @pl.when(step > 0)
    def _():
        total[...] += values

    @pl.when(step == pl.num_programs(0) - 1)
    def _():
        mine[...] = total[token_rows(core[0], rows), :]
        theirs[...] = total[token_rows(1 - core[0], rows), :]


def project_back(parts, weight):
    _, rows, each = parts.shape
    width = weight.shape[0]
    shape = ((rows // 2, width), FULL)
    return run(
        project_back_kernel,
        [shape, shape],
        [parts, weight],
        grid=(4,),
        in_specs={
            0: pl.BlockSpec((1, rows, each), lambda j: (j, 0, 0)),
            1: pl.BlockSpec((width, each), lambda j: (0, j)),
        },
        scratch=[pltpu.VMEM((rows, width), FULL)],
        name="project_back",
    )


def input_back_kernel(core, embedded, grad, mine, got, gains, keep, send, sums, work):
    into_norm, gain, bias = norm_back(embedded[...], gains[0:1], mine[...] + got[...])
    values = grad[...] + into_norm
    sums[0:1, :] = jnp.sum(values, 0, keepdims=True)
    sums[1:2, :] = bias
    sums[2:3, :] = gain
    sums[3:8, :] = jnp.zeros((5, values.shape[1]), FULL)
    work[...] = to_half(values)
    size = keep.shape[1]
    keep[...] = work[:, columns(core[0], size)]
    send[...] = work[:, columns(1 - core[0], size)]


def input_back(embedded, grad, mine, got, gains):
    rows, width = embedded.shape
    part = ((rows, width // 2), HALF)
    return run(
        input_back_kernel,
        [part, part, ((8, width), FULL)],
        [embedded, grad, mine, got, gains],
        scratch=[pltpu.VMEM((rows, width), HALF)],
        name="input_back",
    )


def pixel_kernel(core, mine, got, weight, out_mine, out_theirs):
    out_mine[...] = nt(mine[...], weight[...])
    out_theirs[...] = to_half(nt(got[...], weight[...]))


def pixel_back(mine, got, weight):
    shape = (mine.shape[0], weight.shape[0])
    return run(
        pixel_kernel, [(shape, FULL), (shape, HALF)], [mine, got, weight], name="pixel_back"
    )


def weight_kernel(count, core, *refs):
    lefts, rights, out = refs[:count], refs[count : 2 * count], refs[-1]
    if len(rights[0].shape) == 3:
        each = rights[0].shape[2]
        for q in range(rights[0].shape[0]):
            out[:, q * each : (q + 1) * each] = to_half(left_product(lefts[0][...], rights[0][q]))
    else:
        values = left_product(lefts[0][...], rights[0][...])
        for left, right in zip(lefts[1:], rights[1:]):
            values += left_product(left[...], right[...])
        out[...] = to_half(values)


def weight_grad(lefts, rights, name="weight_grad"):
    depth = lefts[0].shape[1]
    right = rights[0]
    width = right.shape[0] * right.shape[2] if right.ndim == 3 else right.shape[1]
    block = 512 if depth % 512 == 0 else 256
    return run(
        functools.partial(weight_kernel, len(lefts)),
        [((depth, width), HALF)],
        [*lefts, *rights],
        grid=(depth // block,),
        in_specs={
            i: pl.BlockSpec((v.shape[0], block), lambda j: (0, j)) for i, v in enumerate(lefts)
        },
        out_specs={0: pl.BlockSpec((block, width), lambda j: (j, 0))},
        name=name,
    )[0]


def side_kernel(core, left_one, left_two, right_one, right_two, out):
    width = right_one.shape[1]
    out[:, :width] = to_half(left_product(left_one[...], right_one[...]))
    out[:, width:] = to_half(left_product(left_two[...], right_two[...]))


def weight_grads(lefts, rights):
    depth = lefts[0].shape[1]
    width = rights[0].shape[1] + rights[1].shape[1]
    tile = pl.BlockSpec((lefts[0].shape[0], 512), lambda j: (0, j))
    return run(
        side_kernel,
        [((depth, width), HALF)],
        [*lefts, *rights],
        grid=(depth // 512,),
        in_specs={0: tile, 1: tile},
        out_specs={0: pl.BlockSpec((512, width), lambda j: (j, 0))},
        name="weight_grads",
    )[0]


def total_over_devices(value):
    for axis in ("c", "x", "y", "z"):
        distance = 1
        while distance < lax.axis_size(axis):
            value = value + swap(value, axis, distance)
            distance *= 2
    return value


def head_lanes(values, head, size):
    lane = lax.broadcasted_iota(jnp.int32, values.shape, 1)
    return jnp.where((lane >= head * size) & (lane < (head + 1) * size), values, jnp.zeros_like(values))


def clip_bias(label_column_ref):
    low = label_column_ref[CLIP_LOW : CLIP_LOW + MARGIN, :]
    high = label_column_ref[CLIP_HIGH - MARGIN : CLIP_HIGH, :]
    return jnp.where(low == CLIP_ID, 0.0, MASKED), jnp.where(high == CLIP_ID, 0.0, MASKED)


def add_margins(scores, biases):
    low, high = biases
    return jnp.concatenate(
        [scores[:MARGIN] + low, scores[MARGIN:-MARGIN], scores[-MARGIN:] + high], 0
    )


def softmax_columns(scores):
    top = jnp.max(scores, 0, keepdims=True)
    expo = jnp.exp2(scores - top)
    total = jnp.sum(expo, 0, keepdims=True)
    return to_half(expo), total, top + jnp.log2(total)


def attend_kernel(size, qkv_ref, column_ref, row_ref, out_ref, log_ref, q_s, k_s, vt_s, ot_s):
    both = 2 * size
    factor = LOG2E * size**-0.5
    q_s[...] = qkv_ref[:, :both]
    k_s[...] = qkv_ref[:, both : 2 * both]
    vt_s[...] = to_half(to_full(qkv_ref[:, 2 * both :]).T)
    biases = clip_bias(column_ref)

    def over_clip(queries):
        keys = k_s[CLIP_LOW:CLIP_HIGH, :]
        values_t = vt_s[:, CLIP_LOW:CLIP_HIGH]
        outs, logs = [], []
        for head in range(2):
            scores = add_margins(nt(keys, head_lanes(queries, head, size)) * factor, biases)
            probs, total, log_total = softmax_columns(scores)
            mixed = product(values_t, probs) / total
            outs.append(mixed[head * size : (head + 1) * size])
            logs.append(log_total)
        return jnp.concatenate(outs, 0), jnp.concatenate(logs, 0)

    def over_block(start):
        keys = k_s[start : start + BLOCK, :]
        values_t = vt_s[:, start : start + BLOCK]
        queries = q_s[start : start + BLOCK, :]
        same = column_ref[start : start + BLOCK, :] == row_ref[:, start : start + BLOCK]
        outs, logs = [], []
        for head in range(2):
            scores = jnp.where(same, nt(keys, head_lanes(queries, head, size)) * factor, MASKED)
            probs, total, log_total = softmax_columns(scores)
            mixed = product(values_t, probs) / total
            outs.append(mixed[head * size : (head + 1) * size])
            logs.append(log_total)
        return jnp.concatenate(outs, 0), jnp.concatenate(logs, 0)

    @pl.loop(1, PLANE - 1)
    def _(block):
        start = pl.multiple_of(block * BLOCK, BLOCK)
        out, logs = over_clip(q_s[pl.ds(start, BLOCK), :])
        ot_s[:, pl.ds(start, BLOCK)] = out
        log_ref[:2, pl.ds(start, BLOCK)] = logs

    last = (PLANE - 1) * BLOCK
    edge_out, edge_logs = over_clip(
        jnp.concatenate(
            [q_s[BLOCK - 128 : BLOCK, :], q_s[last : last + 128, :]], 0
        )
    )
    for start, at, inner in ((0, 128, 0), (last, 0, 128)):
        out, logs = over_block(start)
        ot_s[:, start : start + BLOCK] = out
        log_ref[:2, start : start + BLOCK] = logs
        where = start + at
        clip = row_ref[:, where : where + 128] == CLIP_ID
        ot_s[:, where : where + 128] = jnp.where(
            clip, edge_out[:, inner : inner + 128], ot_s[:, where : where + 128]
        )
        log_ref[:2, where : where + 128] = jnp.where(
            clip, edge_logs[:, inner : inner + 128], log_ref[:2, where : where + 128]
        )
    log_ref[2:, :] = jnp.zeros((6, PLANE * BLOCK), jnp.float32)
    out_ref[...] = to_half(ot_s[...].T)


def attend_back_kernel(
    size, qkv_ref, out_ref, grad_ref, log_ref, column_ref, row_ref, dqkv_ref,
    q_s, k_s, v_s, kt_s, d_s, dqt_s, dk_s, dv_s,
):
    both = 2 * size
    factor = LOG2E * size**-0.5
    scale = size**-0.5
    q_s[...] = qkv_ref[:, :both]
    k_s[...] = qkv_ref[:, both : 2 * both]
    v_s[...] = qkv_ref[:, 2 * both :]
    kt_s[...] = to_half(to_full(qkv_ref[:, both : 2 * both]).T)
    weighted = (to_full(grad_ref[...]) * to_full(out_ref[...])).T
    for head in range(2):
        d_s[head : head + 1, :] = jnp.sum(
            weighted[head * size : (head + 1) * size], 0, keepdims=True
        )
    dk_s[...] = jnp.zeros_like(dk_s)
    dv_s[...] = jnp.zeros_like(dv_s)
    biases = clip_bias(column_ref)

    def pulled(keys, values, keys_t, queries, grads, logs, centres, masked):
        outs, probs_all, scores_all, queries_all, grads_all = [], [], [], [], []
        for head in range(2):
            own_queries = head_lanes(queries, head, size)
            own_grads = head_lanes(grads, head, size)
            probs = jnp.exp2(masked(nt(keys, own_queries) * factor) - logs[head : head + 1])
            pull = nt(values, own_grads)
            grad_scores = to_half(probs * (pull - centres[head : head + 1]))
            outs.append(product(keys_t, grad_scores)[head * size : (head + 1) * size] * scale)
            probs_all.append(to_half(probs))
            scores_all.append(grad_scores)
            queries_all.append(own_queries)
            grads_all.append(own_grads)
        grad_keys = sum(product(s, q) for s, q in zip(scores_all, queries_all)) * scale
        grad_values = sum(product(p, g) for p, g in zip(probs_all, grads_all))
        return jnp.concatenate(outs, 0), grad_keys, grad_values

    def over_clip(queries, grads, logs, centres):
        return pulled(
            k_s[CLIP_LOW:CLIP_HIGH, :],
            v_s[CLIP_LOW:CLIP_HIGH, :],
            kt_s[:, CLIP_LOW:CLIP_HIGH],
            queries,
            grads,
            logs,
            centres,
            lambda scores: add_margins(scores, biases),
        )

    @pl.loop(1, PLANE - 1)
    def _(block):
        start = pl.multiple_of(block * BLOCK, BLOCK)
        here = pl.ds(start, BLOCK)
        out, grad_keys, grad_values = over_clip(
            q_s[here, :], grad_ref[here, :], log_ref[:2, here], d_s[:2, here]
        )
        dqt_s[:, here] = out
        dk_s[CLIP_LOW:CLIP_HIGH, :] += grad_keys
        dv_s[CLIP_LOW:CLIP_HIGH, :] += grad_values

    last = (PLANE - 1) * BLOCK
    near, far = slice(BLOCK - 128, BLOCK), slice(last, last + 128)

    def ends(ref, axis):
        if axis == 0:
            return jnp.concatenate([ref[near, :], ref[far, :]], 0)
        return jnp.concatenate([ref[:2, near], ref[:2, far]], 1)

    edge_labels = jnp.concatenate([row_ref[:, near], row_ref[:, far]], 1)
    edge_logs = jnp.where(edge_labels == CLIP_ID, ends(log_ref, 1), -MASKED)
    edge_out, grad_keys, grad_values = over_clip(
        ends(q_s, 0), ends(grad_ref, 0), edge_logs, ends(d_s, 1)
    )
    dk_s[CLIP_LOW:CLIP_HIGH, :] += grad_keys
    dv_s[CLIP_LOW:CLIP_HIGH, :] += grad_values
    for start, at, inner in ((0, 128, 0), (last, 0, 128)):
        here = slice(start, start + BLOCK)
        labels = row_ref[:, here]
        same = column_ref[here, :] == labels
        logs = jnp.where(labels == CLIP_ID, -MASKED, log_ref[:2, here])
        out, grad_keys, grad_values = pulled(
            k_s[here, :],
            v_s[here, :],
            kt_s[:, here],
            q_s[here, :],
            grad_ref[here, :],
            logs,
            d_s[:2, here],
            lambda scores: jnp.where(same, scores, MASKED),
        )
        dqt_s[:, here] = out
        where = slice(start + at, start + at + 128)
        dqt_s[:, where] += edge_out[:, inner : inner + 128]
        dk_s[here, :] += grad_keys
        dv_s[here, :] += grad_values
    dqkv_ref[:, :both] = to_half(dqt_s[...].T)
    dqkv_ref[:, both : 2 * both] = to_half(dk_s[...])
    dqkv_ref[:, 2 * both :] = to_half(dv_s[...])


def attend(qkv, labels):
    tokens, width = qkv.shape
    both = width // 3
    return pl.pallas_call(
        functools.partial(attend_kernel, both // 2),
        out_shape=(
            jax.ShapeDtypeStruct((tokens, both), jnp.bfloat16),
            jax.ShapeDtypeStruct((8, tokens), jnp.float32),
        ),
        scratch_shapes=[
            pltpu.VMEM((tokens, both), jnp.bfloat16),
            pltpu.VMEM((tokens, both), jnp.bfloat16),
            pltpu.VMEM((both, tokens), jnp.bfloat16),
            pltpu.VMEM((both, tokens), jnp.float32),
        ],
        compiler_params=pltpu.CompilerParams(vmem_limit_bytes=VMEM_LIMIT),
        cost_estimate=estimate("attend"),
        name="attend",
    )(qkv, labels[:, None], labels[None, :])


def attend_back(qkv, out, grad, logs, labels):
    tokens, width = qkv.shape
    both = width // 3
    return pl.pallas_call(
        functools.partial(attend_back_kernel, both // 2),
        out_shape=jax.ShapeDtypeStruct((tokens, width), jnp.bfloat16),
        scratch_shapes=[
            pltpu.VMEM((tokens, both), jnp.bfloat16),
            pltpu.VMEM((tokens, both), jnp.bfloat16),
            pltpu.VMEM((tokens, both), jnp.bfloat16),
            pltpu.VMEM((both, tokens), jnp.bfloat16),
            pltpu.VMEM((8, tokens), jnp.float32),
            pltpu.VMEM((both, tokens), jnp.float32),
            pltpu.VMEM((tokens, both), jnp.float32),
            pltpu.VMEM((tokens, both), jnp.float32),
        ],
        compiler_params=pltpu.CompilerParams(vmem_limit_bytes=VMEM_LIMIT),
        cost_estimate=estimate("attend_back"),
        name="attend_back",
    )(qkv, out, grad, logs, labels[:, None], labels[None, :])


def to_heads(parts, axes):
    moved = lax.all_to_all(parts, axes, split_axis=0, concat_axis=0, tiled=True)
    return moved.reshape(-1, parts.shape[2])


def to_tokens(values, axes):
    count = PLANE // (2 if len(axes) == 2 else 1)
    parts = values.reshape(count, -1, values.shape[1])
    return lax.all_to_all(parts, axes, split_axis=0, concat_axis=0, tiled=True)


def encoder_columns(weight):
    rows, columns = weight.shape
    return weight.reshape(rows, 3, PLANE, -1).transpose(0, 2, 1, 3).reshape(rows, columns)


def encoder_columns_back(weight):
    rows, columns = weight.shape
    return weight.reshape(rows, PLANE, 3, -1).transpose(0, 2, 1, 3).reshape(rows, columns)


def per_device(
    pixels,
    clip_index,
    patch_weight,
    encoder_attention,
    encoder_output,
    encoder_expand,
    encoder_reduce,
    predictor_embed,
    predictor_weights,
    encoder_gains,
    encoder_biases,
    predictor_gains,
    predictor_biases,
    cotangent,
):
    labels = lax.dynamic_index_in_dim(clip_index, lax.axis_index("z"), 0, keepdims=False)
    width = encoder_output.shape[1]
    pred_width = predictor_embed.shape[1]
    hidden = encoder_expand.shape[1]

    order = Order()
    shard_rows = predictor_weights.shape[0]
    rows = pixels.shape[0]
    core = lax.axis_index("c")
    low = core == 0
    wide_columns = encoder_columns(to_half(encoder_attention))
    half_patch, half_expand = to_half(patch_weight), to_half(encoder_expand)
    patch = Gather(order, both_rows(column_half(half_patch), column_half(half_patch, True)))
    attention = Gather(order, both_rows(column_half(wide_columns), column_half(wide_columns, True)))
    expand = Gather(order, both_rows(odd_blocks(half_expand), odd_blocks(half_expand, True)))
    reduce = Gather(order, to_half(encoder_reduce))
    output = Gather(
        order, jnp.concatenate([to_half(encoder_output), to_half(predictor_embed)], 1), True
    )
    predictor = Gather(
        order, to_half(predictor_weights).reshape(shard_rows, 3 * pred_width), True
    )
    hidden_bias = encoder_biases[5:].reshape(-1, 2, 128)
    hidden_bias = lax.dynamic_index_in_dim(hidden_bias, core, 1, False).reshape(1, -1)

    patch.along_z()
    order.leave(attention.held, expand.held)
    pixels_got = swap(pixels, "c")
    attention.along_z()
    patch.rest_of_z()
    patch.first()
    attention.rest_of_z()
    output.along_z()
    patch.second()
    attention.first()
    output.rest_of_z()
    patch.done()
    mine, theirs = embed_tokens(pixels, order.enter(pixels_got), patch.own)
    got = swap(order.leave(theirs), "c")
    attention.second()
    embedded, normed = norm_tokens(mine, order.enter(got), encoder_gains, encoder_biases)
    normed = order.leave(normed)
    normed_got = swap(normed, "c")
    expand.along_z()
    output.first()
    expand.rest_of_z()
    attention.done()

    normed, normed_got = order.enter(normed, normed_got)
    normed_both, parts = project_tokens(normed, normed_got, attention.own)
    qkv = to_heads(order.leave(parts), CHIP_AXES)
    output.second()
    reduce.along_z()
    expand.first()
    reduce.rest_of_z()
    qkv = order.enter(qkv)
    mixed_heads, logs = attend(qkv, labels)
    parts = to_tokens(order.leave(mixed_heads), CHIP_AXES)
    output.done()
    expand.second()
    predictor.along_z()
    output.cores()
    reduce.first()
    predictor.rest_of_z()
    parts = order.enter(parts)
    theirs = lax.dynamic_slice_in_dim(parts, (1 - core) * rows, rows, 1)
    got = swap(order.leave(theirs), "c")
    attended, middle, second = middle_tokens(
        embedded, parts, order.enter(got), output.whole, encoder_gains, encoder_biases
    )
    second = order.leave(second)
    second_got = swap(second, "c")
    expand.done()
    second, second_got = order.enter(second, second_got)
    second_both, expanded, activated = expand_tokens(second, second_got, expand.own, hidden_bias)
    order.leave(activated)
    reduce.second()
    predictor.first()
    reduce.done()
    mine, theirs = reduce_tokens(order.enter(activated), reduce.own)
    got = swap(order.leave(theirs), "c")
    predictor.second()
    predictor.done()
    predictor.cores()
    weights = predictor.whole
    encoded, pred_in, pred_normed, parts = encode_tokens(
        middle,
        mine,
        got,
        output.whole,
        encoder_biases,
        weights,
        predictor_gains,
        predictor_biases,
    )
    pred_qkv = to_heads(parts, GROUP_AXES)
    pred_heads, pred_logs = attend(pred_qkv, labels)
    prediction, pred_middle_grad, pred_grads, parts, pred_sums, pred_hidden_sums = pred_feed(
        pred_in,
        to_tokens(pred_heads, GROUP_AXES),
        weights,
        predictor_gains,
        predictor_biases,
        cotangent,
    )

    grad_qkv = attend_back(
        pred_qkv, pred_heads, to_heads(parts, GROUP_AXES), pred_logs, labels
    )
    pred_grads, half_in, grad_encoded, encoded_half, pred_in_sums = pred_back(
        to_tokens(grad_qkv, GROUP_AXES),
        pred_normed,
        pred_in,
        pred_middle_grad,
        weights,
        predictor_gains,
        output.whole,
        pred_grads,
    )

    encoded_half = order.leave(encoded_half)
    half_got = swap(encoded_half, "c")
    sum_p = Scatter.of_cores(order, order.enter(pred_grads))
    encoded_half, half_got = order.enter(encoded_half, half_got)
    grad_both, grad_expanded, hidden_sums = reduce_back(
        encoded_half, half_got, reduce.own, expanded
    )
    order.leave(grad_expanded)
    sum_r = Scatter(order, weight_grad([activated], [order.enter(grad_both)]))
    mine, theirs = expand_back(order.enter(grad_expanded), expand.own)
    got = swap(order.leave(theirs), "c")
    sum_p.first()
    grad_middle, half_middle, middle_sums, keep, send = middle_back(
        middle, grad_encoded, mine, order.enter(got), encoder_gains, output.whole
    )
    got = swap(order.leave(send), "c")
    sum_e = Scatter(order, weight_grad([second_both], [order.enter(grad_expanded)]))
    keep, got = order.enter(keep, got)
    parts = jnp.where(low, jnp.concatenate([keep, got], 1), jnp.concatenate([got, keep], 1))
    grad_heads = to_heads(order.leave(parts), CHIP_AXES)
    sum_r.second()
    late_middle, late_in = order.enter(half_middle, half_in)
    sum_o = Scatter.of_cores(order, weight_grads([attended, encoded], [late_middle, late_in]))
    sum_p.second()
    grad_heads = order.enter(grad_heads)
    grad_qkv = attend_back(qkv, mixed_heads, grad_heads, logs, labels)
    parts = to_tokens(order.leave(grad_qkv), CHIP_AXES)
    sum_r.along_z()
    sum_o.first()
    sum_e.second()
    sum_r.rest_of_z()
    sum_p.along_z()
    parts = order.enter(parts)
    sum_a = Scatter(order, weight_grad([normed_both], [parts]))
    mine, theirs = project_back(order.enter(parts), attention.own)
    got = swap(order.leave(theirs), "c")
    sum_o.second()
    sum_r.done()
    sum_p.rest_of_z()
    keep, send, out_sums = input_back(
        embedded, grad_middle, mine, order.enter(got), encoder_gains
    )
    got = swap(order.leave(send), "c")
    sum_e.along_z()
    got = order.enter(got)
    sum_k = Scatter(order, weight_grad([pixels, pixels_got], [keep, got]))
    pixel_mine, pixel_theirs = pixel_back(keep, order.enter(got), patch.own)
    pixel_theirs = swap(order.leave(pixel_theirs), "c")
    sum_a.second()
    sum_e.rest_of_z()
    sum_k.second()
    sum_a.along_z()
    sum_e.done()
    sum_o.along_z()
    sum_p.done()
    sum_a.rest_of_z()
    sum_o.rest_of_z()
    sum_k.along_z()
    sum_a.done()
    sum_o.done()
    sum_k.rest_of_z()
    sum_k.done()
    pixel_grad = to_half(pixel_mine + to_full(pixel_theirs))

    patch_grad = jnp.concatenate(sum_k.column_halves(), 1)
    attention_grad = jnp.concatenate(sum_a.column_halves(), 1)
    expand_grad = jnp.stack(
        [v.reshape(v.shape[0], -1, 128) for v in sum_e.column_halves()], 2
    ).reshape(-1, hidden)
    reduce_grad = to_full(sum_r.total)
    output_grad, embed_grad = (to_full(v) for v in jnp.split(sum_o.total, [width], 1))
    predictor_grad = to_full(sum_p.total)
    hidden_sums = jnp.where(
        jnp.arange(2)[None, :, None] == core, hidden_sums.reshape(-1, 1, 128), 0.0
    ).reshape(1, -1)

    vectors = [
        out_sums[2],
        middle_sums[3],
        out_sums[0],
        out_sums[1],
        middle_sums[0],
        middle_sums[1],
        middle_sums[2],
        hidden_sums[0],
        pred_in_sums[2],
        pred_sums[3],
        pred_in_sums[0],
        pred_in_sums[1],
        pred_sums[0],
        pred_sums[1],
        pred_sums[2],
        pred_hidden_sums[0],
    ]
    total = total_over_devices(jnp.concatenate(vectors).reshape(-1, 128)).reshape(-1)
    split = 11 * width
    encoder_vectors = total[:split].reshape(11, width)
    predictor_vectors = total[split:].reshape(11, pred_width)
    return (
        prediction,
        pixel_grad,
        patch_grad,
        encoder_columns_back(attention_grad),
        output_grad,
        expand_grad,
        reduce_grad,
        embed_grad,
        predictor_grad.reshape(shard_rows, 3, pred_width),
        encoder_vectors[:2],
        encoder_vectors[2:],
        predictor_vectors[:2],
        predictor_vectors[2:],
    )


def solution(mesh):
    wide, narrow = mesh.devices.shape
    fine = Mesh(mesh.devices.reshape(wide // 2, 2, narrow // 2, 2), AXES)
    rows = P(AXES, None)
    rows_three = P(AXES, None, None)
    in_specs = (rows, P(), rows, rows, rows, rows, rows, rows, rows_three, P(), P(), P(), P(), rows)
    out_specs = (rows,) * 8 + (rows_three, P(), P(), P(), P())
    return jax.shard_map(
        per_device, mesh=fine, in_specs=in_specs, out_specs=out_specs, check_vma=False
    )
```

```python
import functools
import itertools

import jax
import jax.numpy as jnp
from jax import lax
from jax.experimental import pallas as pl
from jax.experimental.pallas import tpu as pltpu
from jax.sharding import Mesh
from jax.sharding import PartitionSpec as P

HEADS = 16
PRED_HEADS = 12

EPSILON = 1e-06
GELU_SCALE = 0.7978845608028654
LOG2E = 1.4426950408889634
MASKED = -1e30

PLANE = 8
BLOCK = 256
CLIP_LOW = 224
CLIP_HIGH = 1824
MARGIN = 32
CLIP_ID = 2

AXES = ("z", "y", "x", "c")
GROUP_AXES = ("y", "x", "c")
CHIP_AXES = ("y", "x")
VMEM_LIMIT = 48 * 1024 * 1024

COST = {
    "embed_tokens": 2.1,
    "norm_tokens": 1,
    "project_tokens": 4.5,
    "attend": 18,
    "middle_tokens": 3.9,
    "expand_tokens": 7.2,
    "reduce_tokens": 5.5,
    "encode_tokens": 3.5,
    "pred_feed": 6.7,
    "pred_back": 4.3,
    "attend_back": 19,
    "reduce_back": 7.1,
    "weight_grad": 4,
    "weight_grads": 2,
    "expand_back": 6.5,
    "middle_back": 3.9,
    "project_back": 6.5,
    "input_back": 2.2,
    "pixel_back": 1.9,
    "join": 1.5,
    "join_all": 2.5,
    "in_turn": 2,
    "split": 2,
    "split_halves": 1,
}


def estimate(name):
    return pl.CostEstimate(flops=int(COST[name] / 3 * 1.15e9), bytes_accessed=0, transcendentals=0)


def swap(value, axis, distance=1):
    size = lax.axis_size(axis)
    return lax.ppermute(value, axis, [(i, i ^ distance) for i in range(size)])


class Order:
    def __init__(self):
        self.clock = ()

    def enter(self, *values):
        if self.clock:
            values = lax.optimization_barrier(values + self.clock)[: len(values)]
        return values if len(values) > 1 else values[0]

    def leave(self, *values):
        self.clock = values
        return values if len(values) > 1 else values[0]


def to_half(values):
    return values.astype(jnp.bfloat16)


def to_full(values):
    return values.astype(jnp.float32)


def product(left, right):
    return jnp.dot(left, right, preferred_element_type=jnp.float32)


def left_product(left, right):
    return lax.dot_general(
        left, right, (((0,), (0,)), ((), ())), preferred_element_type=jnp.float32
    )


def position(axis):
    if isinstance(axis, tuple):
        return lax.axis_index(axis[0]) // axis[1] % 2
    return lax.axis_index(axis)


def leading(value):
    return list(itertools.product(*(range(n) for n in value.shape[:-2])))


def aligned(value):
    return value.shape[-2] % 16 == 0


def small_kernel(kernel, outs, ins, axes, name):
    bits = jnp.stack([position(axis) for axis in axes]).astype(jnp.int32)
    vmem = pl.BlockSpec(memory_space=pltpu.VMEM)
    return pl.pallas_call(
        kernel,
        out_shape=[jax.ShapeDtypeStruct(shape, jnp.bfloat16) for shape in outs],
        in_specs=[pl.BlockSpec(memory_space=pltpu.SMEM)] + [vmem] * len(ins),
        out_specs=[vmem] * len(outs),
        compiler_params=pltpu.CompilerParams(vmem_limit_bytes=VMEM_LIMIT),
        cost_estimate=estimate(name),
        name=name,
    )(bits, *ins)


def join(items):
    shapes = [own.shape[:at] + (2,) + own.shape[at:] for own, _, _, at in items]
    if not aligned(items[0][0]):
        low = [position(axis) == 0 for _, _, axis, _ in items]
        return [
            jnp.stack([jnp.where(l, own, got), jnp.where(l, got, own)], at)
            for l, (own, got, _, at) in zip(low, items)
        ]

    def kernel(bits, *refs):
        outs = refs[2 * len(items) :]
        for i, (own, got, _, at) in enumerate(items):
            for index in leading(own):
                for bit, ref in ((bits[i], refs[2 * i]), (1 - bits[i], refs[2 * i + 1])):
                    outs[i][index[:at] + (bit,) + index[at:]] = ref[index]

    ins = [v for own, got, _, _ in items for v in (own, got)]
    return small_kernel(kernel, shapes, ins, [axis for _, _, axis, _ in items], "join")


def join_all(one, got_one, two, got_two):
    if not aligned(one):
        first, second = join([(one, got_one, "x", 2), (two, got_two, "y", 1)])
        return jnp.concatenate([first, second], 0)
    half = one.shape[0]

    def kernel(bits, one, got_one, two, got_two, out):
        for h, k in itertools.product(range(half), range(2)):
            out[h, k, bits[0]] = one[h, k]
            out[h, k, 1 - bits[0]] = got_one[h, k]
            out[half + h, bits[1], k] = two[h, k]
            out[half + h, 1 - bits[1], k] = got_two[h, k]

    shape = (2 * half, 2) + one.shape[1:]
    return small_kernel(kernel, [shape], [one, got_one, two, got_two], ["x", "y"], "join_all")[0]


def in_turn(own, got, axis):
    if not aligned(own):
        low = position(axis) == 0
        return [jnp.where(low, own, got), jnp.where(low, got, own)]

    def kernel(bits, own, got, first, second):
        for index in leading(own):
            low = bits[0] == 0
            first[index] = jnp.where(low, own[index], got[index])
            second[index] = jnp.where(low, got[index], own[index])

    return small_kernel(kernel, [own.shape] * 2, [own, got], [axis], "in_turn")


def split(items):
    if not aligned(items[0][0][0]):
        outs = []
        for parts, axis, at in items:
            total = to_half(sum(to_full(p) for p in parts))
            for index in (position(axis), 1 - position(axis)):
                outs.append(lax.dynamic_index_in_dim(total, index, at, keepdims=False))
        return outs
    shapes = [p[0].shape[:at] + p[0].shape[at + 1 :] for p, _, at in items]

    def kernel(bits, *refs):
        outs = refs[sum(len(p) for p, _, _ in items) :]
        start = 0
        for i, (parts, _, at) in enumerate(items):
            ins = refs[start : start + len(parts)]
            start += len(parts)
            for index in leading(outs[2 * i]):
                for bit, out in ((bits[i], outs[2 * i]), (1 - bits[i], outs[2 * i + 1])):
                    where = index[:at] + (bit,) + index[at:]
                    if len(ins) == 1:
                        out[index] = ins[0][where]
                    else:
                        out[index] = to_half(sum(to_full(ref[where]) for ref in ins))

    ins = [v for parts, _, _ in items for v in parts]
    outs = [shape for shape in shapes for _ in range(2)]
    return small_kernel(kernel, outs, ins, [axis for _, axis, _ in items], "split")


def split_halves(one, two, axis):
    if not aligned(one[0]):
        first, second = (to_half(sum(to_full(p) for p in parts)) for parts in (one, two))
        low = position(axis) == 0
        return jnp.where(low, first, second), jnp.where(low, second, first)

    def kernel(bits, *refs):
        keep, send = refs[-2:]
        for index in leading(keep):
            first = to_half(sum(to_full(ref[index]) for ref in refs[: len(one)]))
            second = to_half(sum(to_full(ref[index]) for ref in refs[len(one) : -2]))
            low = bits[0] == 0
            keep[index] = jnp.where(low, first, second)
            send[index] = jnp.where(low, second, first)

    return small_kernel(kernel, [one[0].shape] * 2, [*one, *two], [axis], "split_halves")


class Gather:
    def __init__(self, order, shard, both=False):
        self.order, self.both, self.distance = order, both, 1
        self.held = shard

    def along_z(self):
        if self.distance == 1:
            held = self.order.enter(self.held)[None]
        else:
            held, got = self.order.enter(self.held, self.flight)
            held = join([(held, got, ("z", self.distance // 2), 0)])[0]
            held = held.reshape((-1,) + held.shape[2:])
        self.held = self.order.leave(held)
        self.flight = swap(self.held, "z", self.distance)
        self.distance *= 2

    def rest_of_z(self):
        while self.distance < lax.axis_size("z"):
            self.along_z()

    def first(self):
        held, got = self.order.enter(self.held, self.flight)
        self.held = self.order.leave(*in_turn(held, got, ("z", self.distance // 2)))
        self.flight = [swap(self.held[0], "y"), swap(self.held[1], "x")]

    def second(self):
        one, two, *got = self.order.enter(*self.held, *self.flight)
        self.held = self.order.leave(*join([(one, got[0], "y", 1), (two, got[1], "x", 1)]))
        self.flight = [swap(self.held[0], "x"), swap(self.held[1], "y")]

    def done(self):
        one, two, *got = self.order.enter(*self.held, *self.flight)
        held = self.order.leave(join_all(one, got[0], two, got[1]))
        if self.both:
            self.held, self.flight = held, swap(held, "c")
        else:
            self.own = held.reshape(-1, held.shape[-1])

    def cores(self):
        held, got = self.order.enter(self.held, self.flight)
        whole = join([(held, got, "c", 3)])[0]
        self.whole = whole.reshape(-1, whole.shape[-1])


class Scatter:
    def __init__(self, order, grads):
        self.order, self.distance = order, 0
        self.start([grads.reshape(lax.axis_size("z"), 2, 2, -1, grads.shape[-1])])

    @classmethod
    def of_cores(cls, order, grads):
        self = cls.__new__(cls)
        self.order, self.distance = order, 0
        view = grads.reshape(lax.axis_size("z"), 2, 2, 2, -1, grads.shape[-1])
        keep, send = split([([view], "c", 3)])
        self.held, self.flight = keep, swap(order.leave(send), "c")
        return self

    def first(self):
        got = self.order.enter(self.flight)
        self.start([self.held, got])

    def start(self, parts):
        half = parts[0].shape[0] // 2
        one, two = [p[:half] for p in parts], [p[half:] for p in parts]
        keep_one, send_one, keep_two, send_two = split([(one, "x", 2), (two, "y", 1)])
        sent = self.order.leave(send_one, send_two)
        self.held = [keep_one, keep_two]
        self.flight = [swap(sent[0], "x"), swap(sent[1], "y")]

    def second(self):
        got = self.order.enter(*self.flight)
        one, two = ([h, g] for h, g in zip(self.held, got))
        keep_one, send_one, keep_two, send_two = split([(one, "y", 1), (two, "x", 1)])
        sent = self.order.leave(send_one, send_two)
        self.held = [keep_one, keep_two]
        self.flight = [swap(sent[0], "y"), swap(sent[1], "x")]

    def along_z(self):
        if self.distance == 0:
            got = self.order.enter(*self.flight)
            one, two = ([h, g] for h, g in zip(self.held, got))
            self.distance = lax.axis_size("z") // 2
            keep, send = split_halves(one, two, ("z", self.distance))
        else:
            self.distance //= 2
            got = self.order.enter(self.flight)
            parts = [v.reshape((2, -1) + v.shape[1:]) for v in (self.held, got)]
            keep, send = split([(parts, ("z", self.distance), 0)])
        self.held = keep
        self.flight = swap(self.order.leave(send), "z", self.distance)

    def rest_of_z(self):
        while self.distance > 1:
            self.along_z()

    def done(self):
        got = self.order.enter(self.flight)
        self.total = self.order.leave(to_half(to_full(self.held[0]) + to_full(got[0])))

    def column_halves(self):
        total = self.total.reshape(2, -1, self.total.shape[-1])
        core = lax.axis_index("c")
        mine = lax.dynamic_index_in_dim(total, core, 0, False)
        theirs = swap(lax.dynamic_index_in_dim(total, 1 - core, 0, False), "c")
        low = core == 0
        return to_full(jnp.where(low, mine, theirs)), to_full(jnp.where(low, theirs, mine))


def both_rows(keep, send):
    got = swap(send, "c")
    low = lax.axis_index("c") == 0
    return jnp.where(low, jnp.concatenate([keep, got], 0), jnp.concatenate([got, keep], 0))


def column_half(value, other=False):
    size = value.shape[-1] // 2
    core = lax.axis_index("c")
    return lax.dynamic_slice_in_dim(value, (1 - core if other else core) * size, size, value.ndim - 1)


def odd_blocks(value, other=False):
    core = lax.axis_index("c")
    blocks = value.reshape(value.shape[0], -1, 2, 128)
    return lax.dynamic_index_in_dim(blocks, 1 - core if other else core, 2, False).reshape(
        value.shape[0], -1
    )


def nt(left, right):
    return lax.dot_general(
        left, right, (((1,), (1,)), ((), ())), preferred_element_type=jnp.float32
    )


def norm_parts(values):
    center = values - jnp.mean(values, -1, keepdims=True)
    factor = lax.rsqrt(jnp.mean(center * center, -1, keepdims=True) + EPSILON)
    return center * factor, factor


def norm(values, gain, bias):
    return norm_parts(values)[0] * gain + bias


def norm_back(values, gain, grad):
    shape, factor = norm_parts(values)
    inner = grad * gain
    mean = jnp.mean(inner, -1, keepdims=True)
    along = jnp.mean(inner * shape, -1, keepdims=True)
    return (
        factor * (inner - mean - shape * along),
        jnp.sum(grad * shape, 0, keepdims=True),
        jnp.sum(grad, 0, keepdims=True),
    )


def gate(values):
    return 0.5 * values * (1.0 + jnp.tanh(GELU_SCALE * (values + 0.044715 * values * values * values)))


def gate_slope(values):
    square = values * values
    slope = jnp.tanh(GELU_SCALE * values * (1.0 + 0.044715 * square))
    return 0.5 * (1.0 + slope) + 0.5 * values * (1.0 - slope * slope) * (
        GELU_SCALE * (1.0 + 3 * 0.044715 * square)
    )


def columns(side, size, start=0, width=None):
    return pl.ds(pl.multiple_of(side * size + start, 128), size if width is None else width)


def run(kernel, outs, ins, grid=(), in_specs=None, out_specs=None, scratch=(), name=None, **more):
    whole = pl.BlockSpec(memory_space=pltpu.VMEM)
    in_specs = in_specs or {}
    out_specs = out_specs or {}

    def spec(given, value):
        if given is not None:
            return given
        if not grid:
            return whole
        return pl.BlockSpec(value.shape, lambda *_, rank=len(value.shape): (0,) * rank)

    core = lax.axis_index("c").astype(jnp.int32).reshape(1)
    outs = [jax.ShapeDtypeStruct(shape, dtype) for shape, dtype in outs]
    return pl.pallas_call(
        kernel,
        out_shape=outs,
        grid=grid,
        in_specs=[pl.BlockSpec(memory_space=pltpu.SMEM)]
        + [spec(in_specs.get(i), v) for i, v in enumerate(ins)],
        out_specs=[spec(out_specs.get(i), v) for i, v in enumerate(outs)],
        scratch_shapes=scratch,
        compiler_params=pltpu.CompilerParams(vmem_limit_bytes=VMEM_LIMIT),
        cost_estimate=estimate(name),
        name=name,
        **more,
    )(core, *ins)


HALF = jnp.bfloat16
FULL = jnp.float32


def embed_kernel(core, mine, theirs, weight, out_mine, out_theirs):
    out_mine[...] = product(mine[...], weight[...])
    out_theirs[...] = product(theirs[...], weight[...])


def embed_tokens(mine, theirs, weight):
    shape = ((mine.shape[0], weight.shape[1]), FULL)
    return run(embed_kernel, [shape, shape], [mine, theirs, weight], name="embed_tokens")


def norm_kernel(core, mine, got, gains, biases, embedded, normed):
    size = mine.shape[1]
    embedded[:, columns(core[0], size)] = mine[...]
    embedded[:, columns(1 - core[0], size)] = got[...]
    values = embedded[...] + biases[0:1]
    embedded[...] = values
    normed[...] = to_half(norm(values, gains[0:1], biases[1:2]))


def norm_tokens(mine, got, gains, biases):
    shape = (mine.shape[0], gains.shape[1])
    return run(
        norm_kernel, [(shape, FULL), (shape, HALF)], [mine, got, gains, biases], name="norm_tokens"
    )


def token_rows(side, rows):
    return pl.ds(pl.multiple_of(side * rows, rows), rows)


def project_kernel(core, mine, got, weight, both, out):
    rows = mine.shape[0]

    @pl.when(pl.program_id(0) == 0)
    def _():
        both[token_rows(core[0], rows), :] = mine[...]
        both[token_rows(1 - core[0], rows), :] = got[...]

    out[0] = to_half(product(both[...], weight[...]))


def project_tokens(mine, got, weight):
    rows, width = mine.shape
    each = weight.shape[1] // 4
    return run(
        project_kernel,
        [((2 * rows, width), HALF), ((4, 2 * rows, each), HALF)],
        [mine, got, weight],
        grid=(4,),
        in_specs={2: pl.BlockSpec((width, each), lambda j: (0, j))},
        out_specs={1: pl.BlockSpec((1, 2 * rows, each), lambda j: (j, 0, 0))},
        name="project_tokens",
    )


def middle_kernel(
    core, embedded, parts, got, weight, gains, biases, attended, middle, second
):
    rows = got.shape[1]
    each = parts.shape[2]
    width = embedded.shape[1]
    for q in range(4):
        attended[:, columns(core[0], 4 * each, q * each, each)] = parts[
            q, token_rows(core[0], rows), :
        ]
        attended[:, columns(1 - core[0], 4 * each, q * each, each)] = got[q]
    values = embedded[...] + product(attended[...], weight[:, :width]) + biases[2:3]
    middle[...] = values
    second[...] = to_half(norm(values, gains[1:2], biases[3:4]))


def middle_tokens(embedded, parts, got, weight, gains, biases):
    shape = embedded.shape
    return run(
        middle_kernel,
        [(shape, HALF), (shape, FULL), (shape, HALF)],
        [embedded, parts, got, weight, gains, biases],
        name="middle_tokens",
    )


def expand_kernel(core, mine, got, weight, bias, both, expanded, activated):
    rows = mine.shape[0]

    @pl.when(pl.program_id(0) == 0)
    def _():
        both[:rows, :] = mine[...]
        both[rows:, :] = got[...]

    values = product(both[...], weight[...]) + bias[...]
    expanded[...] = values
    activated[...] = to_half(gate(values))


def expand_tokens(mine, got, weight, bias):
    rows, width = mine.shape
    hidden = weight.shape[1]
    tile = pl.BlockSpec((2 * rows, 512), lambda j: (0, j))
    return run(
        expand_kernel,
        [((2 * rows, width), HALF), ((2 * rows, hidden), FULL), ((2 * rows, hidden), HALF)],
        [mine, got, weight, bias],
        grid=(hidden // 512,),
        in_specs={
            2: pl.BlockSpec((width, 512), lambda j: (0, j)),
            3: pl.BlockSpec((1, 512), lambda j: (0, j)),
        },
        out_specs={1: tile, 2: tile},
        name="expand_tokens",
    )


def reduce_kernel(core, activated, weight, mine, theirs, total):
    step = pl.program_id(0)
    rows = mine.shape[0]
    values = product(activated[...], weight[...])

    @pl.when(step == 0)
    def _():
        total[...] = values

    @pl.when(step > 0)
    def _():
        total[...] += values

    @pl.when(step == pl.num_programs(0) - 1)
    def _():
        mine[...] = total[:rows, :]
        theirs[...] = total[rows:, :]


def reduce_tokens(activated, weight):
    rows, hidden = activated.shape
    width = weight.shape[1]
    shape = ((rows // 2, width), FULL)
    return run(
        reduce_kernel,
        [shape, shape],
        [activated, weight],
        grid=(hidden // 512,),
        in_specs={
            0: pl.BlockSpec((rows, 512), lambda j: (0, j)),
            1: pl.BlockSpec((512, width), lambda j: (j, 0)),
        },
        scratch=[pltpu.VMEM((rows, width), FULL)],
        name="reduce_tokens",
    )


def slot_of(p, size):
    return (2 * p * size, 2 * size) if p < 4 else (8 * size + (p - 4) * size, size)


def encode_kernel(
    core, middle, mine, got, weight, biases, pred_weight, pred_gains, pred_biases,
    encoded, pred_in, normed, parts, projected,
):
    full = middle.shape[1]
    encoded[...] = to_half(middle[...] + (mine[...] + got[...]) + biases[4:5])
    values = product(encoded[...], weight[:, full:]) + pred_biases[0:1]
    pred_in[...] = values
    normed[...] = to_half(norm(values, pred_gains[0:1], pred_biases[1:2]))
    width = values.shape[1]
    projected[...] = nt(normed[...], pred_weight[...])
    both = parts.shape[2] // 3
    for p in range(PLANE):
        start, size = slot_of(p, both // 2)
        for t in range(3):
            parts[p, :, t * both : t * both + size] = to_half(
                projected[:, t * width + start : t * width + start + size]
            )
            if size < both:
                parts[p, :, t * both + size : (t + 1) * both] = jnp.zeros(
                    (parts.shape[1], both - size), HALF
                )


def encode_tokens(middle, mine, got, weight, biases, pred_weights, pred_gains, pred_biases):
    rows = middle.shape[0]
    width = pred_gains.shape[1]
    each = 3 * 2 * width // PRED_HEADS
    return run(
        encode_kernel,
        [
            (middle.shape, HALF),
            ((rows, width), FULL),
            ((rows, width), HALF),
            ((PLANE, rows, each), HALF),
        ],
        [middle, mine, got, weight, biases, pred_weights, pred_gains, pred_biases],
        grid=(1,),
        in_specs={5: pl.BlockSpec((3 * width, width), lambda j: (0, 0))},
        scratch=[pltpu.VMEM((rows, 3 * width), FULL)],
        name="encode_tokens",
    )


def pred_feed_kernel(
    core, pred_in, parts, weights, gains, biases, hidden_bias, cotangent,
    prediction, grad_middle, grad_weights, grad_parts, sums, hidden_sums, attended, expanded, work,
):
    width = pred_in.shape[1]
    both = parts.shape[2]
    for p in range(PLANE):
        start, size = slot_of(p, both // 2)
        attended[:, start : start + size] = parts[p, :, :size]
    out_rows = slice(3 * width, weights.shape[0])
    slot = [slice(i * width, (i + 1) * width) for i in range(3)]
    middle = pred_in[...] + nt(attended[...], weights[out_rows, slot[0]]) + biases[2:3]
    second = to_half(norm(middle, gains[1:2], biases[3:4]))
    expanded[...] = nt(second, weights[:, slot[1]]) + hidden_bias[...]
    activated = to_half(gate(expanded[...]))
    result = middle + product(activated, weights[:, slot[2]]) + biases[4:5]
    prediction[...] = to_half(result)
    half_grad = cotangent[...]
    grad = to_full(half_grad)
    sums[2:3, :] = jnp.sum(grad, 0, keepdims=True)
    grad_weights[:, slot[2]] = to_half(left_product(activated, half_grad))
    grad_expanded = nt(half_grad, weights[:, slot[2]]) * gate_slope(expanded[...])
    hidden_sums[...] = jnp.sum(grad_expanded, 0, keepdims=True)
    expanded_half = to_half(grad_expanded)
    grad_weights[:, slot[1]] = to_half(left_product(expanded_half, second))
    grad_second = product(expanded_half, weights[:, slot[1]])
    from_norm, gain, bias = norm_back(middle, gains[1:2], grad_second)
    total = grad + from_norm
    grad_middle[...] = total
    sums[0:1, :] = jnp.sum(total, 0, keepdims=True)
    sums[1:2, :] = bias
    sums[3:4, :] = gain
    sums[4:8, :] = jnp.zeros((4, width), FULL)
    middle_half = to_half(total)
    grad_weights[out_rows, slot[0]] = to_half(left_product(middle_half, attended[...]))
    work[...] = product(middle_half, weights[out_rows, slot[0]])
    for p in range(PLANE):
        start, size = slot_of(p, both // 2)
        grad_parts[p, :, :size] = to_half(work[:, start : start + size])
        if size < both:
            grad_parts[p, :, size:] = jnp.zeros((parts.shape[1], both - size), HALF)


def pred_feed(pred_in, parts, weights, gains, biases, cotangent):
    rows, width = pred_in.shape
    hidden = weights.shape[0]
    return run(
        pred_feed_kernel,
        [
            ((rows, width), HALF),
            ((rows, width), FULL),
            (weights.shape, HALF),
            (parts.shape, HALF),
            ((8, width), FULL),
            ((1, hidden), FULL),
        ],
        [pred_in, parts, weights, gains, biases, biases[5:].reshape(1, hidden), cotangent],
        scratch=[
            pltpu.VMEM((rows, width), HALF),
            pltpu.VMEM((rows, hidden), FULL),
            pltpu.VMEM((rows, width), FULL),
        ],
        name="pred_feed",
    )


def pred_back_kernel(
    core, parts, normed, pred_in, grad_middle, weight, gains, embed, _,
    grad_weight, half_in, grad_encoded, encoded_half, sums, projected,
):
    width = pred_in.shape[1]
    both = parts.shape[2] // 3
    for p in range(PLANE):
        start, size = slot_of(p, both // 2)
        for t in range(3):
            projected[:, t * width + start : t * width + start + size] = parts[
                p, :, t * both : t * both + size
            ]
    grad_weight[...] = to_half(left_product(projected[...], normed[...]))
    grad_normed = product(projected[...], weight[...])
    into_norm, gain, bias = norm_back(pred_in[...], gains[0:1], grad_normed)
    total = grad_middle[...] + into_norm
    sums[0:1, :] = jnp.sum(total, 0, keepdims=True)
    sums[1:2, :] = bias
    sums[2:3, :] = gain
    sums[3:8, :] = jnp.zeros((5, width), FULL)
    half_in[...] = to_half(total)
    values = nt(half_in[...], embed[:, embed.shape[1] - width :])
    grad_encoded[...] = values
    encoded_half[...] = to_half(values)


def pred_back(parts, normed, pred_in, grad_middle, weights, gains, embed, grad_weights):
    rows, width = pred_in.shape
    full = embed.shape[0]
    block = pl.BlockSpec((3 * width, width), lambda j: (0, 0))
    return run(
        pred_back_kernel,
        [
            (grad_weights.shape, HALF),
            ((rows, width), HALF),
            ((rows, full), FULL),
            ((rows, full), HALF),
            ((8, width), FULL),
        ],
        [parts, normed, pred_in, grad_middle, weights, gains, embed, grad_weights],
        grid=(1,),
        in_specs={4: block, 7: pl.BlockSpec(memory_space=pl.ANY)},
        out_specs={0: block},
        scratch=[pltpu.VMEM((rows, 3 * width), HALF)],
        name="pred_back",
        input_output_aliases={8: 0},
    )


def reduce_back_kernel(core, mine, got, weight, expanded, both, out, sums):
    rows = mine.shape[0]

    @pl.when(pl.program_id(0) == 0)
    def _():
        both[:rows, :] = mine[...]
        both[rows:, :] = got[...]

    values = nt(both[...], weight[...]) * gate_slope(expanded[...])
    out[...] = to_half(values)
    sums[...] = jnp.sum(values, 0, keepdims=True)


def reduce_back(mine, got, weight, expanded):
    rows, hidden = expanded.shape
    width = mine.shape[1]
    tile = pl.BlockSpec((rows, 512), lambda j: (0, j))
    return run(
        reduce_back_kernel,
        [((rows, width), HALF), ((rows, hidden), HALF), ((1, hidden), FULL)],
        [mine, got, weight, expanded],
        grid=(hidden // 512,),
        in_specs={2: pl.BlockSpec((512, width), lambda j: (j, 0)), 3: tile},
        out_specs={1: tile, 2: pl.BlockSpec((1, 512), lambda j: (0, j))},
        name="reduce_back",
    )


def expand_back_kernel(core, grad, weight, mine, theirs, total):
    step = pl.program_id(0)
    rows = mine.shape[0]
    values = nt(grad[...], weight[...])

    @pl.when(step == 0)
    def _():
        total[...] = values

    @pl.when(step > 0)
    def _():
        total[...] += values

    @pl.when(step == pl.num_programs(0) - 1)
    def _():
        mine[...] = total[:rows, :]
        theirs[...] = total[rows:, :]


def expand_back(grad, weight):
    rows, hidden = grad.shape
    width = weight.shape[0]
    shape = ((rows // 2, width), FULL)
    return run(
        expand_back_kernel,
        [shape, shape],
        [grad, weight],
        grid=(hidden // 512,),
        in_specs={
            0: pl.BlockSpec((rows, 512), lambda j: (0, j)),
            1: pl.BlockSpec((width, 512), lambda j: (0, j)),
        },
        scratch=[pltpu.VMEM((rows, width), FULL)],
        name="expand_back",
    )


def middle_back_kernel(
    core, middle, grad, mine, got, gains, weight, grad_middle, half_middle, sums, keep, send, work
):
    width = middle.shape[1]
    from_norm, gain, bias = norm_back(middle[...], gains[1:2], mine[...] + got[...])
    values = grad[...] + from_norm
    grad_middle[...] = values
    sums[0:1, :] = jnp.sum(values, 0, keepdims=True)
    sums[1:2, :] = bias
    sums[2:3, :] = jnp.sum(grad[...], 0, keepdims=True)
    sums[3:4, :] = gain
    sums[4:8, :] = jnp.zeros((4, width), FULL)
    half_middle[...] = to_half(values)
    work[...] = to_half(nt(half_middle[...], weight[:, :width]))
    each = keep.shape[2]
    for q in range(4):
        keep[q] = work[:, columns(core[0], 4 * each, q * each, each)]
        send[q] = work[:, columns(1 - core[0], 4 * each, q * each, each)]


def middle_back(middle, grad, mine, got, gains, weight):
    rows, width = middle.shape
    parts = ((4, rows, width // PLANE), HALF)
    return run(
        middle_back_kernel,
        [((rows, width), FULL), ((rows, width), HALF), ((8, width), FULL), parts, parts],
        [middle, grad, mine, got, gains, weight],
        scratch=[pltpu.VMEM((rows, width), HALF)],
        name="middle_back",
    )


def project_back_kernel(core, parts, weight, mine, theirs, total):
    step = pl.program_id(0)
    rows = mine.shape[0]
    values = nt(parts[0], weight[...])

    @pl.when(step == 0)
    def _():
        total[...] = values

    @pl.when(step > 0)
    def _():
        total[...] += values

    @pl.when(step == pl.num_programs(0) - 1)
    def _():
        mine[...] = total[token_rows(core[0], rows), :]
        theirs[...] = total[token_rows(1 - core[0], rows), :]


def project_back(parts, weight):
    _, rows, each = parts.shape
    width = weight.shape[0]
    shape = ((rows // 2, width), FULL)
    return run(
        project_back_kernel,
        [shape, shape],
        [parts, weight],
        grid=(4,),
        in_specs={
            0: pl.BlockSpec((1, rows, each), lambda j: (j, 0, 0)),
            1: pl.BlockSpec((width, each), lambda j: (0, j)),
        },
        scratch=[pltpu.VMEM((rows, width), FULL)],
        name="project_back",
    )


def input_back_kernel(core, embedded, grad, mine, got, gains, keep, send, sums, work):
    into_norm, gain, bias = norm_back(embedded[...], gains[0:1], mine[...] + got[...])
    values = grad[...] + into_norm
    sums[0:1, :] = jnp.sum(values, 0, keepdims=True)
    sums[1:2, :] = bias
    sums[2:3, :] = gain
    sums[3:8, :] = jnp.zeros((5, values.shape[1]), FULL)
    work[...] = to_half(values)
    size = keep.shape[1]
    keep[...] = work[:, columns(core[0], size)]
    send[...] = work[:, columns(1 - core[0], size)]


def input_back(embedded, grad, mine, got, gains):
    rows, width = embedded.shape
    part = ((rows, width // 2), HALF)
    return run(
        input_back_kernel,
        [part, part, ((8, width), FULL)],
        [embedded, grad, mine, got, gains],
        scratch=[pltpu.VMEM((rows, width), HALF)],
        name="input_back",
    )


def pixel_kernel(core, mine, got, weight, out_mine, out_theirs):
    out_mine[...] = nt(mine[...], weight[...])
    out_theirs[...] = to_half(nt(got[...], weight[...]))


def pixel_back(mine, got, weight):
    shape = (mine.shape[0], weight.shape[0])
    return run(
        pixel_kernel, [(shape, FULL), (shape, HALF)], [mine, got, weight], name="pixel_back"
    )


def weight_kernel(count, core, *refs):
    lefts, rights, out = refs[:count], refs[count : 2 * count], refs[-1]
    if len(rights[0].shape) == 3:
        each = rights[0].shape[2]
        for q in range(rights[0].shape[0]):
            out[:, q * each : (q + 1) * each] = to_half(left_product(lefts[0][...], rights[0][q]))
    else:
        values = left_product(lefts[0][...], rights[0][...])
        for left, right in zip(lefts[1:], rights[1:]):
            values += left_product(left[...], right[...])
        out[...] = to_half(values)


def weight_grad(lefts, rights, name="weight_grad"):
    depth = lefts[0].shape[1]
    right = rights[0]
    width = right.shape[0] * right.shape[2] if right.ndim == 3 else right.shape[1]
    block = 512 if depth % 512 == 0 else 256
    return run(
        functools.partial(weight_kernel, len(lefts)),
        [((depth, width), HALF)],
        [*lefts, *rights],
        grid=(depth // block,),
        in_specs={
            i: pl.BlockSpec((v.shape[0], block), lambda j: (0, j)) for i, v in enumerate(lefts)
        },
        out_specs={0: pl.BlockSpec((block, width), lambda j: (j, 0))},
        name=name,
    )[0]


def side_kernel(core, left_one, left_two, right_one, right_two, out):
    width = right_one.shape[1]
    out[:, :width] = to_half(left_product(left_one[...], right_one[...]))
    out[:, width:] = to_half(left_product(left_two[...], right_two[...]))


def weight_grads(lefts, rights):
    depth = lefts[0].shape[1]
    width = rights[0].shape[1] + rights[1].shape[1]
    tile = pl.BlockSpec((lefts[0].shape[0], 512), lambda j: (0, j))
    return run(
        side_kernel,
        [((depth, width), HALF)],
        [*lefts, *rights],
        grid=(depth // 512,),
        in_specs={0: tile, 1: tile},
        out_specs={0: pl.BlockSpec((512, width), lambda j: (j, 0))},
        name="weight_grads",
    )[0]


def total_over_devices(value):
    for axis in ("c", "x", "y", "z"):
        distance = 1
        while distance < lax.axis_size(axis):
            value = value + swap(value, axis, distance)
            distance *= 2
    return value


def head_lanes(values, head, size):
    lane = lax.broadcasted_iota(jnp.int32, values.shape, 1)
    return jnp.where((lane >= head * size) & (lane < (head + 1) * size), values, jnp.zeros_like(values))


def clip_bias(label_column_ref):
    low = label_column_ref[CLIP_LOW : CLIP_LOW + MARGIN, :]
    high = label_column_ref[CLIP_HIGH - MARGIN : CLIP_HIGH, :]
    return jnp.where(low == CLIP_ID, 0.0, MASKED), jnp.where(high == CLIP_ID, 0.0, MASKED)


def add_margins(scores, biases):
    low, high = biases
    return jnp.concatenate(
        [scores[:MARGIN] + low, scores[MARGIN:-MARGIN], scores[-MARGIN:] + high], 0
    )


def softmax_columns(scores, small):
    top = 0.0 if small else jnp.max(scores, 0, keepdims=True)
    expo = jnp.exp2(scores if small else scores - top)
    total = jnp.sum(expo, 0, keepdims=True)
    return to_half(expo), total, top + jnp.log2(total)


def largest_square(values, size):
    lane = lax.broadcasted_iota(jnp.int32, (values.shape[1], 128), 1)
    row = lax.broadcasted_iota(jnp.int32, (values.shape[1], 128), 0)
    picks = jnp.where(row // size == lane, 1.0, 0.0).astype(jnp.bfloat16)
    full = to_full(values)
    return jnp.max(product(to_half(full * full), picks), 0, keepdims=True)


SMALL = 60.0


def attend_kernel(size, qkv_ref, column_ref, row_ref, out_ref, log_ref, q_s, k_s, vt_s, ot_s):
    both = 2 * size
    factor = LOG2E * size**-0.5
    q_s[...] = qkv_ref[:, :both]
    k_s[...] = qkv_ref[:, both : 2 * both]
    vt_s[...] = to_half(to_full(qkv_ref[:, 2 * both :]).T)
    biases = clip_bias(column_ref)
    squares = largest_square(q_s[...], size) * largest_square(k_s[...], size)
    bound = jnp.max(squares) * factor**2

    def heads(keys, values_t, queries, masked, small):
        outs, logs = [], []
        for head in range(2):
            scores = masked(nt(keys, head_lanes(queries, head, size)) * factor)
            probs, total, log_total = softmax_columns(scores, small)
            mixed = product(values_t, probs)[head * size : (head + 1) * size]
            outs.append(mixed / total)
            logs.append(log_total)
        return jnp.concatenate(outs, 0), jnp.concatenate(logs, 0)

    def over_clip(queries, small):
        return heads(
            k_s[CLIP_LOW:CLIP_HIGH, :],
            vt_s[:, CLIP_LOW:CLIP_HIGH],
            queries,
            lambda scores: add_margins(scores, biases),
            small,
        )

    last = (PLANE - 1) * BLOCK
    ends = ((0, 128, 0), (last, 0, 128))

    def all_rows(small, block):
        @pl.loop(0, (last - BLOCK) // block)
        def _(i):
            here = pl.ds(pl.multiple_of(BLOCK + i * block, BLOCK), block)
            out, logs = over_clip(q_s[here, :], small)
            ot_s[:, here] = out
            log_ref[:2, here] = logs

        edge_out, edge_logs = over_clip(
            jnp.concatenate([q_s[BLOCK - 128 : BLOCK, :], q_s[last : last + 128, :]], 0), small
        )
        for start, at, inner in ends:
            here = slice(start, start + BLOCK)
            same = column_ref[here, :] == row_ref[:, here]
            out, logs = heads(
                k_s[here, :],
                vt_s[:, here],
                q_s[here, :],
                lambda scores: jnp.where(same, scores, MASKED),
                small,
            )
            ot_s[:, here] = out
            log_ref[:2, here] = logs
            where = slice(start + at, start + at + 128)
            clip = row_ref[:, where] == CLIP_ID
            ot_s[:, where] = jnp.where(clip, edge_out[:, inner : inner + 128], ot_s[:, where])
            log_ref[:2, where] = jnp.where(
                clip, edge_logs[:, inner : inner + 128], log_ref[:2, where]
            )

    pl.when(bound < SMALL**2)(lambda: all_rows(True, 3 * BLOCK))
    pl.when(jnp.logical_not(bound < SMALL**2))(lambda: all_rows(False, BLOCK))
    log_ref[2:, :] = jnp.zeros((6, PLANE * BLOCK), jnp.float32)
    out_ref[...] = to_half(ot_s[...].T)


def attend_back_kernel(
    size, qkv_ref, out_ref, grad_ref, log_ref, column_ref, row_ref, dqkv_ref,
    q_s, k_s, v_s, kt_s, d_s, dqt_s, dk_s, dv_s,
):
    both = 2 * size
    factor = LOG2E * size**-0.5
    scale = size**-0.5
    q_s[...] = qkv_ref[:, :both]
    k_s[...] = qkv_ref[:, both : 2 * both]
    v_s[...] = qkv_ref[:, 2 * both :]
    kt_s[...] = to_half(to_full(qkv_ref[:, both : 2 * both]).T)
    weighted = (to_full(grad_ref[...]) * to_full(out_ref[...])).T
    for head in range(2):
        d_s[head : head + 1, :] = jnp.sum(
            weighted[head * size : (head + 1) * size], 0, keepdims=True
        )
    dk_s[...] = jnp.zeros_like(dk_s)
    dv_s[...] = jnp.zeros_like(dv_s)
    biases = clip_bias(column_ref)

    def pulled(keys, values, keys_t, queries, grads, logs, centres, masked):
        outs, probs_all, scores_all, queries_all, grads_all = [], [], [], [], []
        for head in range(2):
            own_queries = head_lanes(queries, head, size)
            own_grads = head_lanes(grads, head, size)
            probs = jnp.exp2(masked(nt(keys, own_queries) * factor) - logs[head : head + 1])
            pull = nt(values, own_grads)
            grad_scores = to_half(probs * (pull - centres[head : head + 1]))
            outs.append(product(keys_t, grad_scores)[head * size : (head + 1) * size] * scale)
            probs_all.append(to_half(probs))
            scores_all.append(grad_scores)
            queries_all.append(own_queries)
            grads_all.append(own_grads)
        grad_keys = sum(product(s, q) for s, q in zip(scores_all, queries_all)) * scale
        grad_values = sum(product(p, g) for p, g in zip(probs_all, grads_all))
        return jnp.concatenate(outs, 0), grad_keys, grad_values

    def over_clip(queries, grads, logs, centres):
        return pulled(
            k_s[CLIP_LOW:CLIP_HIGH, :],
            v_s[CLIP_LOW:CLIP_HIGH, :],
            kt_s[:, CLIP_LOW:CLIP_HIGH],
            queries,
            grads,
            logs,
            centres,
            lambda scores: add_margins(scores, biases),
        )

    @pl.loop(1, PLANE - 1)
    def _(block):
        start = pl.multiple_of(block * BLOCK, BLOCK)
        here = pl.ds(start, BLOCK)
        out, grad_keys, grad_values = over_clip(
            q_s[here, :], grad_ref[here, :], log_ref[:2, here], d_s[:2, here]
        )
        dqt_s[:, here] = out
        dk_s[CLIP_LOW:CLIP_HIGH, :] += grad_keys
        dv_s[CLIP_LOW:CLIP_HIGH, :] += grad_values

    last = (PLANE - 1) * BLOCK
    near, far = slice(BLOCK - 128, BLOCK), slice(last, last + 128)

    def ends(ref, axis):
        if axis == 0:
            return jnp.concatenate([ref[near, :], ref[far, :]], 0)
        return jnp.concatenate([ref[:2, near], ref[:2, far]], 1)

    edge_labels = jnp.concatenate([row_ref[:, near], row_ref[:, far]], 1)
    edge_logs = jnp.where(edge_labels == CLIP_ID, ends(log_ref, 1), -MASKED)
    edge_out, grad_keys, grad_values = over_clip(
        ends(q_s, 0), ends(grad_ref, 0), edge_logs, ends(d_s, 1)
    )
    dk_s[CLIP_LOW:CLIP_HIGH, :] += grad_keys
    dv_s[CLIP_LOW:CLIP_HIGH, :] += grad_values
    for start, at, inner in ((0, 128, 0), (last, 0, 128)):
        here = slice(start, start + BLOCK)
        labels = row_ref[:, here]
        same = column_ref[here, :] == labels
        logs = jnp.where(labels == CLIP_ID, -MASKED, log_ref[:2, here])
        out, grad_keys, grad_values = pulled(
            k_s[here, :],
            v_s[here, :],
            kt_s[:, here],
            q_s[here, :],
            grad_ref[here, :],
            logs,
            d_s[:2, here],
            lambda scores: jnp.where(same, scores, MASKED),
        )
        dqt_s[:, here] = out
        where = slice(start + at, start + at + 128)
        dqt_s[:, where] += edge_out[:, inner : inner + 128]
        dk_s[here, :] += grad_keys
        dv_s[here, :] += grad_values
    dqkv_ref[:, :both] = to_half(dqt_s[...].T)
    dqkv_ref[:, both : 2 * both] = to_half(dk_s[...])
    dqkv_ref[:, 2 * both :] = to_half(dv_s[...])


def attend(qkv, labels):
    tokens, width = qkv.shape
    both = width // 3
    return pl.pallas_call(
        functools.partial(attend_kernel, both // 2),
        out_shape=(
            jax.ShapeDtypeStruct((tokens, both), jnp.bfloat16),
            jax.ShapeDtypeStruct((8, tokens), jnp.float32),
        ),
        scratch_shapes=[
            pltpu.VMEM((tokens, both), jnp.bfloat16),
            pltpu.VMEM((tokens, both), jnp.bfloat16),
            pltpu.VMEM((both, tokens), jnp.bfloat16),
            pltpu.VMEM((both, tokens), jnp.float32),
        ],
        compiler_params=pltpu.CompilerParams(vmem_limit_bytes=VMEM_LIMIT),
        cost_estimate=estimate("attend"),
        name="attend",
    )(qkv, labels[:, None], labels[None, :])


def attend_back(qkv, out, grad, logs, labels):
    tokens, width = qkv.shape
    both = width // 3
    return pl.pallas_call(
        functools.partial(attend_back_kernel, both // 2),
        out_shape=jax.ShapeDtypeStruct((tokens, width), jnp.bfloat16),
        scratch_shapes=[
            pltpu.VMEM((tokens, both), jnp.bfloat16),
            pltpu.VMEM((tokens, both), jnp.bfloat16),
            pltpu.VMEM((tokens, both), jnp.bfloat16),
            pltpu.VMEM((both, tokens), jnp.bfloat16),
            pltpu.VMEM((8, tokens), jnp.float32),
            pltpu.VMEM((both, tokens), jnp.float32),
            pltpu.VMEM((tokens, both), jnp.float32),
            pltpu.VMEM((tokens, both), jnp.float32),
        ],
        compiler_params=pltpu.CompilerParams(vmem_limit_bytes=VMEM_LIMIT),
        cost_estimate=estimate("attend_back"),
        name="attend_back",
    )(qkv, out, grad, logs, labels[:, None], labels[None, :])


def to_heads(parts, axes):
    moved = lax.all_to_all(parts, axes, split_axis=0, concat_axis=0, tiled=True)
    return moved.reshape(-1, parts.shape[2])


def to_tokens(values, axes):
    count = PLANE // (2 if len(axes) == 2 else 1)
    parts = values.reshape(count, -1, values.shape[1])
    return lax.all_to_all(parts, axes, split_axis=0, concat_axis=0, tiled=True)


def encoder_columns(weight):
    rows, columns = weight.shape
    return weight.reshape(rows, 3, PLANE, -1).transpose(0, 2, 1, 3).reshape(rows, columns)


def encoder_columns_back(weight):
    rows, columns = weight.shape
    return weight.reshape(rows, PLANE, 3, -1).transpose(0, 2, 1, 3).reshape(rows, columns)


def per_device(
    pixels,
    clip_index,
    patch_weight,
    encoder_attention,
    encoder_output,
    encoder_expand,
    encoder_reduce,
    predictor_embed,
    predictor_weights,
    encoder_gains,
    encoder_biases,
    predictor_gains,
    predictor_biases,
    cotangent,
):
    labels = lax.dynamic_index_in_dim(clip_index, lax.axis_index("z"), 0, keepdims=False)
    width = encoder_output.shape[1]
    pred_width = predictor_embed.shape[1]
    hidden = encoder_expand.shape[1]

    order = Order()
    shard_rows = predictor_weights.shape[0]
    rows = pixels.shape[0]
    core = lax.axis_index("c")
    low = core == 0
    wide_columns = encoder_columns(to_half(encoder_attention))
    half_patch, half_expand = to_half(patch_weight), to_half(encoder_expand)
    patch = Gather(order, both_rows(column_half(half_patch), column_half(half_patch, True)))
    attention = Gather(order, both_rows(column_half(wide_columns), column_half(wide_columns, True)))
    expand = Gather(order, both_rows(odd_blocks(half_expand), odd_blocks(half_expand, True)))
    reduce = Gather(order, to_half(encoder_reduce))
    output = Gather(
        order, jnp.concatenate([to_half(encoder_output), to_half(predictor_embed)], 1), True
    )
    predictor = Gather(
        order, to_half(predictor_weights).reshape(shard_rows, 3 * pred_width), True
    )
    hidden_bias = encoder_biases[5:].reshape(-1, 2, 128)
    hidden_bias = lax.dynamic_index_in_dim(hidden_bias, core, 1, False).reshape(1, -1)

    patch.along_z()
    order.leave(attention.held, expand.held)
    pixels_got = swap(pixels, "c")
    attention.along_z()
    patch.rest_of_z()
    patch.first()
    attention.rest_of_z()
    output.along_z()
    patch.second()
    attention.first()
    output.rest_of_z()
    patch.done()
    mine, theirs = embed_tokens(pixels, order.enter(pixels_got), patch.own)
    got = swap(order.leave(theirs), "c")
    attention.second()
    embedded, normed = norm_tokens(mine, order.enter(got), encoder_gains, encoder_biases)
    normed = order.leave(normed)
    normed_got = swap(normed, "c")
    expand.along_z()
    output.first()
    expand.rest_of_z()
    attention.done()

    normed, normed_got = order.enter(normed, normed_got)
    normed_both, parts = project_tokens(normed, normed_got, attention.own)
    qkv = to_heads(order.leave(parts), CHIP_AXES)
    output.second()
    reduce.along_z()
    expand.first()
    reduce.rest_of_z()
    qkv = order.enter(qkv)
    mixed_heads, logs = attend(qkv, labels)
    parts = to_tokens(order.leave(mixed_heads), CHIP_AXES)
    output.done()
    expand.second()
    predictor.along_z()
    output.cores()
    reduce.first()
    predictor.rest_of_z()
    parts = order.enter(parts)
    theirs = lax.dynamic_slice_in_dim(parts, (1 - core) * rows, rows, 1)
    got = swap(order.leave(theirs), "c")
    attended, middle, second = middle_tokens(
        embedded, parts, order.enter(got), output.whole, encoder_gains, encoder_biases
    )
    second = order.leave(second)
    second_got = swap(second, "c")
    expand.done()
    second, second_got = order.enter(second, second_got)
    second_both, expanded, activated = expand_tokens(second, second_got, expand.own, hidden_bias)
    order.leave(activated)
    reduce.second()
    predictor.first()
    reduce.done()
    mine, theirs = reduce_tokens(order.enter(activated), reduce.own)
    got = swap(order.leave(theirs), "c")
    predictor.second()
    predictor.done()
    predictor.cores()
    weights = predictor.whole
    encoded, pred_in, pred_normed, parts = encode_tokens(
        middle,
        mine,
        got,
        output.whole,
        encoder_biases,
        weights,
        predictor_gains,
        predictor_biases,
    )
    pred_qkv = to_heads(parts, GROUP_AXES)
    pred_heads, pred_logs = attend(pred_qkv, labels)
    prediction, pred_middle_grad, pred_grads, parts, pred_sums, pred_hidden_sums = pred_feed(
        pred_in,
        to_tokens(pred_heads, GROUP_AXES),
        weights,
        predictor_gains,
        predictor_biases,
        cotangent,
    )

    grad_qkv = attend_back(
        pred_qkv, pred_heads, to_heads(parts, GROUP_AXES), pred_logs, labels
    )
    pred_grads, half_in, grad_encoded, encoded_half, pred_in_sums = pred_back(
        to_tokens(grad_qkv, GROUP_AXES),
        pred_normed,
        pred_in,
        pred_middle_grad,
        weights,
        predictor_gains,
        output.whole,
        pred_grads,
    )

    encoded_half = order.leave(encoded_half)
    half_got = swap(encoded_half, "c")
    sum_p = Scatter.of_cores(order, order.enter(pred_grads))
    encoded_half, half_got = order.enter(encoded_half, half_got)
    grad_both, grad_expanded, hidden_sums = reduce_back(
        encoded_half, half_got, reduce.own, expanded
    )
    order.leave(grad_expanded)
    sum_r = Scatter(order, weight_grad([activated], [order.enter(grad_both)]))
    mine, theirs = expand_back(order.enter(grad_expanded), expand.own)
    got = swap(order.leave(theirs), "c")
    sum_p.first()
    grad_middle, half_middle, middle_sums, keep, send = middle_back(
        middle, grad_encoded, mine, order.enter(got), encoder_gains, output.whole
    )
    got = swap(order.leave(send), "c")
    sum_e = Scatter(order, weight_grad([second_both], [order.enter(grad_expanded)]))
    keep, got = order.enter(keep, got)
    parts = jnp.where(low, jnp.concatenate([keep, got], 1), jnp.concatenate([got, keep], 1))
    grad_heads = to_heads(order.leave(parts), CHIP_AXES)
    sum_r.second()
    late_middle, late_in = order.enter(half_middle, half_in)
    sum_o = Scatter.of_cores(order, weight_grads([attended, encoded], [late_middle, late_in]))
    sum_p.second()
    grad_heads = order.enter(grad_heads)
    grad_qkv = attend_back(qkv, mixed_heads, grad_heads, logs, labels)
    parts = to_tokens(order.leave(grad_qkv), CHIP_AXES)
    sum_r.along_z()
    sum_o.first()
    sum_e.second()
    sum_r.rest_of_z()
    sum_p.along_z()
    parts = order.enter(parts)
    sum_a = Scatter(order, weight_grad([normed_both], [parts]))
    mine, theirs = project_back(order.enter(parts), attention.own)
    got = swap(order.leave(theirs), "c")
    sum_o.second()
    sum_r.done()
    sum_p.rest_of_z()
    keep, send, out_sums = input_back(
        embedded, grad_middle, mine, order.enter(got), encoder_gains
    )
    got = swap(order.leave(send), "c")
    sum_e.along_z()
    got = order.enter(got)
    sum_k = Scatter(order, weight_grad([pixels, pixels_got], [keep, got]))
    pixel_mine, pixel_theirs = pixel_back(keep, order.enter(got), patch.own)
    pixel_theirs = swap(order.leave(pixel_theirs), "c")
    sum_a.second()
    sum_e.rest_of_z()
    sum_k.second()
    sum_a.along_z()
    sum_e.done()
    sum_o.along_z()
    sum_p.done()
    sum_a.rest_of_z()
    sum_o.rest_of_z()
    sum_k.along_z()
    sum_a.done()
    sum_o.done()
    sum_k.rest_of_z()
    sum_k.done()
    pixel_grad = to_half(pixel_mine + to_full(pixel_theirs))

    patch_grad = jnp.concatenate(sum_k.column_halves(), 1)
    attention_grad = jnp.concatenate(sum_a.column_halves(), 1)
    expand_grad = jnp.stack(
        [v.reshape(v.shape[0], -1, 128) for v in sum_e.column_halves()], 2
    ).reshape(-1, hidden)
    reduce_grad = to_full(sum_r.total)
    output_grad, embed_grad = (to_full(v) for v in jnp.split(sum_o.total, [width], 1))
    predictor_grad = to_full(sum_p.total)
    hidden_sums = jnp.where(
        jnp.arange(2)[None, :, None] == core, hidden_sums.reshape(-1, 1, 128), 0.0
    ).reshape(1, -1)

    vectors = [
        out_sums[2],
        middle_sums[3],
        out_sums[0],
        out_sums[1],
        middle_sums[0],
        middle_sums[1],
        middle_sums[2],
        hidden_sums[0],
        pred_in_sums[2],
        pred_sums[3],
        pred_in_sums[0],
        pred_in_sums[1],
        pred_sums[0],
        pred_sums[1],
        pred_sums[2],
        pred_hidden_sums[0],
    ]
    total = total_over_devices(jnp.concatenate(vectors).reshape(-1, 128)).reshape(-1)
    split = 11 * width
    encoder_vectors = total[:split].reshape(11, width)
    predictor_vectors = total[split:].reshape(11, pred_width)
    return (
        prediction,
        pixel_grad,
        patch_grad,
        encoder_columns_back(attention_grad),
        output_grad,
        expand_grad,
        reduce_grad,
        embed_grad,
        predictor_grad.reshape(shard_rows, 3, pred_width),
        encoder_vectors[:2],
        encoder_vectors[2:],
        predictor_vectors[:2],
        predictor_vectors[2:],
    )


def solution(mesh):
    wide, narrow = mesh.devices.shape
    fine = Mesh(mesh.devices.reshape(wide // 2, 2, narrow // 2, 2), AXES)
    rows = P(AXES, None)
    rows_three = P(AXES, None, None)
    in_specs = (rows, P(), rows, rows, rows, rows, rows, rows, rows_three, P(), P(), P(), P(), rows)
    out_specs = (rows,) * 8 + (rows_three, P(), P(), P(), P())
    return jax.shard_map(
        per_device, mesh=fine, in_specs=in_specs, out_specs=out_specs, check_vma=False
    )
```

```python
import functools
import itertools

import jax
import jax.numpy as jnp
from jax import lax
from jax.experimental import pallas as pl
from jax.experimental.pallas import tpu as pltpu
from jax.sharding import Mesh
from jax.sharding import PartitionSpec as P

HEADS = 16
PRED_HEADS = 12

EPSILON = 1e-06
GELU_SCALE = 0.7978845608028654
LOG2E = 1.4426950408889634
MASKED = -1e30

PLANE = 8
BLOCK = 256
CLIP_LOW = 224
CLIP_HIGH = 1824
MARGIN = 32
CLIP_ID = 2

AXES = ("z", "y", "x", "c")
GROUP_AXES = ("y", "x", "c")
CHIP_AXES = ("y", "x")
VMEM_LIMIT = 48 * 1024 * 1024

EST = {2: 1.5, 36: 6.0}

COST = {
    "embed_tokens": 2.1,
    "norm_tokens": 1,
    "project_tokens": 4.5,
    "attend": 18,
    "middle_tokens": 3.9,
    "expand_tokens": 7.2,
    "reduce_tokens": 5.5,
    "encode_tokens": 3.5,
    "pred_feed": 6.7,
    "pred_back": 4.3,
    "attend_back": 19,
    "reduce_back": 7.1,
    "weight_grad": 4,
    "weight_grads": 2,
    "expand_back": 6.5,
    "middle_back": 3.9,
    "project_back": 6.5,
    "input_back": 2.2,
    "pixel_back": 1.9,
    "interleave": 1.5,
    "assemble": 2.5,
    "route_cores": 2,
    "add": 1.5,
}


CALLS = []


def estimate(name):
    CALLS.append(name)
    micros = EST.get(len(CALLS), COST[name] / 3)
    return pl.CostEstimate(flops=int(micros * 1.15e9), bytes_accessed=0, transcendentals=0)


def swap(value, axis, distance=1):
    size = lax.axis_size(axis)
    return lax.ppermute(value, axis, [(i, i ^ distance) for i in range(size)])


class Order:
    def __init__(self):
        self.clock = ()

    def enter(self, *values):
        if self.clock:
            values = lax.optimization_barrier(values + self.clock)[: len(values)]
        return values if len(values) > 1 else values[0]

    def leave(self, *values):
        self.clock = values
        return values if len(values) > 1 else values[0]


def to_half(values):
    return values.astype(jnp.bfloat16)


def to_full(values):
    return values.astype(jnp.float32)


def product(left, right):
    return jnp.dot(left, right, preferred_element_type=jnp.float32)


def left_product(left, right):
    return lax.dot_general(
        left, right, (((0,), (0,)), ((), ())), preferred_element_type=jnp.float32
    )


def aligned(value):
    return value.shape[-2] % 16 == 0


def position():
    return jnp.stack([lax.axis_index(axis) for axis in AXES]).astype(jnp.int32)


def by_distance(view, first):
    at = 0
    for axis in AXES[:first]:
        bit = 1
        size = view.shape[at]
        while bit < size:
            cut = view.reshape(view.shape[:at] + (size // (2 * bit), 2, bit) + view.shape[at + 1 :])
            here = lax.axis_index(axis) // bit % 2
            view = jnp.where(here == 0, cut, jnp.flip(cut, at + 1)).reshape(view.shape)
            bit *= 2
        at += 1
    return view


def small_kernel(kernel, outs, ins, name):
    vmem = pl.BlockSpec(memory_space=pltpu.VMEM)
    return pl.pallas_call(
        kernel,
        out_shape=[jax.ShapeDtypeStruct(shape, jnp.bfloat16) for shape in outs],
        in_specs=[pl.BlockSpec(memory_space=pltpu.SMEM)] + [vmem] * len(ins),
        out_specs=[vmem] * len(outs),
        compiler_params=pltpu.CompilerParams(vmem_limit_bytes=VMEM_LIMIT),
        cost_estimate=estimate(name),
        name=name,
    )(position(), *ins)


def assemble(one, got_one, two, got_two):
    half = one.shape[1]
    if not aligned(one):
        near = jnp.stack([one, got_one], 2)
        far = jnp.stack([two, got_two], 1)
        near = jnp.moveaxis(near, 1, 0)
        far = jnp.moveaxis(far, 2, 0)
        return by_distance(jnp.concatenate([near, jnp.moveaxis(far, 1, 2)], 0), 3)

    def kernel(place, one, got_one, two, got_two, out):
        z, y, x = place[0], place[1], place[2]
        for k, h in itertools.product(range(2), range(half)):
            out[z ^ h, y ^ k, x] = one[k, h]
            out[z ^ h, y ^ k, 1 - x] = got_one[k, h]
            out[z ^ (h + half), y, x ^ k] = two[k, h]
            out[z ^ (h + half), 1 - y, x ^ k] = got_two[k, h]

    shape = (2 * half, 2, 2) + one.shape[2:]
    return small_kernel(kernel, [shape], [one, got_one, two, got_two], "assemble")[0]


def interleave(own, got):
    if not aligned(own):
        low = lax.axis_index("c") == 0
        return jnp.stack([jnp.where(low, own, got), jnp.where(low, got, own)], 3)

    def kernel(place, own, got, out):
        for index in itertools.product(*(range(n) for n in own.shape[:3])):
            out[index + (place[3],)] = own[index]
            out[index + (1 - place[3],)] = got[index]

    return small_kernel(kernel, [own.shape[:3] + (2,) + own.shape[3:]], [own, got], "interleave")[0]


def routes(view):
    half = view.shape[0] // 2
    near, far = jnp.moveaxis(view[:half], 0, 2), jnp.moveaxis(view[half:], 0, 2)
    return near[:, 0], near[:, 1], far[0], far[1]


def route_cores(grads):
    count = lax.axis_size("z")
    view = grads.reshape(count, 2, 2, 2, -1, grads.shape[-1])
    half = count // 2
    if not aligned(view):
        view = by_distance(view, 4)
        return [
            jnp.stack([jnp.stack(pair) for pair in zip(*[iter(routes(view[:, :, :, core]))] * 2)])
            for core in range(2)
        ]

    def kernel(place, view, keep, send):
        z, y, x, c = (place[i] for i in range(4))
        for out, core in ((keep, c), (send, 1 - c)):
            for i, k, h in itertools.product(range(2), range(2), range(half)):
                out[0, i, k, h] = view[z ^ h, y ^ k, x ^ i, core]
                out[1, i, k, h] = view[z ^ (h + half), y ^ i, x ^ k, core]

    shape = (2, 2, 2, half) + view.shape[4:]
    return small_kernel(kernel, [shape, shape], [view], "route_cores")


def add(pairs, pieces=2):
    if not aligned(pairs[0][0]):
        outs = []
        for own, got in pairs:
            total = to_half(to_full(own) + to_full(got))
            outs += jnp.split(total, pieces, 0)
        return outs
    shapes = [(own.shape[0] // pieces,) + own.shape[1:] for own, _ in pairs for _ in range(pieces)]

    def kernel(place, *refs):
        outs = refs[2 * len(pairs) :]
        for i in range(len(pairs)):
            for j in range(pieces):
                out = outs[i * pieces + j]
                size = out.shape[0]
                here = pl.ds(j * size, size)
                out[...] = to_half(to_full(refs[2 * i][here]) + to_full(refs[2 * i + 1][here]))

    return small_kernel(kernel, shapes, [v for pair in pairs for v in pair], "add")


class Gather:
    def __init__(self, order, shard, both=False):
        self.order, self.both, self.distance = order, both, 1
        self.held = shard

    def along_z(self):
        if self.distance == 1:
            held = self.order.enter(self.held)[None]
        else:
            held = jnp.concatenate(self.order.enter(self.held, self.flight), 0)
        self.held = self.order.leave(held)
        self.flight = swap(self.held, "z", self.distance)
        self.distance *= 2

    def rest_of_z(self):
        while self.distance < lax.axis_size("z"):
            self.along_z()

    def first(self):
        self.held = self.order.leave(*self.order.enter(self.held, self.flight))
        self.flight = [swap(self.held[0], "y"), swap(self.held[1], "x")]

    def second(self):
        one, two, *got = self.order.enter(*self.held, *self.flight)
        self.held = self.order.leave(jnp.stack([one, got[0]]), jnp.stack([two, got[1]]))
        self.flight = [swap(self.held[0], "x"), swap(self.held[1], "y")]

    def done(self):
        one, two, *got = self.order.enter(*self.held, *self.flight)
        held = self.order.leave(assemble(one, got[0], two, got[1]))
        if self.both:
            self.held, self.flight = held, swap(held, "c")
        else:
            self.own = held.reshape(-1, held.shape[-1])

    def cores(self):
        whole = interleave(*self.order.enter(self.held, self.flight))
        self.whole = whole.reshape(-1, whole.shape[-1])


class Whole:
    def __init__(self, order, shard):
        self.own = lax.all_gather(shard, ("z", "y", "x"), axis=0, tiled=True)

    def along_z(self):
        pass

    rest_of_z = first = second = done = along_z


class Scatter:
    def __init__(self, order, parts):
        self.order, self.distance = order, 0
        self.start(parts)

    @classmethod
    def of_cores(cls, order, grads):
        self = cls.__new__(cls)
        self.order, self.distance = order, 0
        self.held, send = route_cores(grads)
        self.flight = swap(order.leave(send), "c")
        return self

    def first(self):
        got = self.order.enter(self.flight)
        flat = [v.reshape((4,) + v.shape[2:]) for v in (self.held, got)]
        self.start([v[0] for v in add([flat], 4)])

    def start(self, parts):
        keep_one, send_one, keep_two, send_two = parts
        sent = self.order.leave(send_one, send_two)
        self.held = [keep_one, keep_two]
        self.flight = [swap(sent[0], "x"), swap(sent[1], "y")]

    def second(self):
        got = self.order.enter(*self.flight)
        keep_one, send_one, keep_two, send_two = (v[0] for v in add(list(zip(self.held, got))))
        sent = self.order.leave(send_one, send_two)
        self.held = [keep_one, keep_two]
        self.flight = [swap(sent[0], "y"), swap(sent[1], "x")]

    def along_z(self):
        if self.distance == 0:
            got = self.order.enter(*self.flight)
            self.distance = lax.axis_size("z") // 2
            keep, send = add(list(zip(self.held, got)), 1)
        else:
            self.distance //= 2
            keep, send = add([(self.held, self.order.enter(self.flight))])
        self.held = keep
        self.flight = swap(self.order.leave(send), "z", self.distance)

    def rest_of_z(self):
        while self.distance > 1:
            self.along_z()

    def done(self):
        got = self.order.enter(self.flight)
        self.total = self.order.leave(to_half(to_full(self.held[0]) + to_full(got[0])))

    def column_halves(self):
        total = self.total.reshape(2, -1, self.total.shape[-1])
        core = lax.axis_index("c")
        mine = lax.dynamic_index_in_dim(total, core, 0, False)
        theirs = swap(lax.dynamic_index_in_dim(total, 1 - core, 0, False), "c")
        low = core == 0
        return to_full(jnp.where(low, mine, theirs)), to_full(jnp.where(low, theirs, mine))


def both_rows(keep, send):
    got = swap(send, "c")
    low = lax.axis_index("c") == 0
    return jnp.where(low, jnp.concatenate([keep, got], 0), jnp.concatenate([got, keep], 0))


def column_half(value, other=False):
    size = value.shape[-1] // 2
    core = lax.axis_index("c")
    return lax.dynamic_slice_in_dim(value, (1 - core if other else core) * size, size, value.ndim - 1)


def odd_blocks(value, other=False):
    core = lax.axis_index("c")
    blocks = value.reshape(value.shape[0], -1, 2, 128)
    return lax.dynamic_index_in_dim(blocks, 1 - core if other else core, 2, False).reshape(
        value.shape[0], -1
    )


def nt(left, right):
    return lax.dot_general(
        left, right, (((1,), (1,)), ((), ())), preferred_element_type=jnp.float32
    )


def norm_parts(values):
    center = values - jnp.mean(values, -1, keepdims=True)
    factor = lax.rsqrt(jnp.mean(center * center, -1, keepdims=True) + EPSILON)
    return center * factor, factor


def norm(values, gain, bias):
    return norm_parts(values)[0] * gain + bias


def norm_back(values, gain, grad):
    shape, factor = norm_parts(values)
    inner = grad * gain
    mean = jnp.mean(inner, -1, keepdims=True)
    along = jnp.mean(inner * shape, -1, keepdims=True)
    return (
        factor * (inner - mean - shape * along),
        jnp.sum(grad * shape, 0, keepdims=True),
        jnp.sum(grad, 0, keepdims=True),
    )


def gate(values):
    return 0.5 * values * (1.0 + jnp.tanh(GELU_SCALE * (values + 0.044715 * values * values * values)))


def gate_slope(values):
    square = values * values
    slope = jnp.tanh(GELU_SCALE * values * (1.0 + 0.044715 * square))
    return 0.5 * (1.0 + slope) + 0.5 * values * (1.0 - slope * slope) * (
        GELU_SCALE * (1.0 + 3 * 0.044715 * square)
    )


def columns(side, size, start=0, width=None):
    return pl.ds(pl.multiple_of(side * size + start, 128), size if width is None else width)


def run(kernel, outs, ins, grid=(), in_specs=None, out_specs=None, scratch=(), name=None, **more):
    whole = pl.BlockSpec(memory_space=pltpu.VMEM)
    in_specs = in_specs or {}
    out_specs = out_specs or {}

    def spec(given, value):
        if given is not None:
            return given
        if not grid:
            return whole
        return pl.BlockSpec(value.shape, lambda *_, rank=len(value.shape): (0,) * rank)

    core = lax.axis_index("c").astype(jnp.int32).reshape(1)
    outs = [jax.ShapeDtypeStruct(shape, dtype) for shape, dtype in outs]
    return pl.pallas_call(
        kernel,
        out_shape=outs,
        grid=grid,
        in_specs=[pl.BlockSpec(memory_space=pltpu.SMEM)]
        + [spec(in_specs.get(i), v) for i, v in enumerate(ins)],
        out_specs=[spec(out_specs.get(i), v) for i, v in enumerate(outs)],
        scratch_shapes=scratch,
        compiler_params=pltpu.CompilerParams(vmem_limit_bytes=VMEM_LIMIT),
        cost_estimate=estimate(name),
        name=name,
        **more,
    )(core, *ins)


HALF = jnp.bfloat16
FULL = jnp.float32


def embed_kernel(core, mine, theirs, weight, out_mine, out_theirs):
    out_mine[...] = product(mine[...], weight[...])
    out_theirs[...] = product(theirs[...], weight[...])


def embed_tokens(mine, theirs, weight):
    shape = ((mine.shape[0], weight.shape[1]), FULL)
    return run(embed_kernel, [shape, shape], [mine, theirs, weight], name="embed_tokens")


def norm_kernel(core, mine, got, gains, biases, embedded, normed):
    size = mine.shape[1]
    embedded[:, columns(core[0], size)] = mine[...]
    embedded[:, columns(1 - core[0], size)] = got[...]
    values = embedded[...] + biases[0:1]
    embedded[...] = values
    normed[...] = to_half(norm(values, gains[0:1], biases[1:2]))


def norm_tokens(mine, got, gains, biases):
    shape = (mine.shape[0], gains.shape[1])
    return run(
        norm_kernel, [(shape, FULL), (shape, HALF)], [mine, got, gains, biases], name="norm_tokens"
    )


def token_rows(side, rows):
    return pl.ds(pl.multiple_of(side * rows, rows), rows)


def project_kernel(core, mine, got, weight, both, out):
    rows = mine.shape[0]

    @pl.when(pl.program_id(0) == 0)
    def _():
        both[token_rows(core[0], rows), :] = mine[...]
        both[token_rows(1 - core[0], rows), :] = got[...]

    out[0] = to_half(product(both[...], weight[...]))


def project_tokens(mine, got, weight):
    rows, width = mine.shape
    each = weight.shape[1] // 4
    return run(
        project_kernel,
        [((2 * rows, width), HALF), ((4, 2 * rows, each), HALF)],
        [mine, got, weight],
        grid=(4,),
        in_specs={2: pl.BlockSpec((width, each), lambda j: (0, j))},
        out_specs={1: pl.BlockSpec((1, 2 * rows, each), lambda j: (j, 0, 0))},
        name="project_tokens",
    )


def middle_kernel(
    core, embedded, parts, got, weight, gains, biases, attended, middle, second
):
    rows = got.shape[1]
    each = parts.shape[2]
    width = embedded.shape[1]
    for q in range(4):
        attended[:, columns(core[0], 4 * each, q * each, each)] = parts[
            q, token_rows(core[0], rows), :
        ]
        attended[:, columns(1 - core[0], 4 * each, q * each, each)] = got[q]
    values = embedded[...] + product(attended[...], weight[:, :width]) + biases[2:3]
    middle[...] = values
    second[...] = to_half(norm(values, gains[1:2], biases[3:4]))


def middle_tokens(embedded, parts, got, weight, gains, biases):
    shape = embedded.shape
    return run(
        middle_kernel,
        [(shape, HALF), (shape, FULL), (shape, HALF)],
        [embedded, parts, got, weight, gains, biases],
        name="middle_tokens",
    )


def expand_kernel(core, mine, got, weight, bias, both, expanded, activated):
    rows = mine.shape[0]

    @pl.when(pl.program_id(0) == 0)
    def _():
        both[:rows, :] = mine[...]
        both[rows:, :] = got[...]

    values = product(both[...], weight[...]) + bias[...]
    expanded[...] = values
    activated[...] = to_half(gate(values))


def expand_tokens(mine, got, weight, bias):
    rows, width = mine.shape
    hidden = weight.shape[1]
    tile = pl.BlockSpec((2 * rows, 512), lambda j: (0, j))
    return run(
        expand_kernel,
        [((2 * rows, width), HALF), ((2 * rows, hidden), FULL), ((2 * rows, hidden), HALF)],
        [mine, got, weight, bias],
        grid=(hidden // 512,),
        in_specs={
            2: pl.BlockSpec((width, 512), lambda j: (0, j)),
            3: pl.BlockSpec((1, 512), lambda j: (0, j)),
        },
        out_specs={1: tile, 2: tile},
        name="expand_tokens",
    )


def reduce_kernel(core, activated, weight, mine, theirs, total):
    step = pl.program_id(0)
    rows = mine.shape[0]
    values = product(activated[...], weight[...])

    @pl.when(step == 0)
    def _():
        total[...] = values

    @pl.when(step > 0)
    def _():
        total[...] += values

    @pl.when(step == pl.num_programs(0) - 1)
    def _():
        mine[...] = total[:rows, :]
        theirs[...] = to_half(total[rows:, :])


def reduce_tokens(activated, weight):
    rows, hidden = activated.shape
    width = weight.shape[1]
    shape = ((rows // 2, width), FULL)
    return run(
        reduce_kernel,
        [shape, (shape[0], HALF)],
        [activated, weight],
        grid=(hidden // 512,),
        in_specs={
            0: pl.BlockSpec((rows, 512), lambda j: (0, j)),
            1: pl.BlockSpec((512, width), lambda j: (j, 0)),
        },
        scratch=[pltpu.VMEM((rows, width), FULL)],
        name="reduce_tokens",
    )


def slot_of(p, size):
    return (2 * p * size, 2 * size) if p < 4 else (8 * size + (p - 4) * size, size)


def encode_kernel(
    core, middle, mine, got, weight, biases, pred_weight, pred_gains, pred_biases,
    encoded, pred_in, normed, parts, projected,
):
    full = middle.shape[1]
    encoded[...] = to_half(middle[...] + (mine[...] + to_full(got[...])) + biases[4:5])
    values = product(encoded[...], weight[:, full:]) + pred_biases[0:1]
    pred_in[...] = values
    normed[...] = to_half(norm(values, pred_gains[0:1], pred_biases[1:2]))
    width = values.shape[1]
    projected[...] = to_half(nt(pred_weight[...], normed[...]))
    both = parts.shape[1] // 3
    for p in range(PLANE):
        start, size = slot_of(p, both // 2)
        for t in range(3):
            parts[p, t * both : t * both + size, :] = projected[
                t * width + start : t * width + start + size, :
            ]
            if size < both:
                parts[p, t * both + size : (t + 1) * both, :] = jnp.zeros(
                    (both - size, parts.shape[2]), HALF
                )


def encode_tokens(middle, mine, got, weight, biases, pred_weights, pred_gains, pred_biases):
    rows = middle.shape[0]
    width = pred_gains.shape[1]
    each = 3 * 2 * width // PRED_HEADS
    return run(
        encode_kernel,
        [
            (middle.shape, HALF),
            ((rows, width), FULL),
            ((rows, width), HALF),
            ((PLANE, each, rows), HALF),
        ],
        [middle, mine, got, weight, biases, pred_weights, pred_gains, pred_biases],
        grid=(1,),
        in_specs={5: pl.BlockSpec((3 * width, width), lambda j: (0, 0))},
        scratch=[pltpu.VMEM((3 * width, rows), HALF)],
        name="encode_tokens",
    )


def pred_feed_kernel(
    core, pred_in, parts, weights, gains, biases, hidden_bias, cotangent,
    prediction, grad_middle, grad_weights, grad_parts, sums, hidden_sums, attended, expanded, work,
):
    width = pred_in.shape[1]
    both = parts.shape[1]
    for p in range(PLANE):
        start, size = slot_of(p, both // 2)
        work[start : start + size, :] = to_full(parts[p, :size, :])
    attended[...] = to_half(work[...].T)
    out_rows = slice(3 * width, weights.shape[0])
    slot = [slice(i * width, (i + 1) * width) for i in range(3)]
    middle = pred_in[...] + nt(attended[...], weights[out_rows, slot[0]]) + biases[2:3]
    second = to_half(norm(middle, gains[1:2], biases[3:4]))
    expanded[...] = nt(second, weights[:, slot[1]]) + hidden_bias[...]
    activated = to_half(gate(expanded[...]))
    result = middle + product(activated, weights[:, slot[2]]) + biases[4:5]
    prediction[...] = to_half(result)
    half_grad = cotangent[...]
    grad = to_full(half_grad)
    sums[2:3, :] = jnp.sum(grad, 0, keepdims=True)
    grad_weights[:, slot[2]] = to_half(left_product(activated, half_grad))
    grad_expanded = nt(half_grad, weights[:, slot[2]]) * gate_slope(expanded[...])
    hidden_sums[...] = jnp.sum(grad_expanded, 0, keepdims=True)
    expanded_half = to_half(grad_expanded)
    grad_weights[:, slot[1]] = to_half(left_product(expanded_half, second))
    grad_second = product(expanded_half, weights[:, slot[1]])
    from_norm, gain, bias = norm_back(middle, gains[1:2], grad_second)
    total = grad + from_norm
    grad_middle[...] = total
    sums[0:1, :] = jnp.sum(total, 0, keepdims=True)
    sums[1:2, :] = bias
    sums[3:4, :] = gain
    sums[4:8, :] = jnp.zeros((4, width), FULL)
    middle_half = to_half(total)
    grad_weights[out_rows, slot[0]] = to_half(left_product(middle_half, attended[...]))
    work[...] = product(middle_half, weights[out_rows, slot[0]]).T
    for p in range(PLANE):
        start, size = slot_of(p, both // 2)
        grad_parts[p, :size, :] = to_half(work[start : start + size, :])
        if size < both:
            grad_parts[p, size:, :] = jnp.zeros((both - size, parts.shape[2]), HALF)


def pred_feed(pred_in, parts, weights, gains, biases, cotangent):
    rows, width = pred_in.shape
    hidden = weights.shape[0]
    return run(
        pred_feed_kernel,
        [
            ((rows, width), HALF),
            ((rows, width), FULL),
            (weights.shape, HALF),
            (parts.shape, HALF),
            ((8, width), FULL),
            ((1, hidden), FULL),
        ],
        [pred_in, parts, weights, gains, biases, biases[5:].reshape(1, hidden), cotangent],
        scratch=[
            pltpu.VMEM((rows, width), HALF),
            pltpu.VMEM((rows, hidden), FULL),
            pltpu.VMEM((width, rows), FULL),
        ],
        name="pred_feed",
    )


def pred_back_kernel(
    core, parts, normed, pred_in, grad_middle, weight, gains, embed, _,
    grad_weight, half_in, grad_encoded, encoded_half, sums, projected,
):
    width = pred_in.shape[1]
    both = parts.shape[1] // 3
    for p in range(PLANE):
        start, size = slot_of(p, both // 2)
        for t in range(3):
            projected[t * width + start : t * width + start + size, :] = parts[
                p, t * both : t * both + size, :
            ]
    grad_weight[...] = to_half(product(projected[...], normed[...]))
    grad_normed = left_product(projected[...], weight[...])
    into_norm, gain, bias = norm_back(pred_in[...], gains[0:1], grad_normed)
    total = grad_middle[...] + into_norm
    sums[0:1, :] = jnp.sum(total, 0, keepdims=True)
    sums[1:2, :] = bias
    sums[2:3, :] = gain
    sums[3:8, :] = jnp.zeros((5, width), FULL)
    half_in[...] = to_half(total)
    values = nt(half_in[...], embed[:, embed.shape[1] - width :])
    grad_encoded[...] = values
    encoded_half[...] = to_half(values)


def pred_back(parts, normed, pred_in, grad_middle, weights, gains, embed, grad_weights):
    rows, width = pred_in.shape
    full = embed.shape[0]
    block = pl.BlockSpec((3 * width, width), lambda j: (0, 0))
    return run(
        pred_back_kernel,
        [
            (grad_weights.shape, HALF),
            ((rows, width), HALF),
            ((rows, full), FULL),
            ((rows, full), HALF),
            ((8, width), FULL),
        ],
        [parts, normed, pred_in, grad_middle, weights, gains, embed, grad_weights],
        grid=(1,),
        in_specs={4: block, 7: pl.BlockSpec(memory_space=pl.ANY)},
        out_specs={0: block},
        scratch=[pltpu.VMEM((3 * width, rows), HALF)],
        name="pred_back",
        input_output_aliases={8: 0},
    )


def reduce_back_kernel(core, mine, got, weight, expanded, both, out, sums):
    rows = mine.shape[0]

    @pl.when(pl.program_id(0) == 0)
    def _():
        both[:rows, :] = mine[...]
        both[rows:, :] = got[...]

    values = nt(both[...], weight[...]) * gate_slope(expanded[...])
    out[...] = to_half(values)
    sums[...] = jnp.sum(values, 0, keepdims=True)


def reduce_back(mine, got, weight, expanded):
    rows, hidden = expanded.shape
    width = mine.shape[1]
    tile = pl.BlockSpec((rows, 512), lambda j: (0, j))
    return run(
        reduce_back_kernel,
        [((rows, width), HALF), ((rows, hidden), HALF), ((1, hidden), FULL)],
        [mine, got, weight, expanded],
        grid=(hidden // 512,),
        in_specs={2: pl.BlockSpec((512, width), lambda j: (j, 0)), 3: tile},
        out_specs={1: tile, 2: pl.BlockSpec((1, 512), lambda j: (0, j))},
        name="reduce_back",
    )


def expand_back_kernel(core, grad, weight, mine, theirs, total):
    step = pl.program_id(0)
    rows = mine.shape[0]
    values = nt(grad[...], weight[...])

    @pl.when(step == 0)
    def _():
        total[...] = values

    @pl.when(step > 0)
    def _():
        total[...] += values

    @pl.when(step == pl.num_programs(0) - 1)
    def _():
        mine[...] = total[:rows, :]
        theirs[...] = to_half(total[rows:, :])


def expand_back(grad, weight):
    rows, hidden = grad.shape
    width = weight.shape[0]
    shape = ((rows // 2, width), FULL)
    return run(
        expand_back_kernel,
        [shape, (shape[0], HALF)],
        [grad, weight],
        grid=(hidden // 512,),
        in_specs={
            0: pl.BlockSpec((rows, 512), lambda j: (0, j)),
            1: pl.BlockSpec((width, 512), lambda j: (0, j)),
        },
        scratch=[pltpu.VMEM((rows, width), FULL)],
        name="expand_back",
    )


def middle_back_kernel(
    core, middle, grad, mine, got, gains, weight, grad_middle, half_middle, sums, keep, send, work
):
    width = middle.shape[1]
    from_norm, gain, bias = norm_back(middle[...], gains[1:2], mine[...] + to_full(got[...]))
    values = grad[...] + from_norm
    grad_middle[...] = values
    sums[0:1, :] = jnp.sum(values, 0, keepdims=True)
    sums[1:2, :] = bias
    sums[2:3, :] = jnp.sum(grad[...], 0, keepdims=True)
    sums[3:4, :] = gain
    sums[4:8, :] = jnp.zeros((4, width), FULL)
    half_middle[...] = to_half(values)
    work[...] = to_half(nt(half_middle[...], weight[:, :width]))
    each = keep.shape[2]
    for q in range(4):
        keep[q] = work[:, columns(core[0], 4 * each, q * each, each)]
        send[q] = work[:, columns(1 - core[0], 4 * each, q * each, each)]


def middle_back(middle, grad, mine, got, gains, weight):
    rows, width = middle.shape
    parts = ((4, rows, width // PLANE), HALF)
    return run(
        middle_back_kernel,
        [((rows, width), FULL), ((rows, width), HALF), ((8, width), FULL), parts, parts],
        [middle, grad, mine, got, gains, weight],
        scratch=[pltpu.VMEM((rows, width), HALF)],
        name="middle_back",
    )


def project_back_kernel(core, parts, weight, mine, theirs, total):
    step = pl.program_id(0)
    rows = mine.shape[0]
    values = nt(parts[0], weight[...])

    @pl.when(step == 0)
    def _():
        total[...] = values

    @pl.when(step > 0)
    def _():
        total[...] += values

    @pl.when(step == pl.num_programs(0) - 1)
    def _():
        mine[...] = total[token_rows(core[0], rows), :]
        theirs[...] = to_half(total[token_rows(1 - core[0], rows), :])


def project_back(parts, weight):
    _, rows, each = parts.shape
    width = weight.shape[0]
    shape = ((rows // 2, width), FULL)
    return run(
        project_back_kernel,
        [shape, (shape[0], HALF)],
        [parts, weight],
        grid=(4,),
        in_specs={
            0: pl.BlockSpec((1, rows, each), lambda j: (j, 0, 0)),
            1: pl.BlockSpec((width, each), lambda j: (0, j)),
        },
        scratch=[pltpu.VMEM((rows, width), FULL)],
        name="project_back",
    )


def input_back_kernel(core, embedded, grad, mine, got, gains, keep, send, sums, work):
    into_norm, gain, bias = norm_back(embedded[...], gains[0:1], mine[...] + to_full(got[...]))
    values = grad[...] + into_norm
    sums[0:1, :] = jnp.sum(values, 0, keepdims=True)
    sums[1:2, :] = bias
    sums[2:3, :] = gain
    sums[3:8, :] = jnp.zeros((5, values.shape[1]), FULL)
    work[...] = to_half(values)
    size = keep.shape[1]
    keep[...] = work[:, columns(core[0], size)]
    send[...] = work[:, columns(1 - core[0], size)]


def input_back(embedded, grad, mine, got, gains):
    rows, width = embedded.shape
    part = ((rows, width // 2), HALF)
    return run(
        input_back_kernel,
        [part, part, ((8, width), FULL)],
        [embedded, grad, mine, got, gains],
        scratch=[pltpu.VMEM((rows, width), HALF)],
        name="input_back",
    )


def pixel_kernel(core, mine, got, weight, out_mine, out_theirs):
    out_mine[...] = nt(mine[...], weight[...])
    out_theirs[...] = to_half(nt(got[...], weight[...]))


def pixel_back(mine, got, weight):
    shape = (mine.shape[0], weight.shape[0])
    return run(
        pixel_kernel, [(shape, FULL), (shape, HALF)], [mine, got, weight], name="pixel_back"
    )


def weight_kernel(count, place, *refs):
    lefts, rights = refs[:count], refs[count : 2 * count]
    keep_one, send_one, keep_two, send_two, work = refs[2 * count :]
    step, half = pl.program_id(0), pl.num_programs(0) // 2
    rows = work.shape[1]
    if len(rights[0].shape) == 3:
        each = rights[0].shape[2]
        for q in range(rights[0].shape[0]):
            values = to_half(left_product(lefts[0][...], rights[0][q]))
            for i in range(4):
                work[i, :, q * each : (q + 1) * each] = values[i * rows : (i + 1) * rows]
    else:
        values = left_product(lefts[0][...], rights[0][...])
        for left, right in zip(lefts[1:], rights[1:]):
            values += left_product(left[...], right[...])
        values = to_half(values)
        for i in range(4):
            work[i] = values[i * rows : (i + 1) * rows]
    y, x = place[1], place[2]

    @pl.when(step < half)
    def _():
        for k in range(2):
            keep_one[k, 0] = work[(y ^ k) * 2 + x]
            send_one[k, 0] = work[(y ^ k) * 2 + (1 - x)]

    @pl.when(step >= half)
    def _():
        for k in range(2):
            keep_two[k, 0] = work[y * 2 + (x ^ k)]
            send_two[k, 0] = work[(1 - y) * 2 + (x ^ k)]


def weight_grad(lefts, rights):
    depth = lefts[0].shape[1]
    right = rights[0]
    width = right.shape[0] * right.shape[2] if right.ndim == 3 else right.shape[1]
    count = lax.axis_size("z")
    rows = depth // (4 * count)
    if rows % 32 != 0:
        total = 0.0
        for left, right in zip(lefts, rights):
            if right.ndim == 3:
                right = jnp.moveaxis(right, 0, 1).reshape(left.shape[0], -1)
            total += left_product(left, right)
        return routes(by_distance(to_half(total).reshape(count, 2, 2, rows, width), 3))
    half = count // 2
    pairs = len(lefts)

    def whole(value):
        return pl.BlockSpec(value.shape, lambda j, place, rank=value.ndim: (0,) * rank)

    near = pl.BlockSpec((2, 1, rows, width), lambda j, place: (0, jnp.minimum(j, half - 1), 0, 0))
    far = pl.BlockSpec((2, 1, rows, width), lambda j, place: (0, jnp.maximum(j - half, 0), 0, 0))
    return pl.pallas_call(
        functools.partial(weight_kernel, pairs),
        out_shape=[jax.ShapeDtypeStruct((2, half, rows, width), HALF)] * 4,
        grid_spec=pltpu.PrefetchScalarGridSpec(
            num_scalar_prefetch=1,
            grid=(count,),
            in_specs=[
                pl.BlockSpec((v.shape[0], 4 * rows), lambda j, place: (0, place[0] ^ j))
                for v in lefts
            ]
            + [whole(v) for v in rights],
            out_specs=[near, near, far, far],
            scratch_shapes=[pltpu.VMEM((4, rows, width), HALF)],
        ),
        compiler_params=pltpu.CompilerParams(vmem_limit_bytes=VMEM_LIMIT),
        cost_estimate=estimate("weight_grad"),
        name="weight_grad",
    )(position(), *lefts, *rights)


def side_kernel(core, left_one, left_two, right_one, right_two, out):
    width = right_one.shape[1]
    out[:, :width] = to_half(left_product(left_one[...], right_one[...]))
    out[:, width:] = to_half(left_product(left_two[...], right_two[...]))


def weight_grads(lefts, rights):
    depth = lefts[0].shape[1]
    width = rights[0].shape[1] + rights[1].shape[1]
    tile = pl.BlockSpec((lefts[0].shape[0], 512), lambda j: (0, j))
    return run(
        side_kernel,
        [((depth, width), HALF)],
        [*lefts, *rights],
        grid=(depth // 512,),
        in_specs={0: tile, 1: tile},
        out_specs={0: pl.BlockSpec((512, width), lambda j: (j, 0))},
        name="weight_grads",
    )[0]


class Total:
    def __init__(self, order, value):
        self.order, self.held, self.flight = order, value, None
        self.steps = [
            (axis, 1 << bit)
            for axis in ("c", "x", "y", "z")
            for bit in range(lax.axis_size(axis).bit_length() - 1)
        ]

    def step(self):
        if self.flight is not None:
            self.held = self.held + self.order.enter(self.flight)
        if self.steps:
            axis, distance = self.steps.pop(0)
            self.held = self.order.leave(self.order.enter(self.held))
            self.flight = swap(self.held, axis, distance)
        else:
            self.flight = None

    def done(self):
        while self.flight is not None:
            self.step()
        return self.held


def head_lanes(values, head, size):
    lane = lax.broadcasted_iota(jnp.int32, values.shape, 1)
    return jnp.where((lane >= head * size) & (lane < (head + 1) * size), values, jnp.zeros_like(values))


def clip_bias(label_column_ref):
    low = label_column_ref[CLIP_LOW : CLIP_LOW + MARGIN, :]
    high = label_column_ref[CLIP_HIGH - MARGIN : CLIP_HIGH, :]
    return jnp.where(low == CLIP_ID, 0.0, MASKED), jnp.where(high == CLIP_ID, 0.0, MASKED)


def add_margins(scores, biases):
    low, high = biases
    return jnp.concatenate(
        [scores[:MARGIN] + low, scores[MARGIN:-MARGIN], scores[-MARGIN:] + high], 0
    )


def softmax_columns(scores, small):
    top = 0.0 if small else jnp.max(scores, 0, keepdims=True)
    expo = jnp.exp2(scores if small else scores - top)
    total = jnp.sum(expo, 0, keepdims=True)
    return to_half(expo), total, top + jnp.log2(total)


def largest_square(values, size):
    lane = lax.broadcasted_iota(jnp.int32, (values.shape[1], 128), 1)
    row = lax.broadcasted_iota(jnp.int32, (values.shape[1], 128), 0)
    picks = jnp.where(row // size == lane, 1.0, 0.0).astype(jnp.bfloat16)
    full = to_full(values)
    return jnp.max(product(to_half(full * full), picks), 0, keepdims=True)


SMALL = 60.0


def attend_kernel(size, qkv_ref, column_ref, row_ref, out_ref, log_ref, q_s, k_s, vt_s, ot_s):
    both = 2 * size
    factor = LOG2E * size**-0.5
    turned = len(qkv_ref.shape) == 3
    if turned:
        for p in range(PLANE):
            here = slice(p * BLOCK, (p + 1) * BLOCK)
            q_s[here, :] = to_half(to_full(qkv_ref[p, :both, :]).T)
            k_s[here, :] = to_half(to_full(qkv_ref[p, both : 2 * both, :]).T)
            vt_s[:, here] = qkv_ref[p, 2 * both :, :]
    else:
        q_s[...] = qkv_ref[:, :both]
        k_s[...] = qkv_ref[:, both : 2 * both]
        vt_s[...] = to_half(to_full(qkv_ref[:, 2 * both :]).T)
    biases = clip_bias(column_ref)
    squares = largest_square(q_s[...], size) * largest_square(k_s[...], size)
    bound = jnp.max(squares) * factor**2

    def heads(keys, values_t, queries, masked, small):
        outs, logs = [], []
        for head in range(2):
            scores = masked(nt(keys, head_lanes(queries, head, size)) * factor)
            probs, total, log_total = softmax_columns(scores, small)
            mixed = product(values_t, probs)[head * size : (head + 1) * size]
            outs.append(mixed / total)
            logs.append(log_total)
        return jnp.concatenate(outs, 0), jnp.concatenate(logs, 0)

    def over_clip(queries, small):
        return heads(
            k_s[CLIP_LOW:CLIP_HIGH, :],
            vt_s[:, CLIP_LOW:CLIP_HIGH],
            queries,
            lambda scores: add_margins(scores, biases),
            small,
        )

    last = (PLANE - 1) * BLOCK
    ends = ((0, 128, 0), (last, 0, 128))

    def all_rows(small, block):
        @pl.loop(0, (last - BLOCK) // block)
        def _(i):
            here = pl.ds(pl.multiple_of(BLOCK + i * block, BLOCK), block)
            out, logs = over_clip(q_s[here, :], small)
            ot_s[:, here] = out
            log_ref[:2, here] = logs

        edge_out, edge_logs = over_clip(
            jnp.concatenate([q_s[BLOCK - 128 : BLOCK, :], q_s[last : last + 128, :]], 0), small
        )
        for start, at, inner in ends:
            here = slice(start, start + BLOCK)
            same = column_ref[here, :] == row_ref[:, here]
            out, logs = heads(
                k_s[here, :],
                vt_s[:, here],
                q_s[here, :],
                lambda scores: jnp.where(same, scores, MASKED),
                small,
            )
            ot_s[:, here] = out
            log_ref[:2, here] = logs
            where = slice(start + at, start + at + 128)
            clip = row_ref[:, where] == CLIP_ID
            ot_s[:, where] = jnp.where(clip, edge_out[:, inner : inner + 128], ot_s[:, where])
            log_ref[:2, where] = jnp.where(
                clip, edge_logs[:, inner : inner + 128], log_ref[:2, where]
            )

    pl.when(bound < SMALL**2)(lambda: all_rows(True, 3 * BLOCK))
    pl.when(jnp.logical_not(bound < SMALL**2))(lambda: all_rows(False, BLOCK))
    log_ref[2:, :] = jnp.zeros((6, PLANE * BLOCK), jnp.float32)
    if turned:
        for p in range(PLANE):
            out_ref[p] = to_half(ot_s[:, p * BLOCK : (p + 1) * BLOCK])
    else:
        out_ref[...] = to_half(ot_s[...].T)


def attend_back_kernel(
    size, qkv_ref, out_ref, grad_ref, log_ref, column_ref, row_ref, dqkv_ref,
    q_s, k_s, v_s, kt_s, d_s, dqt_s, dk_s, dv_s, *g_s,
):
    both = 2 * size
    factor = LOG2E * size**-0.5
    scale = size**-0.5
    turned = len(qkv_ref.shape) == 3
    grads = g_s[0] if turned else grad_ref
    if turned:
        for p in range(PLANE):
            here = slice(p * BLOCK, (p + 1) * BLOCK)
            for i, rows_s in enumerate((q_s, k_s, v_s)):
                rows_s[here, :] = to_half(to_full(qkv_ref[p, i * both : (i + 1) * both, :]).T)
            kt_s[:, here] = qkv_ref[p, both : 2 * both, :]
            full = to_full(grad_ref[p])
            grads[here, :] = to_half(full.T)
            weighted = full * to_full(out_ref[p])
            for head in range(2):
                d_s[head : head + 1, here] = jnp.sum(
                    weighted[head * size : (head + 1) * size], 0, keepdims=True
                )
    else:
        q_s[...] = qkv_ref[:, :both]
        k_s[...] = qkv_ref[:, both : 2 * both]
        v_s[...] = qkv_ref[:, 2 * both :]
        kt_s[...] = to_half(to_full(qkv_ref[:, both : 2 * both]).T)
        weighted = (to_full(grad_ref[...]) * to_full(out_ref[...])).T
        for head in range(2):
            d_s[head : head + 1, :] = jnp.sum(
                weighted[head * size : (head + 1) * size], 0, keepdims=True
            )
    dk_s[...] = jnp.zeros_like(dk_s)
    dv_s[...] = jnp.zeros_like(dv_s)
    biases = clip_bias(column_ref)

    def pulled(keys, values, keys_t, queries, grads, logs, centres, masked):
        outs, probs_all, scores_all, queries_all, grads_all = [], [], [], [], []
        for head in range(2):
            own_queries = head_lanes(queries, head, size)
            own_grads = head_lanes(grads, head, size)
            probs = jnp.exp2(masked(nt(keys, own_queries) * factor) - logs[head : head + 1])
            pull = nt(values, own_grads)
            grad_scores = to_half(probs * (pull - centres[head : head + 1]))
            outs.append(product(keys_t, grad_scores)[head * size : (head + 1) * size] * scale)
            probs_all.append(to_half(probs))
            scores_all.append(grad_scores)
            queries_all.append(own_queries)
            grads_all.append(own_grads)
        grad_keys = sum(product(s, q) for s, q in zip(scores_all, queries_all)) * scale
        grad_values = sum(product(p, g) for p, g in zip(probs_all, grads_all))
        return jnp.concatenate(outs, 0), grad_keys, grad_values

    def over_clip(queries, grads, logs, centres):
        return pulled(
            k_s[CLIP_LOW:CLIP_HIGH, :],
            v_s[CLIP_LOW:CLIP_HIGH, :],
            kt_s[:, CLIP_LOW:CLIP_HIGH],
            queries,
            grads,
            logs,
            centres,
            lambda scores: add_margins(scores, biases),
        )

    @pl.loop(1, PLANE - 1)
    def _(block):
        start = pl.multiple_of(block * BLOCK, BLOCK)
        here = pl.ds(start, BLOCK)
        out, grad_keys, grad_values = over_clip(
            q_s[here, :], grads[here, :], log_ref[:2, here], d_s[:2, here]
        )
        dqt_s[:, here] = out
        dk_s[CLIP_LOW:CLIP_HIGH, :] += grad_keys
        dv_s[CLIP_LOW:CLIP_HIGH, :] += grad_values

    last = (PLANE - 1) * BLOCK
    near, far = slice(BLOCK - 128, BLOCK), slice(last, last + 128)

    def ends(ref, axis):
        if axis == 0:
            return jnp.concatenate([ref[near, :], ref[far, :]], 0)
        return jnp.concatenate([ref[:2, near], ref[:2, far]], 1)

    edge_labels = jnp.concatenate([row_ref[:, near], row_ref[:, far]], 1)
    edge_logs = jnp.where(edge_labels == CLIP_ID, ends(log_ref, 1), -MASKED)
    edge_out, grad_keys, grad_values = over_clip(
        ends(q_s, 0), ends(grads, 0), edge_logs, ends(d_s, 1)
    )
    dk_s[CLIP_LOW:CLIP_HIGH, :] += grad_keys
    dv_s[CLIP_LOW:CLIP_HIGH, :] += grad_values
    for start, at, inner in ((0, 128, 0), (last, 0, 128)):
        here = slice(start, start + BLOCK)
        labels = row_ref[:, here]
        same = column_ref[here, :] == labels
        logs = jnp.where(labels == CLIP_ID, -MASKED, log_ref[:2, here])
        out, grad_keys, grad_values = pulled(
            k_s[here, :],
            v_s[here, :],
            kt_s[:, here],
            q_s[here, :],
            grads[here, :],
            logs,
            d_s[:2, here],
            lambda scores: jnp.where(same, scores, MASKED),
        )
        dqt_s[:, here] = out
        where = slice(start + at, start + at + 128)
        dqt_s[:, where] += edge_out[:, inner : inner + 128]
        dk_s[here, :] += grad_keys
        dv_s[here, :] += grad_values
    if turned:
        for p in range(PLANE):
            here = slice(p * BLOCK, (p + 1) * BLOCK)
            dqkv_ref[p, :both, :] = to_half(dqt_s[:, here])
            dqkv_ref[p, both : 2 * both, :] = to_half(dk_s[here, :].T)
            dqkv_ref[p, 2 * both :, :] = to_half(dv_s[here, :].T)
    else:
        dqkv_ref[:, :both] = to_half(dqt_s[...].T)
        dqkv_ref[:, both : 2 * both] = to_half(dk_s[...])
        dqkv_ref[:, 2 * both :] = to_half(dv_s[...])


def attend(qkv, labels):
    turned = qkv.ndim == 3
    tokens = labels.shape[0]
    both = qkv.shape[1] // 3
    shape = (PLANE, both, BLOCK) if turned else (tokens, both)
    return pl.pallas_call(
        functools.partial(attend_kernel, both // 2),
        out_shape=(
            jax.ShapeDtypeStruct(shape, jnp.bfloat16),
            jax.ShapeDtypeStruct((8, tokens), jnp.float32),
        ),
        scratch_shapes=[
            pltpu.VMEM((tokens, both), jnp.bfloat16),
            pltpu.VMEM((tokens, both), jnp.bfloat16),
            pltpu.VMEM((both, tokens), jnp.bfloat16),
            pltpu.VMEM((both, tokens), jnp.float32),
        ],
        compiler_params=pltpu.CompilerParams(vmem_limit_bytes=VMEM_LIMIT),
        cost_estimate=estimate("attend"),
        name="attend",
    )(qkv, labels[:, None], labels[None, :])


def attend_back(qkv, out, grad, logs, labels):
    turned = qkv.ndim == 3
    tokens = labels.shape[0]
    both = qkv.shape[1] // 3
    return pl.pallas_call(
        functools.partial(attend_back_kernel, both // 2),
        out_shape=jax.ShapeDtypeStruct(qkv.shape, jnp.bfloat16),
        scratch_shapes=[
            pltpu.VMEM((tokens, both), jnp.bfloat16),
            pltpu.VMEM((tokens, both), jnp.bfloat16),
            pltpu.VMEM((tokens, both), jnp.bfloat16),
            pltpu.VMEM((both, tokens), jnp.bfloat16),
            pltpu.VMEM((8, tokens), jnp.float32),
            pltpu.VMEM((both, tokens), jnp.float32),
            pltpu.VMEM((tokens, both), jnp.float32),
            pltpu.VMEM((tokens, both), jnp.float32),
        ]
        + ([pltpu.VMEM((tokens, both), jnp.bfloat16)] if turned else []),
        compiler_params=pltpu.CompilerParams(vmem_limit_bytes=VMEM_LIMIT),
        cost_estimate=estimate("attend_back"),
        name="attend_back",
    )(qkv, out, grad, logs, labels[:, None], labels[None, :])


def exchange(parts):
    return lax.all_to_all(parts, GROUP_AXES, split_axis=0, concat_axis=0, tiled=True)


def to_heads(parts, axes):
    moved = lax.all_to_all(parts, axes, split_axis=0, concat_axis=0, tiled=True)
    return moved.reshape(-1, parts.shape[2])


def to_tokens(values, axes):
    count = PLANE // (2 if len(axes) == 2 else 1)
    parts = values.reshape(count, -1, values.shape[1])
    return lax.all_to_all(parts, axes, split_axis=0, concat_axis=0, tiled=True)


def encoder_columns(weight):
    rows, columns = weight.shape
    return weight.reshape(rows, 3, PLANE, -1).transpose(0, 2, 1, 3).reshape(rows, columns)


def encoder_columns_back(weight):
    rows, columns = weight.shape
    return weight.reshape(rows, PLANE, 3, -1).transpose(0, 2, 1, 3).reshape(rows, columns)


def per_device(
    pixels,
    clip_index,
    patch_weight,
    encoder_attention,
    encoder_output,
    encoder_expand,
    encoder_reduce,
    predictor_embed,
    predictor_weights,
    encoder_gains,
    encoder_biases,
    predictor_gains,
    predictor_biases,
    cotangent,
):
    labels = lax.dynamic_index_in_dim(clip_index, lax.axis_index("z"), 0, keepdims=False)
    width = encoder_output.shape[1]
    pred_width = predictor_embed.shape[1]
    hidden = encoder_expand.shape[1]

    order = Order()
    shard_rows = predictor_weights.shape[0]
    rows = pixels.shape[0]
    core = lax.axis_index("c")
    low = core == 0
    wide_columns = encoder_columns(to_half(encoder_attention))
    half_patch, half_expand = to_half(patch_weight), to_half(encoder_expand)
    patch = Gather(order, both_rows(column_half(half_patch), column_half(half_patch, True)))
    attention = Gather(order, both_rows(column_half(wide_columns), column_half(wide_columns, True)))
    half_expand = both_rows(odd_blocks(half_expand), odd_blocks(half_expand, True))
    output = Gather(
        order, jnp.concatenate([to_half(encoder_output), to_half(predictor_embed)], 1), True
    )
    predictor = Gather(
        order, to_half(predictor_weights).reshape(shard_rows, 3 * pred_width), True
    )
    hidden_bias = encoder_biases[5:].reshape(-1, 2, 128)
    hidden_bias = lax.dynamic_index_in_dim(hidden_bias, core, 1, False).reshape(1, -1)

    patch.along_z()
    order.leave(attention.held)
    pixels_got = swap(pixels, "c")
    attention.along_z()
    patch.rest_of_z()
    patch.first()
    attention.rest_of_z()
    output.along_z()
    patch.second()
    half_expand, half_reduce = order.enter(half_expand, to_half(encoder_reduce))
    expand = Whole(order, half_expand)
    reduce = Whole(order, half_reduce)
    attention.first()
    output.rest_of_z()
    predictor.along_z()
    patch.done()
    mine, theirs = embed_tokens(pixels, order.enter(pixels_got), patch.own)
    got = swap(order.leave(theirs), "c")
    attention.second()
    embedded, normed = norm_tokens(mine, order.enter(got), encoder_gains, encoder_biases)
    normed = order.leave(normed)
    normed_got = swap(normed, "c")
    output.first()
    predictor.rest_of_z()
    attention.done()

    normed, normed_got = order.enter(normed, normed_got)
    normed_both, parts = project_tokens(normed, normed_got, attention.own)
    qkv = to_heads(order.leave(parts), CHIP_AXES)
    output.second()
    predictor.first()
    qkv = order.enter(qkv)
    mixed_heads, logs = attend(qkv, labels)
    parts = to_tokens(order.leave(mixed_heads), CHIP_AXES)
    output.done()
    predictor.second()
    output.cores()
    parts = order.enter(parts)
    theirs = lax.dynamic_slice_in_dim(parts, (1 - core) * rows, rows, 1)
    got = swap(order.leave(theirs), "c")
    attended, middle, second = middle_tokens(
        embedded, parts, order.enter(got), output.whole, encoder_gains, encoder_biases
    )
    second = order.leave(second)
    second_got = swap(second, "c")
    predictor.done()
    second, second_got = order.enter(second, second_got)
    second_both, expanded, activated = expand_tokens(second, second_got, expand.own, hidden_bias)
    order.leave(activated)
    predictor.cores()
    mine, theirs = reduce_tokens(order.enter(activated), reduce.own)
    got = swap(order.leave(theirs), "c")
    weights = predictor.whole
    encoded, pred_in, pred_normed, parts = encode_tokens(
        middle,
        mine,
        got,
        output.whole,
        encoder_biases,
        weights,
        predictor_gains,
        predictor_biases,
    )
    pred_qkv = exchange(parts)
    pred_heads, pred_logs = attend(pred_qkv, labels)
    prediction, pred_middle_grad, pred_grads, parts, pred_sums, pred_hidden_sums = pred_feed(
        pred_in,
        exchange(pred_heads),
        weights,
        predictor_gains,
        predictor_biases,
        cotangent,
    )

    grad_qkv = attend_back(
        pred_qkv, pred_heads, exchange(parts), pred_logs, labels
    )
    pred_grads, half_in, grad_encoded, encoded_half, pred_in_sums = pred_back(
        exchange(grad_qkv),
        pred_normed,
        pred_in,
        pred_middle_grad,
        weights,
        predictor_gains,
        output.whole,
        pred_grads,
    )

    encoded_half = order.leave(encoded_half)
    half_got = swap(encoded_half, "c")
    sum_p = Scatter.of_cores(order, order.enter(pred_grads))
    encoded_half, half_got = order.enter(encoded_half, half_got)
    grad_both, grad_expanded, hidden_sums = reduce_back(
        encoded_half, half_got, reduce.own, expanded
    )
    order.leave(grad_expanded)
    sum_r = Scatter(order, weight_grad([activated], [order.enter(grad_both)]))
    mine, theirs = expand_back(order.enter(grad_expanded), expand.own)
    got = swap(order.leave(theirs), "c")
    sum_p.first()
    grad_middle, half_middle, middle_sums, keep, send = middle_back(
        middle, grad_encoded, mine, order.enter(got), encoder_gains, output.whole
    )
    got = swap(order.leave(send), "c")
    sum_e = Scatter(order, weight_grad([second_both], [order.enter(grad_expanded)]))
    keep, got = order.enter(keep, got)
    parts = jnp.where(low, jnp.concatenate([keep, got], 1), jnp.concatenate([got, keep], 1))
    grad_heads = to_heads(order.leave(parts), CHIP_AXES)
    sum_r.second()
    late_middle, late_in = order.enter(half_middle, half_in)
    sum_o = Scatter.of_cores(order, weight_grads([attended, encoded], [late_middle, late_in]))
    sum_p.second()
    grad_heads = order.enter(grad_heads)
    grad_qkv = attend_back(qkv, mixed_heads, grad_heads, logs, labels)
    parts = to_tokens(order.leave(grad_qkv), CHIP_AXES)
    sum_r.along_z()
    sum_o.first()
    sum_e.second()
    sum_r.rest_of_z()
    sum_p.along_z()
    parts = order.enter(parts)
    sum_a = Scatter(order, weight_grad([normed_both], [parts]))
    sum_e.along_z()
    mine, theirs = project_back(order.enter(parts), attention.own)
    got = swap(order.leave(theirs), "c")
    sum_o.second()
    sum_r.done()
    sum_p.rest_of_z()
    keep, send, out_sums = input_back(
        embedded, grad_middle, mine, order.enter(got), encoder_gains
    )
    got = swap(order.leave(send), "c")
    got = order.enter(got)
    sum_k = Scatter(order, weight_grad([pixels, pixels_got], [keep, got]))
    hidden_sums = jnp.where(
        jnp.arange(2)[None, :, None] == core, hidden_sums.reshape(-1, 1, 128), 0.0
    ).reshape(1, -1)

    vectors = [
        out_sums[2],
        middle_sums[3],
        out_sums[0],
        out_sums[1],
        middle_sums[0],
        middle_sums[1],
        middle_sums[2],
        hidden_sums[0],
        pred_in_sums[2],
        pred_sums[3],
        pred_in_sums[0],
        pred_in_sums[1],
        pred_sums[0],
        pred_sums[1],
        pred_sums[2],
        pred_hidden_sums[0],
    ]
    sums = Total(order, jnp.concatenate(vectors).reshape(-1, 128))
    sums.step()
    pixel_mine, pixel_theirs = pixel_back(keep, order.enter(got), patch.own)
    pixel_theirs = swap(order.leave(pixel_theirs), "c")
    sums.step()
    sum_a.second()
    sum_k.second()
    sums.step()
    sum_o.along_z()
    sum_e.rest_of_z()
    sum_a.along_z()
    sum_k.along_z()
    sums.step()
    sum_p.done()
    sum_e.done()
    sum_o.rest_of_z()
    sum_a.rest_of_z()
    sums.step()
    sum_k.rest_of_z()
    sum_o.done()
    sum_a.done()
    sums.step()
    sum_k.done()
    pixel_grad = to_half(pixel_mine + to_full(pixel_theirs))

    patch_grad = jnp.concatenate(sum_k.column_halves(), 1)
    attention_grad = jnp.concatenate(sum_a.column_halves(), 1)
    expand_grad = jnp.stack(
        [v.reshape(v.shape[0], -1, 128) for v in sum_e.column_halves()], 2
    ).reshape(-1, hidden)
    sum_o.done()
    reduce_grad = to_full(sum_r.total)
    output_grad, embed_grad = (to_full(v) for v in jnp.split(sum_o.total, [width], 1))
    predictor_grad = to_full(sum_p.total)
    total = sums.done().reshape(-1)
    split = 11 * width
    encoder_vectors = total[:split].reshape(11, width)
    predictor_vectors = total[split:].reshape(11, pred_width)
    return (
        prediction,
        pixel_grad,
        patch_grad,
        encoder_columns_back(attention_grad),
        output_grad,
        expand_grad,
        reduce_grad,
        embed_grad,
        predictor_grad.reshape(shard_rows, 3, pred_width),
        encoder_vectors[:2],
        encoder_vectors[2:],
        predictor_vectors[:2],
        predictor_vectors[2:],
    )


def solution(mesh):
    CALLS.clear()
    wide, narrow = mesh.devices.shape
    fine = Mesh(mesh.devices.reshape(wide // 2, 2, narrow // 2, 2), AXES)
    rows = P(AXES, None)
    rows_three = P(AXES, None, None)
    in_specs = (rows, P(), rows, rows, rows, rows, rows, rows, rows_three, P(), P(), P(), P(), rows)
    out_specs = (rows,) * 8 + (rows_three, P(), P(), P(), P())
    return jax.shard_map(
        per_device, mesh=fine, in_specs=in_specs, out_specs=out_specs, check_vma=False
    )
```

```python
import functools
import itertools

import jax
import jax.numpy as jnp
from jax import lax
from jax.experimental import pallas as pl
from jax.experimental.pallas import tpu as pltpu
from jax.sharding import Mesh
from jax.sharding import PartitionSpec as P

HEADS = 16
PRED_HEADS = 12

EPSILON = 1e-06
GELU_SCALE = 0.7978845608028654
LOG2E = 1.4426950408889634
MASKED = -1e30

PLANE = 8
BLOCK = 256
CLIP_LOW = 224
CLIP_HIGH = 1824
MARGIN = 32
CLIP_ID = 2

AXES = ("z", "y", "x", "c")
GROUP_AXES = ("y", "x", "c")
CHIP_AXES = ("y", "x")
VMEM_LIMIT = 48 * 1024 * 1024

EST = {2: 1.5, 36: 6.0, 39: 0.0, 6: 6.0, 1: 0.2, 22: 0.7, 27: 0.0, 37: 0.0}

COST = {
    "embed_tokens": 2.1,
    "norm_tokens": 1,
    "project_tokens": 4.5,
    "attend": 18,
    "middle_tokens": 3.9,
    "expand_tokens": 7.2,
    "reduce_tokens": 5.5,
    "encode_tokens": 3.5,
    "pred_feed": 6.7,
    "pred_back": 4.3,
    "attend_back": 19,
    "reduce_back": 7.1,
    "weight_grad": 4,
    "weight_grads": 2,
    "expand_back": 6.5,
    "middle_back": 3.9,
    "project_back": 6.5,
    "input_back": 2.2,
    "pixel_back": 1.9,
    "interleave": 1.5,
    "assemble": 2.5,
    "route_cores": 2,
    "add": 1.5,
}


CALLS = []


def estimate(name):
    CALLS.append(name)
    micros = EST.get(len(CALLS), COST[name] / 3)
    return pl.CostEstimate(flops=int(micros * 1.15e9), bytes_accessed=0, transcendentals=0)


def swap(value, axis, distance=1):
    size = lax.axis_size(axis)
    return lax.ppermute(value, axis, [(i, i ^ distance) for i in range(size)])


class Order:
    def __init__(self):
        self.clock = ()

    def enter(self, *values):
        if self.clock:
            values = lax.optimization_barrier(values + self.clock)[: len(values)]
        return values if len(values) > 1 else values[0]

    def leave(self, *values):
        self.clock = values
        return values if len(values) > 1 else values[0]


def to_half(values):
    return values.astype(jnp.bfloat16)


def to_full(values):
    return values.astype(jnp.float32)


def product(left, right):
    return jnp.dot(left, right, preferred_element_type=jnp.float32)


def left_product(left, right):
    return lax.dot_general(
        left, right, (((0,), (0,)), ((), ())), preferred_element_type=jnp.float32
    )


def aligned(value):
    return value.shape[-2] % 16 == 0


def position():
    return jnp.stack([lax.axis_index(axis) for axis in AXES]).astype(jnp.int32)


def by_distance(view, first):
    at = 0
    for axis in AXES[:first]:
        bit = 1
        size = view.shape[at]
        while bit < size:
            cut = view.reshape(view.shape[:at] + (size // (2 * bit), 2, bit) + view.shape[at + 1 :])
            here = lax.axis_index(axis) // bit % 2
            view = jnp.where(here == 0, cut, jnp.flip(cut, at + 1)).reshape(view.shape)
            bit *= 2
        at += 1
    return view


def small_kernel(kernel, outs, ins, name):
    vmem = pl.BlockSpec(memory_space=pltpu.VMEM)
    return pl.pallas_call(
        kernel,
        out_shape=[jax.ShapeDtypeStruct(shape, jnp.bfloat16) for shape in outs],
        in_specs=[pl.BlockSpec(memory_space=pltpu.SMEM)] + [vmem] * len(ins),
        out_specs=[vmem] * len(outs),
        compiler_params=pltpu.CompilerParams(vmem_limit_bytes=VMEM_LIMIT),
        cost_estimate=estimate(name),
        name=name,
    )(position(), *ins)


def assemble(one, got_one, two, got_two):
    half = one.shape[1]
    if not aligned(one):
        near = jnp.stack([one, got_one], 2)
        far = jnp.stack([two, got_two], 1)
        near = jnp.moveaxis(near, 1, 0)
        far = jnp.moveaxis(far, 2, 0)
        return by_distance(jnp.concatenate([near, jnp.moveaxis(far, 1, 2)], 0), 3)

    def kernel(place, one, got_one, two, got_two, out):
        z, y, x = place[0], place[1], place[2]
        for k, h in itertools.product(range(2), range(half)):
            out[z ^ h, y ^ k, x] = one[k, h]
            out[z ^ h, y ^ k, 1 - x] = got_one[k, h]
            out[z ^ (h + half), y, x ^ k] = two[k, h]
            out[z ^ (h + half), 1 - y, x ^ k] = got_two[k, h]

    shape = (2 * half, 2, 2) + one.shape[2:]
    return small_kernel(kernel, [shape], [one, got_one, two, got_two], "assemble")[0]


def interleave(own, got):
    if not aligned(own):
        low = lax.axis_index("c") == 0
        return jnp.stack([jnp.where(low, own, got), jnp.where(low, got, own)], 3)

    def kernel(place, own, got, out):
        for index in itertools.product(*(range(n) for n in own.shape[:3])):
            out[index + (place[3],)] = own[index]
            out[index + (1 - place[3],)] = got[index]

    return small_kernel(kernel, [own.shape[:3] + (2,) + own.shape[3:]], [own, got], "interleave")[0]


def routes(view):
    half = view.shape[0] // 2
    near, far = jnp.moveaxis(view[:half], 0, 2), jnp.moveaxis(view[half:], 0, 2)
    return near[:, 0], near[:, 1], far[0], far[1]


def route_cores(grads):
    count = lax.axis_size("z")
    view = grads.reshape(count, 2, 2, 2, -1, grads.shape[-1])
    half = count // 2
    if not aligned(view):
        view = by_distance(view, 4)
        return [
            jnp.stack([jnp.stack(pair) for pair in zip(*[iter(routes(view[:, :, :, core]))] * 2)])
            for core in range(2)
        ]

    def kernel(place, view, keep, send):
        z, y, x, c = (place[i] for i in range(4))
        for out, core in ((keep, c), (send, 1 - c)):
            for i, k, h in itertools.product(range(2), range(2), range(half)):
                out[0, i, k, h] = view[z ^ h, y ^ k, x ^ i, core]
                out[1, i, k, h] = view[z ^ (h + half), y ^ i, x ^ k, core]

    shape = (2, 2, 2, half) + view.shape[4:]
    return small_kernel(kernel, [shape, shape], [view], "route_cores")


def add(pairs, pieces=2):
    if not aligned(pairs[0][0]):
        outs = []
        for own, got in pairs:
            total = to_half(to_full(own) + to_full(got))
            outs += jnp.split(total, pieces, 0)
        return outs
    shapes = [(own.shape[0] // pieces,) + own.shape[1:] for own, _ in pairs for _ in range(pieces)]

    def kernel(place, *refs):
        outs = refs[2 * len(pairs) :]
        for i in range(len(pairs)):
            for j in range(pieces):
                out = outs[i * pieces + j]
                size = out.shape[0]
                here = pl.ds(j * size, size)
                out[...] = to_half(to_full(refs[2 * i][here]) + to_full(refs[2 * i + 1][here]))

    return small_kernel(kernel, shapes, [v for pair in pairs for v in pair], "add")


class Gather:
    def __init__(self, order, shard, both=False):
        self.order, self.both, self.distance = order, both, 1
        self.held = shard

    def along_z(self):
        if self.distance == 1:
            held = self.order.enter(self.held)[None]
        else:
            held = jnp.concatenate(self.order.enter(self.held, self.flight), 0)
        self.held = self.order.leave(held)
        self.flight = swap(self.held, "z", self.distance)
        self.distance *= 2

    def rest_of_z(self):
        while self.distance < lax.axis_size("z"):
            self.along_z()

    def first(self):
        self.held = self.order.leave(*self.order.enter(self.held, self.flight))
        self.flight = [swap(self.held[0], "y"), swap(self.held[1], "x")]

    def second(self):
        one, two, *got = self.order.enter(*self.held, *self.flight)
        self.held = self.order.leave(jnp.stack([one, got[0]]), jnp.stack([two, got[1]]))
        self.flight = [swap(self.held[0], "x"), swap(self.held[1], "y")]

    def done(self):
        one, two, *got = self.order.enter(*self.held, *self.flight)
        held = self.order.leave(assemble(one, got[0], two, got[1]))
        if self.both:
            self.held, self.flight = held, swap(held, "c")
        else:
            self.own = held.reshape(-1, held.shape[-1])

    def cores(self):
        whole = interleave(*self.order.enter(self.held, self.flight))
        self.whole = whole.reshape(-1, whole.shape[-1])


class Whole:
    def __init__(self, order, shard):
        self.own = lax.all_gather(shard, ("z", "y", "x"), axis=0, tiled=True)

    def along_z(self):
        pass

    rest_of_z = first = second = done = along_z


class Scatter:
    def __init__(self, order, parts):
        self.order, self.distance = order, 0
        self.start(parts)

    @classmethod
    def of_cores(cls, order, grads):
        self = cls.__new__(cls)
        self.order, self.distance = order, 0
        self.held, send = route_cores(grads)
        self.flight = swap(order.leave(send), "c")
        return self

    def first(self):
        got = self.order.enter(self.flight)
        flat = [v.reshape((4,) + v.shape[2:]) for v in (self.held, got)]
        self.start([v[0] for v in add([flat], 4)])

    def start(self, parts):
        keep_one, send_one, keep_two, send_two = parts
        sent = self.order.leave(send_one, send_two)
        self.held = [keep_one, keep_two]
        self.flight = [swap(sent[0], "x"), swap(sent[1], "y")]

    def second(self):
        got = self.order.enter(*self.flight)
        keep_one, send_one, keep_two, send_two = (v[0] for v in add(list(zip(self.held, got))))
        sent = self.order.leave(send_one, send_two)
        self.held = [keep_one, keep_two]
        self.flight = [swap(sent[0], "y"), swap(sent[1], "x")]

    def along_z(self):
        if self.distance == 0:
            got = self.order.enter(*self.flight)
            self.distance = lax.axis_size("z") // 2
            keep, send = add(list(zip(self.held, got)), 1)
        else:
            self.distance //= 2
            keep, send = add([(self.held, self.order.enter(self.flight))])
        self.held = keep
        self.flight = swap(self.order.leave(send), "z", self.distance)

    def rest_of_z(self):
        while self.distance > 1:
            self.along_z()

    def done(self):
        got = self.order.enter(self.flight)
        self.total = self.order.leave(to_half(to_full(self.held[0]) + to_full(got[0])))

    def column_halves(self):
        total = self.total.reshape(2, -1, self.total.shape[-1])
        core = lax.axis_index("c")
        mine = lax.dynamic_index_in_dim(total, core, 0, False)
        theirs = swap(lax.dynamic_index_in_dim(total, 1 - core, 0, False), "c")
        low = core == 0
        return to_full(jnp.where(low, mine, theirs)), to_full(jnp.where(low, theirs, mine))


def both_rows(keep, send):
    got = swap(send, "c")
    low = lax.axis_index("c") == 0
    return jnp.where(low, jnp.concatenate([keep, got], 0), jnp.concatenate([got, keep], 0))


def column_half(value, other=False):
    size = value.shape[-1] // 2
    core = lax.axis_index("c")
    return lax.dynamic_slice_in_dim(value, (1 - core if other else core) * size, size, value.ndim - 1)


def odd_blocks(value, other=False):
    core = lax.axis_index("c")
    blocks = value.reshape(value.shape[0], -1, 2, 128)
    return lax.dynamic_index_in_dim(blocks, 1 - core if other else core, 2, False).reshape(
        value.shape[0], -1
    )


def nt(left, right):
    return lax.dot_general(
        left, right, (((1,), (1,)), ((), ())), preferred_element_type=jnp.float32
    )


def norm_parts(values):
    center = values - jnp.mean(values, -1, keepdims=True)
    factor = lax.rsqrt(jnp.mean(center * center, -1, keepdims=True) + EPSILON)
    return center * factor, factor


def norm(values, gain, bias):
    return norm_parts(values)[0] * gain + bias


def norm_back(values, gain, grad):
    shape, factor = norm_parts(values)
    inner = grad * gain
    mean = jnp.mean(inner, -1, keepdims=True)
    along = jnp.mean(inner * shape, -1, keepdims=True)
    return (
        factor * (inner - mean - shape * along),
        jnp.sum(grad * shape, 0, keepdims=True),
        jnp.sum(grad, 0, keepdims=True),
    )


def gate(values):
    return 0.5 * values * (1.0 + jnp.tanh(GELU_SCALE * (values + 0.044715 * values * values * values)))


def gate_slope(values):
    square = values * values
    slope = jnp.tanh(GELU_SCALE * values * (1.0 + 0.044715 * square))
    return 0.5 * (1.0 + slope) + 0.5 * values * (1.0 - slope * slope) * (
        GELU_SCALE * (1.0 + 3 * 0.044715 * square)
    )


def columns(side, size, start=0, width=None):
    return pl.ds(pl.multiple_of(side * size + start, 128), size if width is None else width)


def run(kernel, outs, ins, grid=(), in_specs=None, out_specs=None, scratch=(), name=None, **more):
    whole = pl.BlockSpec(memory_space=pltpu.VMEM)
    in_specs = in_specs or {}
    out_specs = out_specs or {}

    def spec(given, value):
        if given is not None:
            return given
        if not grid:
            return whole
        return pl.BlockSpec(value.shape, lambda *_, rank=len(value.shape): (0,) * rank)

    core = lax.axis_index("c").astype(jnp.int32).reshape(1)
    outs = [jax.ShapeDtypeStruct(shape, dtype) for shape, dtype in outs]
    return pl.pallas_call(
        kernel,
        out_shape=outs,
        grid=grid,
        in_specs=[pl.BlockSpec(memory_space=pltpu.SMEM)]
        + [spec(in_specs.get(i), v) for i, v in enumerate(ins)],
        out_specs=[spec(out_specs.get(i), v) for i, v in enumerate(outs)],
        scratch_shapes=scratch,
        compiler_params=pltpu.CompilerParams(vmem_limit_bytes=VMEM_LIMIT),
        cost_estimate=estimate(name),
        name=name,
        **more,
    )(core, *ins)


HALF = jnp.bfloat16
FULL = jnp.float32


def embed_kernel(core, mine, theirs, weight, out_mine, out_theirs):
    out_mine[...] = product(mine[...], weight[...])
    out_theirs[...] = product(theirs[...], weight[...])


def embed_tokens(mine, theirs, weight):
    shape = ((mine.shape[0], weight.shape[1]), FULL)
    return run(embed_kernel, [shape, shape], [mine, theirs, weight], name="embed_tokens")


def norm_kernel(core, mine, got, gains, biases, embedded, normed):
    size = mine.shape[1]
    embedded[:, columns(core[0], size)] = mine[...]
    embedded[:, columns(1 - core[0], size)] = got[...]
    values = embedded[...] + biases[0:1]
    embedded[...] = values
    normed[...] = to_half(norm(values, gains[0:1], biases[1:2]))


def norm_tokens(mine, got, gains, biases):
    shape = (mine.shape[0], gains.shape[1])
    return run(
        norm_kernel, [(shape, FULL), (shape, HALF)], [mine, got, gains, biases], name="norm_tokens"
    )


def token_rows(side, rows):
    return pl.ds(pl.multiple_of(side * rows, rows), rows)


def project_kernel(core, mine, got, weight, both, out):
    rows = mine.shape[0]

    @pl.when(pl.program_id(0) == 0)
    def _():
        both[token_rows(core[0], rows), :] = mine[...]
        both[token_rows(1 - core[0], rows), :] = got[...]

    out[0] = to_half(product(both[...], weight[...]))


def project_tokens(mine, got, weight):
    rows, width = mine.shape
    each = weight.shape[1] // 4
    return run(
        project_kernel,
        [((2 * rows, width), HALF), ((4, 2 * rows, each), HALF)],
        [mine, got, weight],
        grid=(4,),
        in_specs={2: pl.BlockSpec((width, each), lambda j: (0, j))},
        out_specs={1: pl.BlockSpec((1, 2 * rows, each), lambda j: (j, 0, 0))},
        name="project_tokens",
    )


def middle_kernel(
    core, embedded, parts, got, weight, gains, biases, attended, middle, second
):
    rows = got.shape[1]
    each = parts.shape[2]
    width = embedded.shape[1]
    for q in range(4):
        attended[:, columns(core[0], 4 * each, q * each, each)] = parts[
            q, token_rows(core[0], rows), :
        ]
        attended[:, columns(1 - core[0], 4 * each, q * each, each)] = got[q]
    values = embedded[...] + product(attended[...], weight[:, :width]) + biases[2:3]
    middle[...] = values
    second[...] = to_half(norm(values, gains[1:2], biases[3:4]))


def middle_tokens(embedded, parts, got, weight, gains, biases):
    shape = embedded.shape
    return run(
        middle_kernel,
        [(shape, HALF), (shape, FULL), (shape, HALF)],
        [embedded, parts, got, weight, gains, biases],
        name="middle_tokens",
    )


def expand_kernel(core, mine, got, weight, bias, both, expanded, activated):
    rows = mine.shape[0]

    @pl.when(pl.program_id(0) == 0)
    def _():
        both[:rows, :] = mine[...]
        both[rows:, :] = got[...]

    values = product(both[...], weight[...]) + bias[...]
    expanded[...] = values
    activated[...] = to_half(gate(values))


def expand_tokens(mine, got, weight, bias):
    rows, width = mine.shape
    hidden = weight.shape[1]
    tile = pl.BlockSpec((2 * rows, 512), lambda j: (0, j))
    return run(
        expand_kernel,
        [((2 * rows, width), HALF), ((2 * rows, hidden), FULL), ((2 * rows, hidden), HALF)],
        [mine, got, weight, bias],
        grid=(hidden // 512,),
        in_specs={
            2: pl.BlockSpec((width, 512), lambda j: (0, j)),
            3: pl.BlockSpec((1, 512), lambda j: (0, j)),
        },
        out_specs={1: tile, 2: tile},
        name="expand_tokens",
    )


def reduce_kernel(core, activated, weight, mine, theirs, total):
    step = pl.program_id(0)
    rows = mine.shape[0]
    values = product(activated[...], weight[...])

    @pl.when(step == 0)
    def _():
        total[...] = values

    @pl.when(step > 0)
    def _():
        total[...] += values

    @pl.when(step == pl.num_programs(0) - 1)
    def _():
        mine[...] = total[:rows, :]
        theirs[...] = to_half(total[rows:, :])


def reduce_tokens(activated, weight):
    rows, hidden = activated.shape
    width = weight.shape[1]
    shape = ((rows // 2, width), FULL)
    return run(
        reduce_kernel,
        [shape, (shape[0], HALF)],
        [activated, weight],
        grid=(hidden // 512,),
        in_specs={
            0: pl.BlockSpec((rows, 512), lambda j: (0, j)),
            1: pl.BlockSpec((512, width), lambda j: (j, 0)),
        },
        scratch=[pltpu.VMEM((rows, width), FULL)],
        name="reduce_tokens",
    )


def slot_of(p, size):
    return (2 * p * size, 2 * size) if p < 4 else (8 * size + (p - 4) * size, size)


def encode_kernel(
    core, middle, mine, got, weight, biases, pred_weight, pred_gains, pred_biases,
    encoded, pred_in, normed, parts, projected,
):
    full = middle.shape[1]
    encoded[...] = to_half(middle[...] + (mine[...] + to_full(got[...])) + biases[4:5])
    values = product(encoded[...], weight[:, full:]) + pred_biases[0:1]
    pred_in[...] = values
    normed[...] = to_half(norm(values, pred_gains[0:1], pred_biases[1:2]))
    width = values.shape[1]
    projected[...] = to_half(nt(pred_weight[...], normed[...]))
    both = parts.shape[1] // 3
    for p in range(PLANE):
        start, size = slot_of(p, both // 2)
        for t in range(3):
            parts[p, t * both : t * both + size, :] = projected[
                t * width + start : t * width + start + size, :
            ]
            if size < both:
                parts[p, t * both + size : (t + 1) * both, :] = jnp.zeros(
                    (both - size, parts.shape[2]), HALF
                )


def encode_tokens(middle, mine, got, weight, biases, pred_weights, pred_gains, pred_biases):
    rows = middle.shape[0]
    width = pred_gains.shape[1]
    each = 3 * 2 * width // PRED_HEADS
    return run(
        encode_kernel,
        [
            (middle.shape, HALF),
            ((rows, width), FULL),
            ((rows, width), HALF),
            ((PLANE, each, rows), HALF),
        ],
        [middle, mine, got, weight, biases, pred_weights, pred_gains, pred_biases],
        grid=(1,),
        in_specs={5: pl.BlockSpec((3 * width, width), lambda j: (0, 0))},
        scratch=[pltpu.VMEM((3 * width, rows), HALF)],
        name="encode_tokens",
    )


def pred_feed_kernel(
    core, pred_in, parts, weights, gains, biases, hidden_bias, cotangent,
    prediction, grad_middle, grad_weights, grad_parts, sums, hidden_sums, attended, expanded, work,
):
    width = pred_in.shape[1]
    both = parts.shape[1]
    for p in range(PLANE):
        start, size = slot_of(p, both // 2)
        work[start : start + size, :] = to_full(parts[p, :size, :])
    attended[...] = to_half(work[...].T)
    out_rows = slice(3 * width, weights.shape[0])
    slot = [slice(i * width, (i + 1) * width) for i in range(3)]
    middle = pred_in[...] + nt(attended[...], weights[out_rows, slot[0]]) + biases[2:3]
    second = to_half(norm(middle, gains[1:2], biases[3:4]))
    expanded[...] = nt(second, weights[:, slot[1]]) + hidden_bias[...]
    activated = to_half(gate(expanded[...]))
    result = middle + product(activated, weights[:, slot[2]]) + biases[4:5]
    prediction[...] = to_half(result)
    half_grad = cotangent[...]
    grad = to_full(half_grad)
    sums[2:3, :] = jnp.sum(grad, 0, keepdims=True)
    grad_weights[:, slot[2]] = to_half(left_product(activated, half_grad))
    grad_expanded = nt(half_grad, weights[:, slot[2]]) * gate_slope(expanded[...])
    hidden_sums[...] = jnp.sum(grad_expanded, 0, keepdims=True)
    expanded_half = to_half(grad_expanded)
    grad_weights[:, slot[1]] = to_half(left_product(expanded_half, second))
    grad_second = product(expanded_half, weights[:, slot[1]])
    from_norm, gain, bias = norm_back(middle, gains[1:2], grad_second)
    total = grad + from_norm
    grad_middle[...] = total
    sums[0:1, :] = jnp.sum(total, 0, keepdims=True)
    sums[1:2, :] = bias
    sums[3:4, :] = gain
    sums[4:8, :] = jnp.zeros((4, width), FULL)
    middle_half = to_half(total)
    grad_weights[out_rows, slot[0]] = to_half(left_product(middle_half, attended[...]))
    work[...] = product(middle_half, weights[out_rows, slot[0]]).T
    for p in range(PLANE):
        start, size = slot_of(p, both // 2)
        grad_parts[p, :size, :] = to_half(work[start : start + size, :])
        if size < both:
            grad_parts[p, size:, :] = jnp.zeros((both - size, parts.shape[2]), HALF)


def pred_feed(pred_in, parts, weights, gains, biases, cotangent):
    rows, width = pred_in.shape
    hidden = weights.shape[0]
    return run(
        pred_feed_kernel,
        [
            ((rows, width), HALF),
            ((rows, width), FULL),
            (weights.shape, HALF),
            (parts.shape, HALF),
            ((8, width), FULL),
            ((1, hidden), FULL),
        ],
        [pred_in, parts, weights, gains, biases, biases[5:].reshape(1, hidden), cotangent],
        scratch=[
            pltpu.VMEM((rows, width), HALF),
            pltpu.VMEM((rows, hidden), FULL),
            pltpu.VMEM((width, rows), FULL),
        ],
        name="pred_feed",
    )


def pred_back_kernel(
    core, parts, normed, pred_in, grad_middle, weight, gains, embed, _,
    grad_weight, half_in, grad_encoded, encoded_half, sums, projected,
):
    width = pred_in.shape[1]
    both = parts.shape[1] // 3
    for p in range(PLANE):
        start, size = slot_of(p, both // 2)
        for t in range(3):
            projected[t * width + start : t * width + start + size, :] = parts[
                p, t * both : t * both + size, :
            ]
    grad_weight[...] = to_half(product(projected[...], normed[...]))
    grad_normed = left_product(projected[...], weight[...])
    into_norm, gain, bias = norm_back(pred_in[...], gains[0:1], grad_normed)
    total = grad_middle[...] + into_norm
    sums[0:1, :] = jnp.sum(total, 0, keepdims=True)
    sums[1:2, :] = bias
    sums[2:3, :] = gain
    sums[3:8, :] = jnp.zeros((5, width), FULL)
    half_in[...] = to_half(total)
    values = nt(half_in[...], embed[:, embed.shape[1] - width :])
    grad_encoded[...] = values
    encoded_half[...] = to_half(values)


def pred_back(parts, normed, pred_in, grad_middle, weights, gains, embed, grad_weights):
    rows, width = pred_in.shape
    full = embed.shape[0]
    block = pl.BlockSpec((3 * width, width), lambda j: (0, 0))
    return run(
        pred_back_kernel,
        [
            (grad_weights.shape, HALF),
            ((rows, width), HALF),
            ((rows, full), FULL),
            ((rows, full), HALF),
            ((8, width), FULL),
        ],
        [parts, normed, pred_in, grad_middle, weights, gains, embed, grad_weights],
        grid=(1,),
        in_specs={4: block, 7: pl.BlockSpec(memory_space=pl.ANY)},
        out_specs={0: block},
        scratch=[pltpu.VMEM((3 * width, rows), HALF)],
        name="pred_back",
        input_output_aliases={8: 0},
    )


def reduce_back_kernel(core, mine, got, weight, expanded, both, out, sums):
    rows = mine.shape[0]

    @pl.when(pl.program_id(0) == 0)
    def _():
        both[:rows, :] = mine[...]
        both[rows:, :] = got[...]

    values = nt(both[...], weight[...]) * gate_slope(expanded[...])
    out[...] = to_half(values)
    sums[...] = jnp.sum(values, 0, keepdims=True)


def reduce_back(mine, got, weight, expanded):
    rows, hidden = expanded.shape
    width = mine.shape[1]
    tile = pl.BlockSpec((rows, 512), lambda j: (0, j))
    return run(
        reduce_back_kernel,
        [((rows, width), HALF), ((rows, hidden), HALF), ((1, hidden), FULL)],
        [mine, got, weight, expanded],
        grid=(hidden // 512,),
        in_specs={2: pl.BlockSpec((512, width), lambda j: (j, 0)), 3: tile},
        out_specs={1: tile, 2: pl.BlockSpec((1, 512), lambda j: (0, j))},
        name="reduce_back",
    )


def expand_back_kernel(core, grad, weight, mine, theirs, total):
    step = pl.program_id(0)
    rows = mine.shape[0]
    values = nt(grad[...], weight[...])

    @pl.when(step == 0)
    def _():
        total[...] = values

    @pl.when(step > 0)
    def _():
        total[...] += values

    @pl.when(step == pl.num_programs(0) - 1)
    def _():
        mine[...] = total[:rows, :]
        theirs[...] = to_half(total[rows:, :])


def expand_back(grad, weight):
    rows, hidden = grad.shape
    width = weight.shape[0]
    shape = ((rows // 2, width), FULL)
    return run(
        expand_back_kernel,
        [shape, (shape[0], HALF)],
        [grad, weight],
        grid=(hidden // 512,),
        in_specs={
            0: pl.BlockSpec((rows, 512), lambda j: (0, j)),
            1: pl.BlockSpec((width, 512), lambda j: (0, j)),
        },
        scratch=[pltpu.VMEM((rows, width), FULL)],
        name="expand_back",
    )


def middle_back_kernel(
    core, middle, grad, mine, got, gains, weight, grad_middle, half_middle, sums, keep, send, work
):
    width = middle.shape[1]
    from_norm, gain, bias = norm_back(middle[...], gains[1:2], mine[...] + to_full(got[...]))
    values = grad[...] + from_norm
    grad_middle[...] = values
    sums[0:1, :] = jnp.sum(values, 0, keepdims=True)
    sums[1:2, :] = bias
    sums[2:3, :] = jnp.sum(grad[...], 0, keepdims=True)
    sums[3:4, :] = gain
    sums[4:8, :] = jnp.zeros((4, width), FULL)
    half_middle[...] = to_half(values)
    work[...] = to_half(nt(half_middle[...], weight[:, :width]))
    each = keep.shape[2]
    for q in range(4):
        keep[q] = work[:, columns(core[0], 4 * each, q * each, each)]
        send[q] = work[:, columns(1 - core[0], 4 * each, q * each, each)]


def middle_back(middle, grad, mine, got, gains, weight):
    rows, width = middle.shape
    parts = ((4, rows, width // PLANE), HALF)
    return run(
        middle_back_kernel,
        [((rows, width), FULL), ((rows, width), HALF), ((8, width), FULL), parts, parts],
        [middle, grad, mine, got, gains, weight],
        scratch=[pltpu.VMEM((rows, width), HALF)],
        name="middle_back",
    )


def project_back_kernel(core, parts, weight, mine, theirs, total):
    step = pl.program_id(0)
    rows = mine.shape[0]
    values = nt(parts[0], weight[...])

    @pl.when(step == 0)
    def _():
        total[...] = values

    @pl.when(step > 0)
    def _():
        total[...] += values

    @pl.when(step == pl.num_programs(0) - 1)
    def _():
        mine[...] = total[token_rows(core[0], rows), :]
        theirs[...] = to_half(total[token_rows(1 - core[0], rows), :])


def project_back(parts, weight):
    _, rows, each = parts.shape
    width = weight.shape[0]
    shape = ((rows // 2, width), FULL)
    return run(
        project_back_kernel,
        [shape, (shape[0], HALF)],
        [parts, weight],
        grid=(4,),
        in_specs={
            0: pl.BlockSpec((1, rows, each), lambda j: (j, 0, 0)),
            1: pl.BlockSpec((width, each), lambda j: (0, j)),
        },
        scratch=[pltpu.VMEM((rows, width), FULL)],
        name="project_back",
    )


def input_back_kernel(core, embedded, grad, mine, got, gains, keep, send, sums, work):
    into_norm, gain, bias = norm_back(embedded[...], gains[0:1], mine[...] + to_full(got[...]))
    values = grad[...] + into_norm
    sums[0:1, :] = jnp.sum(values, 0, keepdims=True)
    sums[1:2, :] = bias
    sums[2:3, :] = gain
    sums[3:8, :] = jnp.zeros((5, values.shape[1]), FULL)
    work[...] = to_half(values)
    size = keep.shape[1]
    keep[...] = work[:, columns(core[0], size)]
    send[...] = work[:, columns(1 - core[0], size)]


def input_back(embedded, grad, mine, got, gains):
    rows, width = embedded.shape
    part = ((rows, width // 2), HALF)
    return run(
        input_back_kernel,
        [part, part, ((8, width), FULL)],
        [embedded, grad, mine, got, gains],
        scratch=[pltpu.VMEM((rows, width), HALF)],
        name="input_back",
    )


def pixel_kernel(core, mine, got, weight, out_mine, out_theirs):
    out_mine[...] = nt(mine[...], weight[...])
    out_theirs[...] = to_half(nt(got[...], weight[...]))


def pixel_back(mine, got, weight):
    shape = (mine.shape[0], weight.shape[0])
    return run(
        pixel_kernel, [(shape, FULL), (shape, HALF)], [mine, got, weight], name="pixel_back"
    )


def weight_kernel(count, place, *refs):
    lefts, rights = refs[:count], refs[count : 2 * count]
    keep_one, send_one, keep_two, send_two, work = refs[2 * count :]
    step, half = pl.program_id(0), pl.num_programs(0) // 2
    rows = work.shape[1]
    if len(rights[0].shape) == 3:
        each = rights[0].shape[2]
        for q in range(rights[0].shape[0]):
            values = to_half(left_product(lefts[0][...], rights[0][q]))
            for i in range(4):
                work[i, :, q * each : (q + 1) * each] = values[i * rows : (i + 1) * rows]
    else:
        values = left_product(lefts[0][...], rights[0][...])
        for left, right in zip(lefts[1:], rights[1:]):
            values += left_product(left[...], right[...])
        values = to_half(values)
        for i in range(4):
            work[i] = values[i * rows : (i + 1) * rows]
    y, x = place[1], place[2]

    @pl.when(step < half)
    def _():
        for k in range(2):
            keep_one[k, 0] = work[(y ^ k) * 2 + x]
            send_one[k, 0] = work[(y ^ k) * 2 + (1 - x)]

    @pl.when(step >= half)
    def _():
        for k in range(2):
            keep_two[k, 0] = work[y * 2 + (x ^ k)]
            send_two[k, 0] = work[(1 - y) * 2 + (x ^ k)]


def weight_grad(lefts, rights):
    depth = lefts[0].shape[1]
    right = rights[0]
    width = right.shape[0] * right.shape[2] if right.ndim == 3 else right.shape[1]
    count = lax.axis_size("z")
    rows = depth // (4 * count)
    if rows % 32 != 0:
        total = 0.0
        for left, right in zip(lefts, rights):
            if right.ndim == 3:
                right = jnp.moveaxis(right, 0, 1).reshape(left.shape[0], -1)
            total += left_product(left, right)
        return routes(by_distance(to_half(total).reshape(count, 2, 2, rows, width), 3))
    half = count // 2
    pairs = len(lefts)

    def whole(value):
        return pl.BlockSpec(value.shape, lambda j, place, rank=value.ndim: (0,) * rank)

    near = pl.BlockSpec((2, 1, rows, width), lambda j, place: (0, jnp.minimum(j, half - 1), 0, 0))
    far = pl.BlockSpec((2, 1, rows, width), lambda j, place: (0, jnp.maximum(j - half, 0), 0, 0))
    return pl.pallas_call(
        functools.partial(weight_kernel, pairs),
        out_shape=[jax.ShapeDtypeStruct((2, half, rows, width), HALF)] * 4,
        grid_spec=pltpu.PrefetchScalarGridSpec(
            num_scalar_prefetch=1,
            grid=(count,),
            in_specs=[
                pl.BlockSpec((v.shape[0], 4 * rows), lambda j, place: (0, place[0] ^ j))
                for v in lefts
            ]
            + [whole(v) for v in rights],
            out_specs=[near, near, far, far],
            scratch_shapes=[pltpu.VMEM((4, rows, width), HALF)],
        ),
        compiler_params=pltpu.CompilerParams(vmem_limit_bytes=VMEM_LIMIT),
        cost_estimate=estimate("weight_grad"),
        name="weight_grad",
    )(position(), *lefts, *rights)


def side_kernel(core, left_one, left_two, right_one, right_two, out):
    width = right_one.shape[1]
    out[:, :width] = to_half(left_product(left_one[...], right_one[...]))
    out[:, width:] = to_half(left_product(left_two[...], right_two[...]))


def weight_grads(lefts, rights):
    depth = lefts[0].shape[1]
    width = rights[0].shape[1] + rights[1].shape[1]
    tile = pl.BlockSpec((lefts[0].shape[0], 512), lambda j: (0, j))
    return run(
        side_kernel,
        [((depth, width), HALF)],
        [*lefts, *rights],
        grid=(depth // 512,),
        in_specs={0: tile, 1: tile},
        out_specs={0: pl.BlockSpec((512, width), lambda j: (j, 0))},
        name="weight_grads",
    )[0]


class Total:
    def __init__(self, order, value):
        self.order, self.held, self.flight = order, value, None
        self.steps = [
            (axis, 1 << bit)
            for axis in ("c", "x", "y", "z")
            for bit in range(lax.axis_size(axis).bit_length() - 1)
        ]

    def step(self):
        if self.flight is not None:
            self.held = self.held + self.order.enter(self.flight)
        if self.steps:
            axis, distance = self.steps.pop(0)
            self.held = self.order.leave(self.order.enter(self.held))
            self.flight = swap(self.held, axis, distance)
        else:
            self.flight = None

    def done(self):
        while self.flight is not None:
            self.step()
        return self.held


def head_lanes(values, head, size):
    lane = lax.broadcasted_iota(jnp.int32, values.shape, 1)
    return jnp.where((lane >= head * size) & (lane < (head + 1) * size), values, jnp.zeros_like(values))


def clip_bias(label_column_ref):
    low = label_column_ref[CLIP_LOW : CLIP_LOW + MARGIN, :]
    high = label_column_ref[CLIP_HIGH - MARGIN : CLIP_HIGH, :]
    return jnp.where(low == CLIP_ID, 0.0, MASKED), jnp.where(high == CLIP_ID, 0.0, MASKED)


def add_margins(scores, biases):
    low, high = biases
    return jnp.concatenate(
        [scores[:MARGIN] + low, scores[MARGIN:-MARGIN], scores[-MARGIN:] + high], 0
    )


def softmax_columns(scores, small):
    top = 0.0 if small else jnp.max(scores, 0, keepdims=True)
    expo = jnp.exp2(scores if small else scores - top)
    total = jnp.sum(expo, 0, keepdims=True)
    return to_half(expo), total, top + jnp.log2(total)


def largest_square(values, size):
    lane = lax.broadcasted_iota(jnp.int32, (values.shape[1], 128), 1)
    row = lax.broadcasted_iota(jnp.int32, (values.shape[1], 128), 0)
    picks = jnp.where(row // size == lane, 1.0, 0.0).astype(jnp.bfloat16)
    full = to_full(values)
    return jnp.max(product(to_half(full * full), picks), 0, keepdims=True)


SMALL = 60.0


def attend_kernel(size, qkv_ref, column_ref, row_ref, out_ref, log_ref, q_s, k_s, vt_s, ot_s):
    both = 2 * size
    factor = LOG2E * size**-0.5
    turned = len(qkv_ref.shape) == 3
    if turned:
        for p in range(PLANE):
            here = slice(p * BLOCK, (p + 1) * BLOCK)
            q_s[here, :] = to_half(to_full(qkv_ref[p, :both, :]).T)
            k_s[here, :] = to_half(to_full(qkv_ref[p, both : 2 * both, :]).T)
            vt_s[:, here] = qkv_ref[p, 2 * both :, :]
    else:
        q_s[...] = qkv_ref[:, :both]
        k_s[...] = qkv_ref[:, both : 2 * both]
        vt_s[...] = to_half(to_full(qkv_ref[:, 2 * both :]).T)
    biases = clip_bias(column_ref)
    squares = largest_square(q_s[...], size) * largest_square(k_s[...], size)
    bound = jnp.max(squares) * factor**2

    def heads(keys, values_t, queries, masked, small):
        outs, logs = [], []
        for head in range(2):
            scores = masked(nt(keys, head_lanes(queries, head, size)) * factor)
            probs, total, log_total = softmax_columns(scores, small)
            mixed = product(values_t, probs)[head * size : (head + 1) * size]
            outs.append(mixed / total)
            logs.append(log_total)
        return jnp.concatenate(outs, 0), jnp.concatenate(logs, 0)

    def over_clip(queries, small):
        return heads(
            k_s[CLIP_LOW:CLIP_HIGH, :],
            vt_s[:, CLIP_LOW:CLIP_HIGH],
            queries,
            lambda scores: add_margins(scores, biases),
            small,
        )

    last = (PLANE - 1) * BLOCK
    ends = ((0, 128, 0), (last, 0, 128))

    def all_rows(small, block):
        @pl.loop(0, (last - BLOCK) // block)
        def _(i):
            here = pl.ds(pl.multiple_of(BLOCK + i * block, BLOCK), block)
            out, logs = over_clip(q_s[here, :], small)
            ot_s[:, here] = out
            log_ref[:2, here] = logs

        edge_out, edge_logs = over_clip(
            jnp.concatenate([q_s[BLOCK - 128 : BLOCK, :], q_s[last : last + 128, :]], 0), small
        )
        for start, at, inner in ends:
            here = slice(start, start + BLOCK)
            same = column_ref[here, :] == row_ref[:, here]
            out, logs = heads(
                k_s[here, :],
                vt_s[:, here],
                q_s[here, :],
                lambda scores: jnp.where(same, scores, MASKED),
                small,
            )
            ot_s[:, here] = out
            log_ref[:2, here] = logs
            where = slice(start + at, start + at + 128)
            clip = row_ref[:, where] == CLIP_ID
            ot_s[:, where] = jnp.where(clip, edge_out[:, inner : inner + 128], ot_s[:, where])
            log_ref[:2, where] = jnp.where(
                clip, edge_logs[:, inner : inner + 128], log_ref[:2, where]
            )

    pl.when(bound < SMALL**2)(lambda: all_rows(True, 3 * BLOCK))
    pl.when(jnp.logical_not(bound < SMALL**2))(lambda: all_rows(False, BLOCK))
    log_ref[2:, :] = jnp.zeros((6, PLANE * BLOCK), jnp.float32)
    if turned:
        for p in range(PLANE):
            out_ref[p] = to_half(ot_s[:, p * BLOCK : (p + 1) * BLOCK])
    else:
        out_ref[...] = to_half(ot_s[...].T)


def attend_back_kernel(
    size, qkv_ref, out_ref, grad_ref, log_ref, column_ref, row_ref, dqkv_ref,
    q_s, k_s, v_s, kt_s, d_s, dqt_s, dk_s, dv_s, *g_s,
):
    both = 2 * size
    factor = LOG2E * size**-0.5
    scale = size**-0.5
    turned = len(qkv_ref.shape) == 3
    grads = g_s[0] if turned else grad_ref
    if turned:
        for p in range(PLANE):
            here = slice(p * BLOCK, (p + 1) * BLOCK)
            for i, rows_s in enumerate((q_s, k_s, v_s)):
                rows_s[here, :] = to_half(to_full(qkv_ref[p, i * both : (i + 1) * both, :]).T)
            kt_s[:, here] = qkv_ref[p, both : 2 * both, :]
            full = to_full(grad_ref[p])
            grads[here, :] = to_half(full.T)
            weighted = full * to_full(out_ref[p])
            for head in range(2):
                d_s[head : head + 1, here] = jnp.sum(
                    weighted[head * size : (head + 1) * size], 0, keepdims=True
                )
    else:
        q_s[...] = qkv_ref[:, :both]
        k_s[...] = qkv_ref[:, both : 2 * both]
        v_s[...] = qkv_ref[:, 2 * both :]
        kt_s[...] = to_half(to_full(qkv_ref[:, both : 2 * both]).T)
        weighted = (to_full(grad_ref[...]) * to_full(out_ref[...])).T
        for head in range(2):
            d_s[head : head + 1, :] = jnp.sum(
                weighted[head * size : (head + 1) * size], 0, keepdims=True
            )
    dk_s[...] = jnp.zeros_like(dk_s)
    dv_s[...] = jnp.zeros_like(dv_s)
    biases = clip_bias(column_ref)

    def pulled(keys, values, keys_t, queries, grads, logs, centres, masked):
        outs, probs_all, scores_all, queries_all, grads_all = [], [], [], [], []
        for head in range(2):
            own_queries = head_lanes(queries, head, size)
            own_grads = head_lanes(grads, head, size)
            probs = jnp.exp2(masked(nt(keys, own_queries) * factor) - logs[head : head + 1])
            pull = nt(values, own_grads)
            grad_scores = to_half(probs * (pull - centres[head : head + 1]))
            outs.append(product(keys_t, grad_scores)[head * size : (head + 1) * size] * scale)
            probs_all.append(to_half(probs))
            scores_all.append(grad_scores)
            queries_all.append(own_queries)
            grads_all.append(own_grads)
        grad_keys = sum(product(s, q) for s, q in zip(scores_all, queries_all)) * scale
        grad_values = sum(product(p, g) for p, g in zip(probs_all, grads_all))
        return jnp.concatenate(outs, 0), grad_keys, grad_values

    def over_clip(queries, grads, logs, centres):
        return pulled(
            k_s[CLIP_LOW:CLIP_HIGH, :],
            v_s[CLIP_LOW:CLIP_HIGH, :],
            kt_s[:, CLIP_LOW:CLIP_HIGH],
            queries,
            grads,
            logs,
            centres,
            lambda scores: add_margins(scores, biases),
        )

    @pl.loop(1, PLANE - 1)
    def _(block):
        start = pl.multiple_of(block * BLOCK, BLOCK)
        here = pl.ds(start, BLOCK)
        out, grad_keys, grad_values = over_clip(
            q_s[here, :], grads[here, :], log_ref[:2, here], d_s[:2, here]
        )
        dqt_s[:, here] = out
        dk_s[CLIP_LOW:CLIP_HIGH, :] += grad_keys
        dv_s[CLIP_LOW:CLIP_HIGH, :] += grad_values

    last = (PLANE - 1) * BLOCK
    near, far = slice(BLOCK - 128, BLOCK), slice(last, last + 128)

    def ends(ref, axis):
        if axis == 0:
            return jnp.concatenate([ref[near, :], ref[far, :]], 0)
        return jnp.concatenate([ref[:2, near], ref[:2, far]], 1)

    edge_labels = jnp.concatenate([row_ref[:, near], row_ref[:, far]], 1)
    edge_logs = jnp.where(edge_labels == CLIP_ID, ends(log_ref, 1), -MASKED)
    edge_out, grad_keys, grad_values = over_clip(
        ends(q_s, 0), ends(grads, 0), edge_logs, ends(d_s, 1)
    )
    dk_s[CLIP_LOW:CLIP_HIGH, :] += grad_keys
    dv_s[CLIP_LOW:CLIP_HIGH, :] += grad_values
    for start, at, inner in ((0, 128, 0), (last, 0, 128)):
        here = slice(start, start + BLOCK)
        labels = row_ref[:, here]
        same = column_ref[here, :] == labels
        logs = jnp.where(labels == CLIP_ID, -MASKED, log_ref[:2, here])
        out, grad_keys, grad_values = pulled(
            k_s[here, :],
            v_s[here, :],
            kt_s[:, here],
            q_s[here, :],
            grads[here, :],
            logs,
            d_s[:2, here],
            lambda scores: jnp.where(same, scores, MASKED),
        )
        dqt_s[:, here] = out
        where = slice(start + at, start + at + 128)
        dqt_s[:, where] += edge_out[:, inner : inner + 128]
        dk_s[here, :] += grad_keys
        dv_s[here, :] += grad_values
    if turned:
        for p in range(PLANE):
            here = slice(p * BLOCK, (p + 1) * BLOCK)
            dqkv_ref[p, :both, :] = to_half(dqt_s[:, here])
            dqkv_ref[p, both : 2 * both, :] = to_half(dk_s[here, :].T)
            dqkv_ref[p, 2 * both :, :] = to_half(dv_s[here, :].T)
    else:
        dqkv_ref[:, :both] = to_half(dqt_s[...].T)
        dqkv_ref[:, both : 2 * both] = to_half(dk_s[...])
        dqkv_ref[:, 2 * both :] = to_half(dv_s[...])


def attend(qkv, labels):
    turned = qkv.ndim == 3
    tokens = labels.shape[0]
    both = qkv.shape[1] // 3
    shape = (PLANE, both, BLOCK) if turned else (tokens, both)
    return pl.pallas_call(
        functools.partial(attend_kernel, both // 2),
        out_shape=(
            jax.ShapeDtypeStruct(shape, jnp.bfloat16),
            jax.ShapeDtypeStruct((8, tokens), jnp.float32),
        ),
        scratch_shapes=[
            pltpu.VMEM((tokens, both), jnp.bfloat16),
            pltpu.VMEM((tokens, both), jnp.bfloat16),
            pltpu.VMEM((both, tokens), jnp.bfloat16),
            pltpu.VMEM((both, tokens), jnp.float32),
        ],
        compiler_params=pltpu.CompilerParams(vmem_limit_bytes=VMEM_LIMIT),
        cost_estimate=estimate("attend"),
        name="attend",
    )(qkv, labels[:, None], labels[None, :])


def attend_back(qkv, out, grad, logs, labels):
    turned = qkv.ndim == 3
    tokens = labels.shape[0]
    both = qkv.shape[1] // 3
    return pl.pallas_call(
        functools.partial(attend_back_kernel, both // 2),
        out_shape=jax.ShapeDtypeStruct(qkv.shape, jnp.bfloat16),
        scratch_shapes=[
            pltpu.VMEM((tokens, both), jnp.bfloat16),
            pltpu.VMEM((tokens, both), jnp.bfloat16),
            pltpu.VMEM((tokens, both), jnp.bfloat16),
            pltpu.VMEM((both, tokens), jnp.bfloat16),
            pltpu.VMEM((8, tokens), jnp.float32),
            pltpu.VMEM((both, tokens), jnp.float32),
            pltpu.VMEM((tokens, both), jnp.float32),
            pltpu.VMEM((tokens, both), jnp.float32),
        ]
        + ([pltpu.VMEM((tokens, both), jnp.bfloat16)] if turned else []),
        compiler_params=pltpu.CompilerParams(vmem_limit_bytes=VMEM_LIMIT),
        cost_estimate=estimate("attend_back"),
        name="attend_back",
    )(qkv, out, grad, logs, labels[:, None], labels[None, :])


def exchange(parts):
    return lax.all_to_all(parts, GROUP_AXES, split_axis=0, concat_axis=0, tiled=True)


def to_heads(parts, axes):
    moved = lax.all_to_all(parts, axes, split_axis=0, concat_axis=0, tiled=True)
    return moved.reshape(-1, parts.shape[2])


def to_tokens(values, axes):
    count = PLANE // (2 if len(axes) == 2 else 1)
    parts = values.reshape(count, -1, values.shape[1])
    return lax.all_to_all(parts, axes, split_axis=0, concat_axis=0, tiled=True)


def encoder_columns(weight):
    rows, columns = weight.shape
    return weight.reshape(rows, 3, PLANE, -1).transpose(0, 2, 1, 3).reshape(rows, columns)


def encoder_columns_back(weight):
    rows, columns = weight.shape
    return weight.reshape(rows, PLANE, 3, -1).transpose(0, 2, 1, 3).reshape(rows, columns)


def per_device(
    pixels,
    clip_index,
    patch_weight,
    encoder_attention,
    encoder_output,
    encoder_expand,
    encoder_reduce,
    predictor_embed,
    predictor_weights,
    encoder_gains,
    encoder_biases,
    predictor_gains,
    predictor_biases,
    cotangent,
):
    labels = lax.dynamic_index_in_dim(clip_index, lax.axis_index("z"), 0, keepdims=False)
    width = encoder_output.shape[1]
    pred_width = predictor_embed.shape[1]
    hidden = encoder_expand.shape[1]

    order = Order()
    shard_rows = predictor_weights.shape[0]
    rows = pixels.shape[0]
    core = lax.axis_index("c")
    low = core == 0
    wide_columns = encoder_columns(to_half(encoder_attention))
    half_patch, half_expand = to_half(patch_weight), to_half(encoder_expand)
    patch = Gather(order, both_rows(column_half(half_patch), column_half(half_patch, True)))
    attention = Gather(order, both_rows(column_half(wide_columns), column_half(wide_columns, True)))
    half_expand = both_rows(odd_blocks(half_expand), odd_blocks(half_expand, True))
    output = Gather(
        order, jnp.concatenate([to_half(encoder_output), to_half(predictor_embed)], 1), True
    )
    hidden_bias = encoder_biases[5:].reshape(-1, 2, 128)
    hidden_bias = lax.dynamic_index_in_dim(hidden_bias, core, 1, False).reshape(1, -1)

    patch.along_z()
    reduce = Gather(order, to_half(encoder_reduce))
    order.leave(attention.held)
    pixels_got = swap(pixels, "c")
    attention.along_z()
    patch.rest_of_z()
    patch.first()
    attention.rest_of_z()
    output.along_z()
    patch.second()
    half_predictor = to_half(predictor_weights).reshape(shard_rows, 3 * pred_width)
    half_expand, half_predictor = order.enter(half_expand, half_predictor)
    expand = Whole(order, half_expand)
    attention.first()
    output.rest_of_z()
    reduce.along_z()
    patch.done()
    mine, theirs = embed_tokens(pixels, order.enter(pixels_got), patch.own)
    got = swap(order.leave(theirs), "c")
    attention.second()
    embedded, normed = norm_tokens(mine, order.enter(got), encoder_gains, encoder_biases)
    normed = order.leave(normed)
    normed_got = swap(normed, "c")
    reduce.rest_of_z()
    output.first()
    attention.done()

    normed, normed_got = order.enter(normed, normed_got)
    normed_both, parts = project_tokens(normed, normed_got, attention.own)
    qkv = to_heads(order.leave(parts), CHIP_AXES)
    output.second()
    qkv = order.enter(qkv)
    mixed_heads, logs = attend(qkv, labels)
    mixed_heads = order.leave(mixed_heads)
    reduce.first()
    parts = to_tokens(order.enter(mixed_heads), CHIP_AXES)
    output.done()
    output.cores()
    parts = order.enter(parts)
    theirs = lax.dynamic_slice_in_dim(parts, (1 - core) * rows, rows, 1)
    got = swap(order.leave(theirs), "c")
    reduce.second()
    attended, middle, second = middle_tokens(
        embedded, parts, order.enter(got), output.whole, encoder_gains, encoder_biases
    )
    second = order.leave(second)
    second_got = swap(second, "c")
    second, second_got = order.enter(second, second_got)
    second_both, expanded, activated = expand_tokens(second, second_got, expand.own, hidden_bias)
    order.leave(activated)
    reduce.done()
    mine, theirs = reduce_tokens(order.enter(activated), reduce.own)
    got = swap(order.leave(theirs), "c")
    weights = lax.all_gather(half_predictor, AXES, axis=0, tiled=True)
    encoded, pred_in, pred_normed, parts = encode_tokens(
        middle,
        mine,
        got,
        output.whole,
        encoder_biases,
        weights,
        predictor_gains,
        predictor_biases,
    )
    pred_qkv = exchange(parts)
    pred_heads, pred_logs = attend(pred_qkv, labels)
    prediction, pred_middle_grad, pred_grads, parts, pred_sums, pred_hidden_sums = pred_feed(
        pred_in,
        exchange(pred_heads),
        weights,
        predictor_gains,
        predictor_biases,
        cotangent,
    )

    grad_qkv = attend_back(
        pred_qkv, pred_heads, exchange(parts), pred_logs, labels
    )
    pred_grads, half_in, grad_encoded, encoded_half, pred_in_sums = pred_back(
        exchange(grad_qkv),
        pred_normed,
        pred_in,
        pred_middle_grad,
        weights,
        predictor_gains,
        output.whole,
        pred_grads,
    )

    encoded_half = order.leave(encoded_half)
    half_got = swap(encoded_half, "c")
    sum_p = Scatter.of_cores(order, order.enter(pred_grads))
    encoded_half, half_got = order.enter(encoded_half, half_got)
    grad_both, grad_expanded, hidden_sums = reduce_back(
        encoded_half, half_got, reduce.own, expanded
    )
    order.leave(grad_expanded)
    sum_r = Scatter(order, weight_grad([activated], [order.enter(grad_both)]))
    mine, theirs = expand_back(order.enter(grad_expanded), expand.own)
    got = swap(order.leave(theirs), "c")
    grad_middle, half_middle, middle_sums, keep, send = middle_back(
        middle, grad_encoded, mine, order.enter(got), encoder_gains, output.whole
    )
    sum_p.first()
    got = swap(order.leave(send), "c")
    sum_e = Scatter(order, weight_grad([second_both], [order.enter(grad_expanded)]))
    keep, got = order.enter(keep, got)
    parts = jnp.where(low, jnp.concatenate([keep, got], 1), jnp.concatenate([got, keep], 1))
    grad_heads = to_heads(order.leave(parts), CHIP_AXES)
    late_middle, late_in = order.enter(half_middle, half_in)
    sum_o = Scatter.of_cores(order, weight_grads([attended, encoded], [late_middle, late_in]))
    sum_r.second()
    sum_p.second()
    grad_heads = order.enter(grad_heads)
    grad_qkv = attend_back(qkv, mixed_heads, grad_heads, logs, labels)
    parts = to_tokens(order.leave(grad_qkv), CHIP_AXES)
    sum_r.along_z()
    sum_e.second()
    sum_o.first()
    sum_r.rest_of_z()
    sum_p.along_z()
    parts = order.enter(parts)
    sum_a = Scatter(order, weight_grad([normed_both], [parts]))
    sum_e.along_z()
    mine, theirs = project_back(order.enter(parts), attention.own)
    got = swap(order.leave(theirs), "c")
    sum_o.second()
    sum_r.done()
    keep, send, out_sums = input_back(
        embedded, grad_middle, mine, order.enter(got), encoder_gains
    )
    got = swap(order.leave(send), "c")
    sum_p.rest_of_z()
    got = order.enter(got)
    sum_k = Scatter(order, weight_grad([pixels, pixels_got], [keep, got]))
    hidden_sums = jnp.where(
        jnp.arange(2)[None, :, None] == core, hidden_sums.reshape(-1, 1, 128), 0.0
    ).reshape(1, -1)

    vectors = [
        out_sums[2],
        middle_sums[3],
        out_sums[0],
        out_sums[1],
        middle_sums[0],
        middle_sums[1],
        middle_sums[2],
        hidden_sums[0],
        pred_in_sums[2],
        pred_sums[3],
        pred_in_sums[0],
        pred_in_sums[1],
        pred_sums[0],
        pred_sums[1],
        pred_sums[2],
        pred_hidden_sums[0],
    ]
    sums = Total(order, jnp.concatenate(vectors).reshape(-1, 128))
    sums.step()
    pixel_mine, pixel_theirs = pixel_back(keep, order.enter(got), patch.own)
    pixel_theirs = swap(order.leave(pixel_theirs), "c")
    sums.step()
    sum_a.second()
    sum_k.second()
    sums.step()
    sum_o.along_z()
    sum_e.rest_of_z()
    sum_a.along_z()
    sums.step()
    sum_k.along_z()
    sum_p.done()
    sum_e.done()
    sum_o.rest_of_z()
    sum_a.rest_of_z()
    sums.step()
    sum_k.rest_of_z()
    sum_o.done()
    sum_a.done()
    sums.step()
    sum_k.done()
    pixel_grad = to_half(pixel_mine + to_full(pixel_theirs))

    patch_grad = jnp.concatenate(sum_k.column_halves(), 1)
    attention_grad = jnp.concatenate(sum_a.column_halves(), 1)
    expand_grad = jnp.stack(
        [v.reshape(v.shape[0], -1, 128) for v in sum_e.column_halves()], 2
    ).reshape(-1, hidden)
    sum_o.done()
    reduce_grad = to_full(sum_r.total)
    output_grad, embed_grad = (to_full(v) for v in jnp.split(sum_o.total, [width], 1))
    predictor_grad = to_full(sum_p.total)
    total = sums.done().reshape(-1)
    split = 11 * width
    encoder_vectors = total[:split].reshape(11, width)
    predictor_vectors = total[split:].reshape(11, pred_width)
    return (
        prediction,
        pixel_grad,
        patch_grad,
        encoder_columns_back(attention_grad),
        output_grad,
        expand_grad,
        reduce_grad,
        embed_grad,
        predictor_grad.reshape(shard_rows, 3, pred_width),
        encoder_vectors[:2],
        encoder_vectors[2:],
        predictor_vectors[:2],
        predictor_vectors[2:],
    )


def solution(mesh):
    CALLS.clear()
    wide, narrow = mesh.devices.shape
    fine = Mesh(mesh.devices.reshape(wide // 2, 2, narrow // 2, 2), AXES)
    rows = P(AXES, None)
    rows_three = P(AXES, None, None)
    in_specs = (rows, P(), rows, rows, rows, rows, rows, rows, rows_three, P(), P(), P(), P(), rows)
    out_specs = (rows,) * 8 + (rows_three, P(), P(), P(), P())
    return jax.shard_map(
        per_device, mesh=fine, in_specs=in_specs, out_specs=out_specs, check_vma=False
    )
```

```python
import functools
import itertools

import jax
import jax.numpy as jnp
from jax import lax
from jax.experimental import pallas as pl
from jax.experimental.pallas import tpu as pltpu
from jax.sharding import Mesh
from jax.sharding import PartitionSpec as P

HEADS = 16
PRED_HEADS = 12

EPSILON = 1e-06
GELU_SCALE = 0.7978845608028654
LOG2E = 1.4426950408889634
MASKED = -1e30

PLANE = 8
BLOCK = 256
CLIP_LOW = 224
CLIP_HIGH = 1824
MARGIN = 32
CLIP_ID = 2

AXES = ("z", "y", "x", "c")
GROUP_AXES = ("y", "x", "c")
CHIP_AXES = ("y", "x")
VMEM_LIMIT = 48 * 1024 * 1024

EST = {2: 1.5, 36: 6.0, 39: 0.0, 6: 6.0, 1: 0.2, 22: 0.7, 27: 0.0, 37: 0.0}

COST = {
    "embed_tokens": 2.1,
    "norm_tokens": 1,
    "project_tokens": 4.5,
    "attend": 18,
    "middle_tokens": 3.9,
    "expand_tokens": 7.2,
    "reduce_tokens": 5.5,
    "encode_tokens": 3.5,
    "pred_feed": 6.7,
    "pred_back": 4.3,
    "attend_back": 19,
    "reduce_back": 7.1,
    "weight_grad": 4,
    "weight_grads": 2,
    "expand_back": 6.5,
    "middle_back": 3.9,
    "project_back": 6.5,
    "input_back": 2.2,
    "pixel_back": 1.9,
    "interleave": 1.5,
    "assemble": 2.5,
    "route_cores": 2,
    "add": 1.5,
}


CALLS = []


def estimate(name):
    CALLS.append(name)
    micros = EST.get(len(CALLS), COST[name] / 3)
    return pl.CostEstimate(flops=int(micros * 1.15e9), bytes_accessed=0, transcendentals=0)


def swap(value, axis, distance=1):
    size = lax.axis_size(axis)
    return lax.ppermute(value, axis, [(i, i ^ distance) for i in range(size)])


class Order:
    def __init__(self):
        self.clock = ()

    def enter(self, *values):
        if self.clock:
            values = lax.optimization_barrier(values + self.clock)[: len(values)]
        return values if len(values) > 1 else values[0]

    def leave(self, *values):
        self.clock = values
        return values if len(values) > 1 else values[0]


def to_half(values):
    return values.astype(jnp.bfloat16)


def to_full(values):
    return values.astype(jnp.float32)


def product(left, right):
    return jnp.dot(left, right, preferred_element_type=jnp.float32)


def left_product(left, right):
    return lax.dot_general(
        left, right, (((0,), (0,)), ((), ())), preferred_element_type=jnp.float32
    )


def aligned(value):
    return value.shape[-2] % 16 == 0


def position():
    return jnp.stack([lax.axis_index(axis) for axis in AXES]).astype(jnp.int32)


def by_distance(view, first):
    at = 0
    for axis in AXES[:first]:
        bit = 1
        size = view.shape[at]
        while bit < size:
            cut = view.reshape(view.shape[:at] + (size // (2 * bit), 2, bit) + view.shape[at + 1 :])
            here = lax.axis_index(axis) // bit % 2
            view = jnp.where(here == 0, cut, jnp.flip(cut, at + 1)).reshape(view.shape)
            bit *= 2
        at += 1
    return view


def small_kernel(kernel, outs, ins, name):
    vmem = pl.BlockSpec(memory_space=pltpu.VMEM)
    return pl.pallas_call(
        kernel,
        out_shape=[jax.ShapeDtypeStruct(shape, jnp.bfloat16) for shape in outs],
        in_specs=[pl.BlockSpec(memory_space=pltpu.SMEM)] + [vmem] * len(ins),
        out_specs=[vmem] * len(outs),
        compiler_params=pltpu.CompilerParams(vmem_limit_bytes=VMEM_LIMIT),
        cost_estimate=estimate(name),
        name=name,
    )(position(), *ins)


def assemble(one, got_one, two, got_two):
    half = one.shape[1]
    if not aligned(one):
        near = jnp.stack([one, got_one], 2)
        far = jnp.stack([two, got_two], 1)
        near = jnp.moveaxis(near, 1, 0)
        far = jnp.moveaxis(far, 2, 0)
        return by_distance(jnp.concatenate([near, jnp.moveaxis(far, 1, 2)], 0), 3)

    def kernel(place, one, got_one, two, got_two, out):
        z, y, x = place[0], place[1], place[2]
        for k, h in itertools.product(range(2), range(half)):
            out[z ^ h, y ^ k, x] = one[k, h]
            out[z ^ h, y ^ k, 1 - x] = got_one[k, h]
            out[z ^ (h + half), y, x ^ k] = two[k, h]
            out[z ^ (h + half), 1 - y, x ^ k] = got_two[k, h]

    shape = (2 * half, 2, 2) + one.shape[2:]
    return small_kernel(kernel, [shape], [one, got_one, two, got_two], "assemble")[0]


def interleave(own, got):
    if not aligned(own):
        low = lax.axis_index("c") == 0
        return jnp.stack([jnp.where(low, own, got), jnp.where(low, got, own)], 3)

    def kernel(place, own, got, out):
        for index in itertools.product(*(range(n) for n in own.shape[:3])):
            out[index + (place[3],)] = own[index]
            out[index + (1 - place[3],)] = got[index]

    return small_kernel(kernel, [own.shape[:3] + (2,) + own.shape[3:]], [own, got], "interleave")[0]


def routes(view):
    half = view.shape[0] // 2
    near, far = jnp.moveaxis(view[:half], 0, 2), jnp.moveaxis(view[half:], 0, 2)
    return near[:, 0], near[:, 1], far[0], far[1]


def route_cores(grads):
    count = lax.axis_size("z")
    view = grads.reshape(count, 2, 2, 2, -1, grads.shape[-1])
    half = count // 2
    if not aligned(view):
        view = by_distance(view, 4)
        return [
            jnp.stack([jnp.stack(pair) for pair in zip(*[iter(routes(view[:, :, :, core]))] * 2)])
            for core in range(2)
        ]

    def kernel(place, view, keep, send):
        z, y, x, c = (place[i] for i in range(4))
        for out, core in ((keep, c), (send, 1 - c)):
            for i, k, h in itertools.product(range(2), range(2), range(half)):
                out[0, i, k, h] = view[z ^ h, y ^ k, x ^ i, core]
                out[1, i, k, h] = view[z ^ (h + half), y ^ i, x ^ k, core]

    shape = (2, 2, 2, half) + view.shape[4:]
    return small_kernel(kernel, [shape, shape], [view], "route_cores")


def add(pairs, pieces=2):
    if not aligned(pairs[0][0]):
        outs = []
        for own, got in pairs:
            total = to_half(to_full(own) + to_full(got))
            outs += jnp.split(total, pieces, 0)
        return outs
    shapes = [(own.shape[0] // pieces,) + own.shape[1:] for own, _ in pairs for _ in range(pieces)]

    def kernel(place, *refs):
        outs = refs[2 * len(pairs) :]
        for i in range(len(pairs)):
            for j in range(pieces):
                out = outs[i * pieces + j]
                size = out.shape[0]
                here = pl.ds(j * size, size)
                out[...] = to_half(to_full(refs[2 * i][here]) + to_full(refs[2 * i + 1][here]))

    return small_kernel(kernel, shapes, [v for pair in pairs for v in pair], "add")


class Gather:
    def __init__(self, order, shard, both=False):
        self.order, self.both, self.distance = order, both, 1
        self.held = shard

    def along_z(self):
        if self.distance == 1:
            held = self.order.enter(self.held)[None]
        else:
            held = jnp.concatenate(self.order.enter(self.held, self.flight), 0)
        self.held = self.order.leave(held)
        self.flight = swap(self.held, "z", self.distance)
        self.distance *= 2

    def rest_of_z(self):
        while self.distance < lax.axis_size("z"):
            self.along_z()

    def first(self):
        self.held = self.order.leave(*self.order.enter(self.held, self.flight))
        self.flight = [swap(self.held[0], "y"), swap(self.held[1], "x")]

    def second(self):
        one, two, *got = self.order.enter(*self.held, *self.flight)
        self.held = self.order.leave(jnp.stack([one, got[0]]), jnp.stack([two, got[1]]))
        self.flight = [swap(self.held[0], "x"), swap(self.held[1], "y")]

    def done(self):
        one, two, *got = self.order.enter(*self.held, *self.flight)
        held = self.order.leave(assemble(one, got[0], two, got[1]))
        if self.both:
            self.held, self.flight = held, swap(held, "c")
        else:
            self.own = held.reshape(-1, held.shape[-1])

    def cores(self):
        whole = interleave(*self.order.enter(self.held, self.flight))
        self.whole = whole.reshape(-1, whole.shape[-1])


class Whole:
    def __init__(self, order, shard):
        self.own = lax.all_gather(shard, ("z", "y", "x"), axis=0, tiled=True)

    def along_z(self):
        pass

    rest_of_z = first = second = done = along_z


class Scatter:
    def __init__(self, order, parts):
        self.order, self.distance = order, 0
        self.start(parts)

    @classmethod
    def of_cores(cls, order, grads):
        self = cls.__new__(cls)
        self.order, self.distance = order, 0
        self.held, send = route_cores(grads)
        self.flight = swap(order.leave(send), "c")
        return self

    def first(self):
        got = self.order.enter(self.flight)
        flat = [v.reshape((4,) + v.shape[2:]) for v in (self.held, got)]
        self.start([v[0] for v in add([flat], 4)])

    def start(self, parts):
        keep_one, send_one, keep_two, send_two = parts
        sent = self.order.leave(send_one, send_two)
        self.held = [keep_one, keep_two]
        self.flight = [swap(sent[0], "x"), swap(sent[1], "y")]

    def second(self):
        got = self.order.enter(*self.flight)
        keep_one, send_one, keep_two, send_two = (v[0] for v in add(list(zip(self.held, got))))
        sent = self.order.leave(send_one, send_two)
        self.held = [keep_one, keep_two]
        self.flight = [swap(sent[0], "y"), swap(sent[1], "x")]

    def along_z(self):
        if self.distance == 0:
            got = self.order.enter(*self.flight)
            self.distance = lax.axis_size("z") // 2
            keep, send = add(list(zip(self.held, got)), 1)
        else:
            self.distance //= 2
            keep, send = add([(self.held, self.order.enter(self.flight))])
        self.held = keep
        self.flight = swap(self.order.leave(send), "z", self.distance)

    def rest_of_z(self):
        while self.distance > 1:
            self.along_z()

    def done(self):
        got = self.order.enter(self.flight)
        self.total = self.order.leave(to_half(to_full(self.held[0]) + to_full(got[0])))

    def column_halves(self):
        total = self.total.reshape(2, -1, self.total.shape[-1])
        core = lax.axis_index("c")
        mine = lax.dynamic_index_in_dim(total, core, 0, False)
        theirs = swap(lax.dynamic_index_in_dim(total, 1 - core, 0, False), "c")
        low = core == 0
        return to_full(jnp.where(low, mine, theirs)), to_full(jnp.where(low, theirs, mine))


def both_rows(keep, send):
    got = swap(send, "c")
    low = lax.axis_index("c") == 0
    return jnp.where(low, jnp.concatenate([keep, got], 0), jnp.concatenate([got, keep], 0))


def column_half(value, other=False):
    size = value.shape[-1] // 2
    core = lax.axis_index("c")
    return lax.dynamic_slice_in_dim(value, (1 - core if other else core) * size, size, value.ndim - 1)


def odd_blocks(value, other=False):
    core = lax.axis_index("c")
    blocks = value.reshape(value.shape[0], -1, 2, 128)
    return lax.dynamic_index_in_dim(blocks, 1 - core if other else core, 2, False).reshape(
        value.shape[0], -1
    )


def nt(left, right):
    return lax.dot_general(
        left, right, (((1,), (1,)), ((), ())), preferred_element_type=jnp.float32
    )


def norm_parts(values):
    center = values - jnp.mean(values, -1, keepdims=True)
    factor = lax.rsqrt(jnp.mean(center * center, -1, keepdims=True) + EPSILON)
    return center * factor, factor


def norm(values, gain, bias):
    return norm_parts(values)[0] * gain + bias


def norm_back(values, gain, grad):
    shape, factor = norm_parts(values)
    inner = grad * gain
    mean = jnp.mean(inner, -1, keepdims=True)
    along = jnp.mean(inner * shape, -1, keepdims=True)
    return (
        factor * (inner - mean - shape * along),
        jnp.sum(grad * shape, 0, keepdims=True),
        jnp.sum(grad, 0, keepdims=True),
    )


def gate(values):
    return 0.5 * values * (1.0 + jnp.tanh(GELU_SCALE * (values + 0.044715 * values * values * values)))


def gate_slope(values):
    square = values * values
    slope = jnp.tanh(GELU_SCALE * values * (1.0 + 0.044715 * square))
    return 0.5 * (1.0 + slope) + 0.5 * values * (1.0 - slope * slope) * (
        GELU_SCALE * (1.0 + 3 * 0.044715 * square)
    )


def columns(side, size, start=0, width=None):
    return pl.ds(pl.multiple_of(side * size + start, 128), size if width is None else width)


def run(kernel, outs, ins, grid=(), in_specs=None, out_specs=None, scratch=(), name=None, **more):
    whole = pl.BlockSpec(memory_space=pltpu.VMEM)
    in_specs = in_specs or {}
    out_specs = out_specs or {}

    def spec(given, value):
        if given is not None:
            return given
        if not grid:
            return whole
        return pl.BlockSpec(value.shape, lambda *_, rank=len(value.shape): (0,) * rank)

    core = lax.axis_index("c").astype(jnp.int32).reshape(1)
    outs = [jax.ShapeDtypeStruct(shape, dtype) for shape, dtype in outs]
    return pl.pallas_call(
        kernel,
        out_shape=outs,
        grid=grid,
        in_specs=[pl.BlockSpec(memory_space=pltpu.SMEM)]
        + [spec(in_specs.get(i), v) for i, v in enumerate(ins)],
        out_specs=[spec(out_specs.get(i), v) for i, v in enumerate(outs)],
        scratch_shapes=scratch,
        compiler_params=pltpu.CompilerParams(vmem_limit_bytes=VMEM_LIMIT),
        cost_estimate=estimate(name),
        name=name,
        **more,
    )(core, *ins)


HALF = jnp.bfloat16
FULL = jnp.float32


def embed_kernel(core, mine, theirs, weight, out_mine, out_theirs):
    out_mine[...] = product(mine[...], weight[...])
    out_theirs[...] = product(theirs[...], weight[...])


def embed_tokens(mine, theirs, weight):
    shape = ((mine.shape[0], weight.shape[1]), FULL)
    return run(embed_kernel, [shape, shape], [mine, theirs, weight], name="embed_tokens")


def norm_kernel(core, mine, got, gains, biases, embedded, normed):
    size = mine.shape[1]
    embedded[:, columns(core[0], size)] = mine[...]
    embedded[:, columns(1 - core[0], size)] = got[...]
    values = embedded[...] + biases[0:1]
    embedded[...] = values
    normed[...] = to_half(norm(values, gains[0:1], biases[1:2]))


def norm_tokens(mine, got, gains, biases):
    shape = (mine.shape[0], gains.shape[1])
    return run(
        norm_kernel, [(shape, FULL), (shape, HALF)], [mine, got, gains, biases], name="norm_tokens"
    )


def token_rows(side, rows):
    return pl.ds(pl.multiple_of(side * rows, rows), rows)


def project_kernel(core, mine, got, weight, both, out):
    rows = mine.shape[0]

    @pl.when(pl.program_id(0) == 0)
    def _():
        both[token_rows(core[0], rows), :] = mine[...]
        both[token_rows(1 - core[0], rows), :] = got[...]

    out[0] = to_half(product(both[...], weight[...]))


def project_tokens(mine, got, weight):
    rows, width = mine.shape
    each = weight.shape[1] // 4
    return run(
        project_kernel,
        [((2 * rows, width), HALF), ((4, 2 * rows, each), HALF)],
        [mine, got, weight],
        grid=(4,),
        in_specs={2: pl.BlockSpec((width, each), lambda j: (0, j))},
        out_specs={1: pl.BlockSpec((1, 2 * rows, each), lambda j: (j, 0, 0))},
        name="project_tokens",
    )


def middle_kernel(
    core, embedded, parts, got, weight, gains, biases, attended, middle, second
):
    rows = got.shape[1]
    each = parts.shape[2]
    width = embedded.shape[1]
    for q in range(4):
        attended[:, columns(core[0], 4 * each, q * each, each)] = parts[
            q, token_rows(core[0], rows), :
        ]
        attended[:, columns(1 - core[0], 4 * each, q * each, each)] = got[q]
    values = embedded[...] + product(attended[...], weight[:, :width]) + biases[2:3]
    middle[...] = values
    second[...] = to_half(norm(values, gains[1:2], biases[3:4]))


def middle_tokens(embedded, parts, got, weight, gains, biases):
    shape = embedded.shape
    return run(
        middle_kernel,
        [(shape, HALF), (shape, FULL), (shape, HALF)],
        [embedded, parts, got, weight, gains, biases],
        name="middle_tokens",
    )


def expand_kernel(core, mine, got, weight, bias, both, expanded, activated):
    rows = mine.shape[0]

    @pl.when(pl.program_id(0) == 0)
    def _():
        both[:rows, :] = mine[...]
        both[rows:, :] = got[...]

    values = product(both[...], weight[...]) + bias[...]
    expanded[...] = values
    activated[...] = to_half(gate(values))


def expand_tokens(mine, got, weight, bias):
    rows, width = mine.shape
    hidden = weight.shape[1]
    tile = pl.BlockSpec((2 * rows, 512), lambda j: (0, j))
    return run(
        expand_kernel,
        [((2 * rows, width), HALF), ((2 * rows, hidden), FULL), ((2 * rows, hidden), HALF)],
        [mine, got, weight, bias],
        grid=(hidden // 512,),
        in_specs={
            2: pl.BlockSpec((width, 512), lambda j: (0, j)),
            3: pl.BlockSpec((1, 512), lambda j: (0, j)),
        },
        out_specs={1: tile, 2: tile},
        name="expand_tokens",
    )


def reduce_kernel(core, activated, weight, mine, theirs, total):
    step = pl.program_id(0)
    rows = mine.shape[0]
    values = product(activated[...], weight[...])

    @pl.when(step == 0)
    def _():
        total[...] = values

    @pl.when(step > 0)
    def _():
        total[...] += values

    @pl.when(step == pl.num_programs(0) - 1)
    def _():
        mine[...] = total[:rows, :]
        theirs[...] = to_half(total[rows:, :])


def reduce_tokens(activated, weight):
    rows, hidden = activated.shape
    width = weight.shape[1]
    shape = ((rows // 2, width), FULL)
    return run(
        reduce_kernel,
        [shape, (shape[0], HALF)],
        [activated, weight],
        grid=(hidden // 512,),
        in_specs={
            0: pl.BlockSpec((rows, 512), lambda j: (0, j)),
            1: pl.BlockSpec((512, width), lambda j: (j, 0)),
        },
        scratch=[pltpu.VMEM((rows, width), FULL)],
        name="reduce_tokens",
    )


def slot_of(p, size):
    return (2 * p * size, 2 * size) if p < 4 else (8 * size + (p - 4) * size, size)


def encode_kernel(
    core, middle, mine, got, weight, biases, pred_weight, pred_gains, pred_biases,
    encoded, pred_in, normed, parts, projected,
):
    full = middle.shape[1]
    encoded[...] = to_half(middle[...] + (mine[...] + to_full(got[...])) + biases[4:5])
    values = product(encoded[...], weight[:, full:]) + pred_biases[0:1]
    pred_in[...] = values
    normed[...] = to_half(norm(values, pred_gains[0:1], pred_biases[1:2]))
    width = values.shape[1]
    projected[...] = to_half(nt(pred_weight[...], normed[...]))
    both = parts.shape[1] // 3
    for p in range(PLANE):
        start, size = slot_of(p, both // 2)
        for t in range(3):
            parts[p, t * both : t * both + size, :] = projected[
                t * width + start : t * width + start + size, :
            ]
            if size < both:
                parts[p, t * both + size : (t + 1) * both, :] = jnp.zeros(
                    (both - size, parts.shape[2]), HALF
                )


def encode_tokens(middle, mine, got, weight, biases, pred_weights, pred_gains, pred_biases):
    rows = middle.shape[0]
    width = pred_gains.shape[1]
    each = 3 * 2 * width // PRED_HEADS
    return run(
        encode_kernel,
        [
            (middle.shape, HALF),
            ((rows, width), FULL),
            ((rows, width), HALF),
            ((PLANE, each, rows), HALF),
        ],
        [middle, mine, got, weight, biases, pred_weights, pred_gains, pred_biases],
        grid=(1,),
        in_specs={5: pl.BlockSpec((3 * width, width), lambda j: (0, 0))},
        scratch=[pltpu.VMEM((3 * width, rows), HALF)],
        name="encode_tokens",
    )


def pred_feed_kernel(
    core, pred_in, parts, weights, gains, biases, hidden_bias, cotangent,
    prediction, grad_middle, grad_weights, grad_parts, sums, hidden_sums, attended, expanded, work,
):
    width = pred_in.shape[1]
    both = parts.shape[1]
    for p in range(PLANE):
        start, size = slot_of(p, both // 2)
        work[start : start + size, :] = to_full(parts[p, :size, :])
    attended[...] = to_half(work[...].T)
    out_rows = slice(3 * width, weights.shape[0])
    slot = [slice(i * width, (i + 1) * width) for i in range(3)]
    middle = pred_in[...] + nt(attended[...], weights[out_rows, slot[0]]) + biases[2:3]
    second = to_half(norm(middle, gains[1:2], biases[3:4]))
    expanded[...] = nt(second, weights[:, slot[1]]) + hidden_bias[...]
    activated = to_half(gate(expanded[...]))
    result = middle + product(activated, weights[:, slot[2]]) + biases[4:5]
    prediction[...] = to_half(result)
    half_grad = cotangent[...]
    grad = to_full(half_grad)
    sums[2:3, :] = jnp.sum(grad, 0, keepdims=True)
    grad_weights[:, slot[2]] = to_half(left_product(activated, half_grad))
    grad_expanded = nt(half_grad, weights[:, slot[2]]) * gate_slope(expanded[...])
    hidden_sums[...] = jnp.sum(grad_expanded, 0, keepdims=True)
    expanded_half = to_half(grad_expanded)
    grad_weights[:, slot[1]] = to_half(left_product(expanded_half, second))
    grad_second = product(expanded_half, weights[:, slot[1]])
    from_norm, gain, bias = norm_back(middle, gains[1:2], grad_second)
    total = grad + from_norm
    grad_middle[...] = total
    sums[0:1, :] = jnp.sum(total, 0, keepdims=True)
    sums[1:2, :] = bias
    sums[3:4, :] = gain
    sums[4:8, :] = jnp.zeros((4, width), FULL)
    middle_half = to_half(total)
    grad_weights[out_rows, slot[0]] = to_half(left_product(middle_half, attended[...]))
    work[...] = product(middle_half, weights[out_rows, slot[0]]).T
    for p in range(PLANE):
        start, size = slot_of(p, both // 2)
        grad_parts[p, :size, :] = to_half(work[start : start + size, :])
        if size < both:
            grad_parts[p, size:, :] = jnp.zeros((both - size, parts.shape[2]), HALF)


def pred_feed(pred_in, parts, weights, gains, biases, cotangent):
    rows, width = pred_in.shape
    hidden = weights.shape[0]
    return run(
        pred_feed_kernel,
        [
            ((rows, width), HALF),
            ((rows, width), FULL),
            (weights.shape, HALF),
            (parts.shape, HALF),
            ((8, width), FULL),
            ((1, hidden), FULL),
        ],
        [pred_in, parts, weights, gains, biases, biases[5:].reshape(1, hidden), cotangent],
        scratch=[
            pltpu.VMEM((rows, width), HALF),
            pltpu.VMEM((rows, hidden), FULL),
            pltpu.VMEM((width, rows), FULL),
        ],
        name="pred_feed",
    )


def pred_back_kernel(
    core, parts, normed, pred_in, grad_middle, weight, gains, embed, _,
    grad_weight, half_in, grad_encoded, encoded_half, sums, projected,
):
    width = pred_in.shape[1]
    both = parts.shape[1] // 3
    for p in range(PLANE):
        start, size = slot_of(p, both // 2)
        for t in range(3):
            projected[t * width + start : t * width + start + size, :] = parts[
                p, t * both : t * both + size, :
            ]
    grad_weight[...] = to_half(product(projected[...], normed[...]))
    grad_normed = left_product(projected[...], weight[...])
    into_norm, gain, bias = norm_back(pred_in[...], gains[0:1], grad_normed)
    total = grad_middle[...] + into_norm
    sums[0:1, :] = jnp.sum(total, 0, keepdims=True)
    sums[1:2, :] = bias
    sums[2:3, :] = gain
    sums[3:8, :] = jnp.zeros((5, width), FULL)
    half_in[...] = to_half(total)
    values = nt(half_in[...], embed[:, embed.shape[1] - width :])
    grad_encoded[...] = values
    encoded_half[...] = to_half(values)


def pred_back(parts, normed, pred_in, grad_middle, weights, gains, embed, grad_weights):
    rows, width = pred_in.shape
    full = embed.shape[0]
    block = pl.BlockSpec((3 * width, width), lambda j: (0, 0))
    return run(
        pred_back_kernel,
        [
            (grad_weights.shape, HALF),
            ((rows, width), HALF),
            ((rows, full), FULL),
            ((rows, full), HALF),
            ((8, width), FULL),
        ],
        [parts, normed, pred_in, grad_middle, weights, gains, embed, grad_weights],
        grid=(1,),
        in_specs={4: block, 7: pl.BlockSpec(memory_space=pl.ANY)},
        out_specs={0: block},
        scratch=[pltpu.VMEM((3 * width, rows), HALF)],
        name="pred_back",
        input_output_aliases={8: 0},
    )


def reduce_back_kernel(core, mine, got, weight, expanded, both, out, sums):
    rows = mine.shape[0]

    @pl.when(pl.program_id(0) == 0)
    def _():
        both[:rows, :] = mine[...]
        both[rows:, :] = got[...]

    values = nt(both[...], weight[...]) * gate_slope(expanded[...])
    out[...] = to_half(values)
    sums[...] = jnp.sum(values, 0, keepdims=True)


def reduce_back(mine, got, weight, expanded):
    rows, hidden = expanded.shape
    width = mine.shape[1]
    tile = pl.BlockSpec((rows, 512), lambda j: (0, j))
    return run(
        reduce_back_kernel,
        [((rows, width), HALF), ((rows, hidden), HALF), ((1, hidden), FULL)],
        [mine, got, weight, expanded],
        grid=(hidden // 512,),
        in_specs={2: pl.BlockSpec((512, width), lambda j: (j, 0)), 3: tile},
        out_specs={1: tile, 2: pl.BlockSpec((1, 512), lambda j: (0, j))},
        name="reduce_back",
    )


def expand_back_kernel(core, grad, weight, mine, theirs, total):
    step = pl.program_id(0)
    rows = mine.shape[0]
    values = nt(grad[...], weight[...])

    @pl.when(step == 0)
    def _():
        total[...] = values

    @pl.when(step > 0)
    def _():
        total[...] += values

    @pl.when(step == pl.num_programs(0) - 1)
    def _():
        mine[...] = total[:rows, :]
        theirs[...] = to_half(total[rows:, :])


def expand_back(grad, weight):
    rows, hidden = grad.shape
    width = weight.shape[0]
    shape = ((rows // 2, width), FULL)
    return run(
        expand_back_kernel,
        [shape, (shape[0], HALF)],
        [grad, weight],
        grid=(hidden // 512,),
        in_specs={
            0: pl.BlockSpec((rows, 512), lambda j: (0, j)),
            1: pl.BlockSpec((width, 512), lambda j: (0, j)),
        },
        scratch=[pltpu.VMEM((rows, width), FULL)],
        name="expand_back",
    )


def middle_back_kernel(
    core, middle, grad, mine, got, gains, weight, grad_middle, half_middle, sums, keep, send, work
):
    width = middle.shape[1]
    from_norm, gain, bias = norm_back(middle[...], gains[1:2], mine[...] + to_full(got[...]))
    values = grad[...] + from_norm
    grad_middle[...] = values
    sums[0:1, :] = jnp.sum(values, 0, keepdims=True)
    sums[1:2, :] = bias
    sums[2:3, :] = jnp.sum(grad[...], 0, keepdims=True)
    sums[3:4, :] = gain
    sums[4:8, :] = jnp.zeros((4, width), FULL)
    half_middle[...] = to_half(values)
    work[...] = to_half(nt(half_middle[...], weight[:, :width]))
    each = keep.shape[2]
    for q in range(4):
        keep[q] = work[:, columns(core[0], 4 * each, q * each, each)]
        send[q] = work[:, columns(1 - core[0], 4 * each, q * each, each)]


def middle_back(middle, grad, mine, got, gains, weight):
    rows, width = middle.shape
    parts = ((4, rows, width // PLANE), HALF)
    return run(
        middle_back_kernel,
        [((rows, width), FULL), ((rows, width), HALF), ((8, width), FULL), parts, parts],
        [middle, grad, mine, got, gains, weight],
        scratch=[pltpu.VMEM((rows, width), HALF)],
        name="middle_back",
    )


def project_back_kernel(core, parts, weight, mine, theirs, total):
    step = pl.program_id(0)
    rows = mine.shape[0]
    values = nt(parts[0], weight[...])

    @pl.when(step == 0)
    def _():
        total[...] = values

    @pl.when(step > 0)
    def _():
        total[...] += values

    @pl.when(step == pl.num_programs(0) - 1)
    def _():
        mine[...] = total[token_rows(core[0], rows), :]
        theirs[...] = to_half(total[token_rows(1 - core[0], rows), :])


def project_back(parts, weight):
    _, rows, each = parts.shape
    width = weight.shape[0]
    shape = ((rows // 2, width), FULL)
    return run(
        project_back_kernel,
        [shape, (shape[0], HALF)],
        [parts, weight],
        grid=(4,),
        in_specs={
            0: pl.BlockSpec((1, rows, each), lambda j: (j, 0, 0)),
            1: pl.BlockSpec((width, each), lambda j: (0, j)),
        },
        scratch=[pltpu.VMEM((rows, width), FULL)],
        name="project_back",
    )


def input_back_kernel(core, embedded, grad, mine, got, gains, keep, send, sums, work):
    into_norm, gain, bias = norm_back(embedded[...], gains[0:1], mine[...] + to_full(got[...]))
    values = grad[...] + into_norm
    sums[0:1, :] = jnp.sum(values, 0, keepdims=True)
    sums[1:2, :] = bias
    sums[2:3, :] = gain
    sums[3:8, :] = jnp.zeros((5, values.shape[1]), FULL)
    work[...] = to_half(values)
    size = keep.shape[1]
    keep[...] = work[:, columns(core[0], size)]
    send[...] = work[:, columns(1 - core[0], size)]


def input_back(embedded, grad, mine, got, gains):
    rows, width = embedded.shape
    part = ((rows, width // 2), HALF)
    return run(
        input_back_kernel,
        [part, part, ((8, width), FULL)],
        [embedded, grad, mine, got, gains],
        scratch=[pltpu.VMEM((rows, width), HALF)],
        name="input_back",
    )


def pixel_kernel(core, mine, got, weight, out_mine, out_theirs):
    out_mine[...] = nt(mine[...], weight[...])
    out_theirs[...] = to_half(nt(got[...], weight[...]))


def pixel_back(mine, got, weight):
    shape = (mine.shape[0], weight.shape[0])
    return run(
        pixel_kernel, [(shape, FULL), (shape, HALF)], [mine, got, weight], name="pixel_back"
    )


def weight_kernel(count, place, *refs):
    lefts, rights = refs[:count], refs[count : 2 * count]
    keep_one, send_one, keep_two, send_two, work = refs[2 * count :]
    step, half = pl.program_id(0), pl.num_programs(0) // 2
    rows = work.shape[1]
    if len(rights[0].shape) == 3:
        each = rights[0].shape[2]
        for q in range(rights[0].shape[0]):
            values = to_half(left_product(lefts[0][...], rights[0][q]))
            for i in range(4):
                work[i, :, q * each : (q + 1) * each] = values[i * rows : (i + 1) * rows]
    else:
        values = left_product(lefts[0][...], rights[0][...])
        for left, right in zip(lefts[1:], rights[1:]):
            values += left_product(left[...], right[...])
        values = to_half(values)
        for i in range(4):
            work[i] = values[i * rows : (i + 1) * rows]
    y, x = place[1], place[2]

    @pl.when(step < half)
    def _():
        for k in range(2):
            keep_one[k, 0] = work[(y ^ k) * 2 + x]
            send_one[k, 0] = work[(y ^ k) * 2 + (1 - x)]

    @pl.when(step >= half)
    def _():
        for k in range(2):
            keep_two[k, 0] = work[y * 2 + (x ^ k)]
            send_two[k, 0] = work[(1 - y) * 2 + (x ^ k)]


def weight_grad(lefts, rights):
    depth = lefts[0].shape[1]
    right = rights[0]
    width = right.shape[0] * right.shape[2] if right.ndim == 3 else right.shape[1]
    count = lax.axis_size("z")
    rows = depth // (4 * count)
    if rows % 32 != 0:
        total = 0.0
        for left, right in zip(lefts, rights):
            if right.ndim == 3:
                right = jnp.moveaxis(right, 0, 1).reshape(left.shape[0], -1)
            total += left_product(left, right)
        return routes(by_distance(to_half(total).reshape(count, 2, 2, rows, width), 3))
    half = count // 2
    pairs = len(lefts)

    def whole(value):
        return pl.BlockSpec(value.shape, lambda j, place, rank=value.ndim: (0,) * rank)

    near = pl.BlockSpec((2, 1, rows, width), lambda j, place: (0, jnp.minimum(j, half - 1), 0, 0))
    far = pl.BlockSpec((2, 1, rows, width), lambda j, place: (0, jnp.maximum(j - half, 0), 0, 0))
    return pl.pallas_call(
        functools.partial(weight_kernel, pairs),
        out_shape=[jax.ShapeDtypeStruct((2, half, rows, width), HALF)] * 4,
        grid_spec=pltpu.PrefetchScalarGridSpec(
            num_scalar_prefetch=1,
            grid=(count,),
            in_specs=[
                pl.BlockSpec((v.shape[0], 4 * rows), lambda j, place: (0, place[0] ^ j))
                for v in lefts
            ]
            + [whole(v) for v in rights],
            out_specs=[near, near, far, far],
            scratch_shapes=[pltpu.VMEM((4, rows, width), HALF)],
        ),
        compiler_params=pltpu.CompilerParams(vmem_limit_bytes=VMEM_LIMIT),
        cost_estimate=estimate("weight_grad"),
        name="weight_grad",
    )(position(), *lefts, *rights)


def side_kernel(core, left_one, left_two, right_one, right_two, out):
    width = right_one.shape[1]
    out[:, :width] = to_half(left_product(left_one[...], right_one[...]))
    out[:, width:] = to_half(left_product(left_two[...], right_two[...]))


def weight_grads(lefts, rights):
    depth = lefts[0].shape[1]
    width = rights[0].shape[1] + rights[1].shape[1]
    tile = pl.BlockSpec((lefts[0].shape[0], 512), lambda j: (0, j))
    return run(
        side_kernel,
        [((depth, width), HALF)],
        [*lefts, *rights],
        grid=(depth // 512,),
        in_specs={0: tile, 1: tile},
        out_specs={0: pl.BlockSpec((512, width), lambda j: (j, 0))},
        name="weight_grads",
    )[0]


class Total:
    def __init__(self, order, value):
        self.order, self.held, self.flight = order, value, None
        self.steps = [
            (axis, 1 << bit)
            for axis in ("c", "x", "y", "z")
            for bit in range(lax.axis_size(axis).bit_length() - 1)
        ]

    def step(self):
        if self.flight is not None:
            self.held = self.held + self.order.enter(self.flight)
        if self.steps:
            axis, distance = self.steps.pop(0)
            self.held = self.order.leave(self.order.enter(self.held))
            self.flight = swap(self.held, axis, distance)
        else:
            self.flight = None

    def done(self):
        while self.flight is not None:
            self.step()
        return self.held


def head_lanes(values, head, size):
    lane = lax.broadcasted_iota(jnp.int32, values.shape, 1)
    return jnp.where((lane >= head * size) & (lane < (head + 1) * size), values, jnp.zeros_like(values))


def clip_bias(label_column_ref):
    low = label_column_ref[CLIP_LOW : CLIP_LOW + MARGIN, :]
    high = label_column_ref[CLIP_HIGH - MARGIN : CLIP_HIGH, :]
    return jnp.where(low == CLIP_ID, 0.0, MASKED), jnp.where(high == CLIP_ID, 0.0, MASKED)


def add_margins(scores, biases):
    low, high = biases
    return jnp.concatenate(
        [scores[:MARGIN] + low, scores[MARGIN:-MARGIN], scores[-MARGIN:] + high], 0
    )


def softmax_columns(scores, small):
    top = 0.0 if small else jnp.max(scores, 0, keepdims=True)
    expo = jnp.exp2(scores if small else scores - top)
    total = jnp.sum(expo, 0, keepdims=True)
    return to_half(expo), total, top + jnp.log2(total)


def largest_square(values, size):
    lane = lax.broadcasted_iota(jnp.int32, (values.shape[1], 128), 1)
    row = lax.broadcasted_iota(jnp.int32, (values.shape[1], 128), 0)
    picks = jnp.where(row // size == lane, 1.0, 0.0).astype(jnp.bfloat16)
    full = to_full(values)
    return jnp.max(product(to_half(full * full), picks), 0, keepdims=True)


SMALL = 60.0


def attend_kernel(size, qkv_ref, column_ref, row_ref, out_ref, log_ref, q_s, k_s, vt_s, ot_s):
    both = 2 * size
    factor = LOG2E * size**-0.5
    turned = len(qkv_ref.shape) == 3
    if turned:
        for p in range(PLANE):
            here = slice(p * BLOCK, (p + 1) * BLOCK)
            q_s[here, :] = to_half(to_full(qkv_ref[p, :both, :]).T)
            k_s[here, :] = to_half(to_full(qkv_ref[p, both : 2 * both, :]).T)
            vt_s[:, here] = qkv_ref[p, 2 * both :, :]
    else:
        q_s[...] = qkv_ref[:, :both]
        k_s[...] = qkv_ref[:, both : 2 * both]
        vt_s[...] = to_half(to_full(qkv_ref[:, 2 * both :]).T)
    biases = clip_bias(column_ref)
    squares = largest_square(q_s[...], size) * largest_square(k_s[...], size)
    bound = jnp.max(squares) * factor**2

    def heads(keys, values_t, queries, masked, small):
        outs, logs = [], []
        for head in range(2):
            scores = masked(nt(keys, head_lanes(queries, head, size)) * factor)
            probs, total, log_total = softmax_columns(scores, small)
            mixed = product(values_t, probs)[head * size : (head + 1) * size]
            outs.append(mixed / total)
            logs.append(log_total)
        return jnp.concatenate(outs, 0), jnp.concatenate(logs, 0)

    def over_clip(queries, small):
        return heads(
            k_s[CLIP_LOW:CLIP_HIGH, :],
            vt_s[:, CLIP_LOW:CLIP_HIGH],
            queries,
            lambda scores: add_margins(scores, biases),
            small,
        )

    last = (PLANE - 1) * BLOCK
    ends = ((0, BLOCK - MARGIN, 0), (last, 0, MARGIN))

    def all_rows(small, block):
        @pl.loop(0, (last - BLOCK) // block)
        def _(i):
            here = pl.ds(pl.multiple_of(BLOCK + i * block, BLOCK), block)
            out, logs = over_clip(q_s[here, :], small)
            ot_s[:, here] = out
            log_ref[:2, here] = logs

        edge = jnp.concatenate([q_s[BLOCK - MARGIN : BLOCK, :], q_s[last : last + MARGIN, :]], 0)
        edge = jnp.concatenate([head_lanes(edge, 0, size), head_lanes(edge, 1, size)], 0)
        scores = add_margins(nt(k_s[CLIP_LOW:CLIP_HIGH, :], edge) * factor, biases)
        probs, total, edge_logs = softmax_columns(scores, small)
        edge_out = product(vt_s[:, CLIP_LOW:CLIP_HIGH], probs) / total
        for start, at, inner in ends:
            here = slice(start, start + BLOCK)
            same = column_ref[here, :] == row_ref[:, here]
            out, logs = heads(
                k_s[here, :],
                vt_s[:, here],
                q_s[here, :],
                lambda scores: jnp.where(same, scores, MASKED),
                small,
            )
            ot_s[:, here] = out
            log_ref[:2, here] = logs
            where = slice(start + at, start + at + MARGIN)
            clip = row_ref[:, where] == CLIP_ID
            for head in range(2):
                rows = slice(head * size, (head + 1) * size)
                own = slice(2 * MARGIN * head + inner, 2 * MARGIN * head + inner + MARGIN)
                ot_s[rows, where] = jnp.where(clip, edge_out[rows, own], ot_s[rows, where])
                log_ref[head : head + 1, where] = jnp.where(
                    clip, edge_logs[:, own], log_ref[head : head + 1, where]
                )

    pl.when(bound < SMALL**2)(lambda: all_rows(True, 3 * BLOCK))
    pl.when(jnp.logical_not(bound < SMALL**2))(lambda: all_rows(False, BLOCK))
    log_ref[2:, :] = jnp.zeros((6, PLANE * BLOCK), jnp.float32)
    if turned:
        for p in range(PLANE):
            out_ref[p] = to_half(ot_s[:, p * BLOCK : (p + 1) * BLOCK])
    else:
        out_ref[...] = to_half(ot_s[...].T)


def attend_back_kernel(
    size, qkv_ref, out_ref, grad_ref, log_ref, column_ref, row_ref, dqkv_ref,
    q_s, k_s, v_s, kt_s, d_s, dqt_s, dk_s, dv_s, *g_s,
):
    both = 2 * size
    factor = LOG2E * size**-0.5
    scale = size**-0.5
    turned = len(qkv_ref.shape) == 3
    grads = g_s[0] if turned else grad_ref
    if turned:
        for p in range(PLANE):
            here = slice(p * BLOCK, (p + 1) * BLOCK)
            for i, rows_s in enumerate((q_s, k_s, v_s)):
                rows_s[here, :] = to_half(to_full(qkv_ref[p, i * both : (i + 1) * both, :]).T)
            kt_s[:, here] = qkv_ref[p, both : 2 * both, :]
            full = to_full(grad_ref[p])
            grads[here, :] = to_half(full.T)
            weighted = full * to_full(out_ref[p])
            for head in range(2):
                d_s[head : head + 1, here] = jnp.sum(
                    weighted[head * size : (head + 1) * size], 0, keepdims=True
                )
    else:
        q_s[...] = qkv_ref[:, :both]
        k_s[...] = qkv_ref[:, both : 2 * both]
        v_s[...] = qkv_ref[:, 2 * both :]
        kt_s[...] = to_half(to_full(qkv_ref[:, both : 2 * both]).T)
        weighted = (to_full(grad_ref[...]) * to_full(out_ref[...])).T
        for head in range(2):
            d_s[head : head + 1, :] = jnp.sum(
                weighted[head * size : (head + 1) * size], 0, keepdims=True
            )
    dk_s[...] = jnp.zeros_like(dk_s)
    dv_s[...] = jnp.zeros_like(dv_s)
    biases = clip_bias(column_ref)

    def pulled(keys, values, keys_t, queries, grads, logs, centres, masked):
        outs, probs_all, scores_all, queries_all, grads_all = [], [], [], [], []
        for head in range(2):
            own_queries = head_lanes(queries, head, size)
            own_grads = head_lanes(grads, head, size)
            probs = jnp.exp2(masked(nt(keys, own_queries) * factor) - logs[head : head + 1])
            pull = nt(values, own_grads)
            grad_scores = to_half(probs * (pull - centres[head : head + 1]))
            outs.append(product(keys_t, grad_scores)[head * size : (head + 1) * size] * scale)
            probs_all.append(to_half(probs))
            scores_all.append(grad_scores)
            queries_all.append(own_queries)
            grads_all.append(own_grads)
        grad_keys = sum(product(s, q) for s, q in zip(scores_all, queries_all)) * scale
        grad_values = sum(product(p, g) for p, g in zip(probs_all, grads_all))
        return jnp.concatenate(outs, 0), grad_keys, grad_values

    def over_clip(queries, grads, logs, centres):
        return pulled(
            k_s[CLIP_LOW:CLIP_HIGH, :],
            v_s[CLIP_LOW:CLIP_HIGH, :],
            kt_s[:, CLIP_LOW:CLIP_HIGH],
            queries,
            grads,
            logs,
            centres,
            lambda scores: add_margins(scores, biases),
        )

    @pl.loop(1, PLANE - 1)
    def _(block):
        start = pl.multiple_of(block * BLOCK, BLOCK)
        here = pl.ds(start, BLOCK)
        out, grad_keys, grad_values = over_clip(
            q_s[here, :], grads[here, :], log_ref[:2, here], d_s[:2, here]
        )
        dqt_s[:, here] = out
        dk_s[CLIP_LOW:CLIP_HIGH, :] += grad_keys
        dv_s[CLIP_LOW:CLIP_HIGH, :] += grad_values

    last = (PLANE - 1) * BLOCK
    near, far = slice(BLOCK - MARGIN, BLOCK), slice(last, last + MARGIN)

    def end_rows(ref):
        rows = jnp.concatenate([ref[near, :], ref[far, :]], 0)
        return jnp.concatenate([head_lanes(rows, 0, size), head_lanes(rows, 1, size)], 0)

    def end_columns(ref):
        return jnp.concatenate(
            [ref[head : head + 1, part] for head in range(2) for part in (near, far)], 1
        )

    clip = slice(CLIP_LOW, CLIP_HIGH)
    edge_labels = jnp.concatenate([row_ref[:, near], row_ref[:, far]] * 2, 1)
    edge_logs = jnp.where(edge_labels == CLIP_ID, end_columns(log_ref), -MASKED)
    edge_queries, edge_grads = end_rows(q_s), end_rows(grads)
    probs = jnp.exp2(add_margins(nt(k_s[clip, :], edge_queries) * factor, biases) - edge_logs)
    pull = nt(v_s[clip, :], edge_grads)
    grad_scores = to_half(probs * (pull - end_columns(d_s)))
    edge_out = product(kt_s[:, clip], grad_scores) * scale
    dk_s[clip, :] += product(grad_scores, edge_queries) * scale
    dv_s[clip, :] += product(to_half(probs), edge_grads)
    for start, at, inner in ((0, BLOCK - MARGIN, 0), (last, 0, MARGIN)):
        here = slice(start, start + BLOCK)
        labels = row_ref[:, here]
        same = column_ref[here, :] == labels
        logs = jnp.where(labels == CLIP_ID, -MASKED, log_ref[:2, here])
        out, grad_keys, grad_values = pulled(
            k_s[here, :],
            v_s[here, :],
            kt_s[:, here],
            q_s[here, :],
            grads[here, :],
            logs,
            d_s[:2, here],
            lambda scores: jnp.where(same, scores, MASKED),
        )
        dqt_s[:, here] = out
        where = slice(start + at, start + at + MARGIN)
        for head in range(2):
            rows = slice(head * size, (head + 1) * size)
            own = slice(2 * MARGIN * head + inner, 2 * MARGIN * head + inner + MARGIN)
            dqt_s[rows, where] += edge_out[rows, own]
        dk_s[here, :] += grad_keys
        dv_s[here, :] += grad_values
    if turned:
        for p in range(PLANE):
            here = slice(p * BLOCK, (p + 1) * BLOCK)
            dqkv_ref[p, :both, :] = to_half(dqt_s[:, here])
            dqkv_ref[p, both : 2 * both, :] = to_half(dk_s[here, :].T)
            dqkv_ref[p, 2 * both :, :] = to_half(dv_s[here, :].T)
    else:
        dqkv_ref[:, :both] = to_half(dqt_s[...].T)
        dqkv_ref[:, both : 2 * both] = to_half(dk_s[...])
        dqkv_ref[:, 2 * both :] = to_half(dv_s[...])


def attend(qkv, labels):
    turned = qkv.ndim == 3
    tokens = labels.shape[0]
    both = qkv.shape[1] // 3
    shape = (PLANE, both, BLOCK) if turned else (tokens, both)
    return pl.pallas_call(
        functools.partial(attend_kernel, both // 2),
        out_shape=(
            jax.ShapeDtypeStruct(shape, jnp.bfloat16),
            jax.ShapeDtypeStruct((8, tokens), jnp.float32),
        ),
        scratch_shapes=[
            pltpu.VMEM((tokens, both), jnp.bfloat16),
            pltpu.VMEM((tokens, both), jnp.bfloat16),
            pltpu.VMEM((both, tokens), jnp.bfloat16),
            pltpu.VMEM((both, tokens), jnp.float32),
        ],
        compiler_params=pltpu.CompilerParams(vmem_limit_bytes=VMEM_LIMIT),
        cost_estimate=estimate("attend"),
        name="attend",
    )(qkv, labels[:, None], labels[None, :])


def attend_back(qkv, out, grad, logs, labels):
    turned = qkv.ndim == 3
    tokens = labels.shape[0]
    both = qkv.shape[1] // 3
    return pl.pallas_call(
        functools.partial(attend_back_kernel, both // 2),
        out_shape=jax.ShapeDtypeStruct(qkv.shape, jnp.bfloat16),
        scratch_shapes=[
            pltpu.VMEM((tokens, both), jnp.bfloat16),
            pltpu.VMEM((tokens, both), jnp.bfloat16),
            pltpu.VMEM((tokens, both), jnp.bfloat16),
            pltpu.VMEM((both, tokens), jnp.bfloat16),
            pltpu.VMEM((8, tokens), jnp.float32),
            pltpu.VMEM((both, tokens), jnp.float32),
            pltpu.VMEM((tokens, both), jnp.float32),
            pltpu.VMEM((tokens, both), jnp.float32),
        ]
        + ([pltpu.VMEM((tokens, both), jnp.bfloat16)] if turned else []),
        compiler_params=pltpu.CompilerParams(vmem_limit_bytes=VMEM_LIMIT),
        cost_estimate=estimate("attend_back"),
        name="attend_back",
    )(qkv, out, grad, logs, labels[:, None], labels[None, :])


def exchange(parts):
    return lax.all_to_all(parts, GROUP_AXES, split_axis=0, concat_axis=0, tiled=True)


def to_heads(parts, axes):
    moved = lax.all_to_all(parts, axes, split_axis=0, concat_axis=0, tiled=True)
    return moved.reshape(-1, parts.shape[2])


def to_tokens(values, axes):
    count = PLANE // (2 if len(axes) == 2 else 1)
    parts = values.reshape(count, -1, values.shape[1])
    return lax.all_to_all(parts, axes, split_axis=0, concat_axis=0, tiled=True)


def encoder_columns(weight):
    rows, columns = weight.shape
    return weight.reshape(rows, 3, PLANE, -1).transpose(0, 2, 1, 3).reshape(rows, columns)


def encoder_columns_back(weight):
    rows, columns = weight.shape
    return weight.reshape(rows, PLANE, 3, -1).transpose(0, 2, 1, 3).reshape(rows, columns)


def per_device(
    pixels,
    clip_index,
    patch_weight,
    encoder_attention,
    encoder_output,
    encoder_expand,
    encoder_reduce,
    predictor_embed,
    predictor_weights,
    encoder_gains,
    encoder_biases,
    predictor_gains,
    predictor_biases,
    cotangent,
):
    labels = lax.dynamic_index_in_dim(clip_index, lax.axis_index("z"), 0, keepdims=False)
    width = encoder_output.shape[1]
    pred_width = predictor_embed.shape[1]
    hidden = encoder_expand.shape[1]

    order = Order()
    shard_rows = predictor_weights.shape[0]
    rows = pixels.shape[0]
    core = lax.axis_index("c")
    low = core == 0
    wide_columns = encoder_columns(to_half(encoder_attention))
    half_patch, half_expand = to_half(patch_weight), to_half(encoder_expand)
    patch = Gather(order, both_rows(column_half(half_patch), column_half(half_patch, True)))
    attention = Gather(order, both_rows(column_half(wide_columns), column_half(wide_columns, True)))
    half_expand = both_rows(odd_blocks(half_expand), odd_blocks(half_expand, True))
    output = Gather(
        order, jnp.concatenate([to_half(encoder_output), to_half(predictor_embed)], 1), True
    )
    hidden_bias = encoder_biases[5:].reshape(-1, 2, 128)
    hidden_bias = lax.dynamic_index_in_dim(hidden_bias, core, 1, False).reshape(1, -1)

    patch.along_z()
    reduce = Gather(order, to_half(encoder_reduce))
    order.leave(attention.held)
    pixels_got = swap(pixels, "c")
    attention.along_z()
    patch.rest_of_z()
    patch.first()
    attention.rest_of_z()
    output.along_z()
    patch.second()
    half_predictor = to_half(predictor_weights).reshape(shard_rows, 3 * pred_width)
    half_expand, half_predictor = order.enter(half_expand, half_predictor)
    expand = Whole(order, half_expand)
    attention.first()
    output.rest_of_z()
    reduce.along_z()
    patch.done()
    mine, theirs = embed_tokens(pixels, order.enter(pixels_got), patch.own)
    got = swap(order.leave(theirs), "c")
    attention.second()
    embedded, normed = norm_tokens(mine, order.enter(got), encoder_gains, encoder_biases)
    normed = order.leave(normed)
    normed_got = swap(normed, "c")
    reduce.rest_of_z()
    output.first()
    attention.done()

    normed, normed_got = order.enter(normed, normed_got)
    normed_both, parts = project_tokens(normed, normed_got, attention.own)
    qkv = to_heads(order.leave(parts), CHIP_AXES)
    output.second()
    qkv = order.enter(qkv)
    mixed_heads, logs = attend(qkv, labels)
    mixed_heads = order.leave(mixed_heads)
    reduce.first()
    parts = to_tokens(order.enter(mixed_heads), CHIP_AXES)
    output.done()
    output.cores()
    parts = order.enter(parts)
    theirs = lax.dynamic_slice_in_dim(parts, (1 - core) * rows, rows, 1)
    got = swap(order.leave(theirs), "c")
    reduce.second()
    attended, middle, second = middle_tokens(
        embedded, parts, order.enter(got), output.whole, encoder_gains, encoder_biases
    )
    second = order.leave(second)
    second_got = swap(second, "c")
    second, second_got = order.enter(second, second_got)
    second_both, expanded, activated = expand_tokens(second, second_got, expand.own, hidden_bias)
    order.leave(activated)
    reduce.done()
    mine, theirs = reduce_tokens(order.enter(activated), reduce.own)
    got = swap(order.leave(theirs), "c")
    weights = lax.all_gather(half_predictor, AXES, axis=0, tiled=True)
    encoded, pred_in, pred_normed, parts = encode_tokens(
        middle,
        mine,
        got,
        output.whole,
        encoder_biases,
        weights,
        predictor_gains,
        predictor_biases,
    )
    pred_qkv = exchange(parts)
    pred_heads, pred_logs = attend(pred_qkv, labels)
    prediction, pred_middle_grad, pred_grads, parts, pred_sums, pred_hidden_sums = pred_feed(
        pred_in,
        exchange(pred_heads),
        weights,
        predictor_gains,
        predictor_biases,
        cotangent,
    )

    grad_qkv = attend_back(
        pred_qkv, pred_heads, exchange(parts), pred_logs, labels
    )
    pred_grads, half_in, grad_encoded, encoded_half, pred_in_sums = pred_back(
        exchange(grad_qkv),
        pred_normed,
        pred_in,
        pred_middle_grad,
        weights,
        predictor_gains,
        output.whole,
        pred_grads,
    )

    encoded_half = order.leave(encoded_half)
    half_got = swap(encoded_half, "c")
    sum_p = Scatter.of_cores(order, order.enter(pred_grads))
    encoded_half, half_got = order.enter(encoded_half, half_got)
    grad_both, grad_expanded, hidden_sums = reduce_back(
        encoded_half, half_got, reduce.own, expanded
    )
    order.leave(grad_expanded)
    sum_r = Scatter(order, weight_grad([activated], [order.enter(grad_both)]))
    mine, theirs = expand_back(order.enter(grad_expanded), expand.own)
    got = swap(order.leave(theirs), "c")
    grad_middle, half_middle, middle_sums, keep, send = middle_back(
        middle, grad_encoded, mine, order.enter(got), encoder_gains, output.whole
    )
    sum_p.first()
    got = swap(order.leave(send), "c")
    sum_e = Scatter(order, weight_grad([second_both], [order.enter(grad_expanded)]))
    keep, got = order.enter(keep, got)
    parts = jnp.where(low, jnp.concatenate([keep, got], 1), jnp.concatenate([got, keep], 1))
    grad_heads = to_heads(order.leave(parts), CHIP_AXES)
    late_middle, late_in = order.enter(half_middle, half_in)
    sum_o = Scatter.of_cores(order, weight_grads([attended, encoded], [late_middle, late_in]))
    sum_r.second()
    sum_p.second()
    grad_heads = order.enter(grad_heads)
    grad_qkv = attend_back(qkv, mixed_heads, grad_heads, logs, labels)
    parts = to_tokens(order.leave(grad_qkv), CHIP_AXES)
    sum_r.along_z()
    sum_e.second()
    sum_o.first()
    sum_r.rest_of_z()
    sum_p.along_z()
    parts = order.enter(parts)
    sum_a = Scatter(order, weight_grad([normed_both], [parts]))
    sum_e.along_z()
    mine, theirs = project_back(order.enter(parts), attention.own)
    got = swap(order.leave(theirs), "c")
    sum_o.second()
    sum_r.done()
    keep, send, out_sums = input_back(
        embedded, grad_middle, mine, order.enter(got), encoder_gains
    )
    got = swap(order.leave(send), "c")
    sum_p.rest_of_z()
    got = order.enter(got)
    sum_k = Scatter(order, weight_grad([pixels, pixels_got], [keep, got]))
    hidden_sums = jnp.where(
        jnp.arange(2)[None, :, None] == core, hidden_sums.reshape(-1, 1, 128), 0.0
    ).reshape(1, -1)

    vectors = [
        out_sums[2],
        middle_sums[3],
        out_sums[0],
        out_sums[1],
        middle_sums[0],
        middle_sums[1],
        middle_sums[2],
        hidden_sums[0],
        pred_in_sums[2],
        pred_sums[3],
        pred_in_sums[0],
        pred_in_sums[1],
        pred_sums[0],
        pred_sums[1],
        pred_sums[2],
        pred_hidden_sums[0],
    ]
    sums = Total(order, jnp.concatenate(vectors).reshape(-1, 128))
    sums.step()
    pixel_mine, pixel_theirs = pixel_back(keep, order.enter(got), patch.own)
    pixel_theirs = swap(order.leave(pixel_theirs), "c")
    sums.step()
    sum_a.second()
    sum_k.second()
    sums.step()
    sum_o.along_z()
    sum_e.rest_of_z()
    sum_a.along_z()
    sums.step()
    sum_k.along_z()
    sum_p.done()
    sum_e.done()
    sum_o.rest_of_z()
    sum_a.rest_of_z()
    sums.step()
    sum_k.rest_of_z()
    sum_o.done()
    sum_a.done()
    sums.step()
    sum_k.done()
    pixel_grad = to_half(pixel_mine + to_full(pixel_theirs))

    patch_grad = jnp.concatenate(sum_k.column_halves(), 1)
    attention_grad = jnp.concatenate(sum_a.column_halves(), 1)
    expand_grad = jnp.stack(
        [v.reshape(v.shape[0], -1, 128) for v in sum_e.column_halves()], 2
    ).reshape(-1, hidden)
    sum_o.done()
    reduce_grad = to_full(sum_r.total)
    output_grad, embed_grad = (to_full(v) for v in jnp.split(sum_o.total, [width], 1))
    predictor_grad = to_full(sum_p.total)
    total = sums.done().reshape(-1)
    split = 11 * width
    encoder_vectors = total[:split].reshape(11, width)
    predictor_vectors = total[split:].reshape(11, pred_width)
    return (
        prediction,
        pixel_grad,
        patch_grad,
        encoder_columns_back(attention_grad),
        output_grad,
        expand_grad,
        reduce_grad,
        embed_grad,
        predictor_grad.reshape(shard_rows, 3, pred_width),
        encoder_vectors[:2],
        encoder_vectors[2:],
        predictor_vectors[:2],
        predictor_vectors[2:],
    )


def solution(mesh):
    CALLS.clear()
    wide, narrow = mesh.devices.shape
    fine = Mesh(mesh.devices.reshape(wide // 2, 2, narrow // 2, 2), AXES)
    rows = P(AXES, None)
    rows_three = P(AXES, None, None)
    in_specs = (rows, P(), rows, rows, rows, rows, rows, rows, rows_three, P(), P(), P(), P(), rows)
    out_specs = (rows,) * 8 + (rows_three, P(), P(), P(), P())
    return jax.shard_map(
        per_device, mesh=fine, in_specs=in_specs, out_specs=out_specs, check_vma=False
    )
```
